32 devices in a mesh: group: 4 (over x, core), dp: 8 (over z, y).
Axes of the slice: x: 2, y: 2, z: 4, core: 2. Of those that a mesh axis runs over, the one named last changes fastest.
Arguments:
- query_hidden: bfloat16 [256, 32, 768], P(('dp', 'group')), may hold values from -6 to 6
- passage_hidden: bfloat16 [512, 128, 768], P(('dp', 'group')), may hold values from -6 to 6
- projection: bfloat16 [768, 128], replicated, may hold values from -0.21875 to 0.21875
- positive: int32 [256], P(('dp', 'group')), may hold values from 0 to 63
- hard_ids: int32 [256, 32], P(('dp', 'group')), may hold values from -1 to 63, as said below
- passage_len: int32 [512], P(('dp', 'group')), may hold values from 16 to 128, as said below
Outputs:
- losses: float32 [256], P(('dp', 'group'))
- grad_proj: float32 [768, 128], replicated
- grad_query: bfloat16 [256, 32, 768], P(('dp', 'group'))
- grad_passage: bfloat16 [512, 128, 768], P(('dp', 'group'))
The draws below stay inside these ranges and needn't reach their ends.
Inputs may be any that keep to these rules, and one draw needn't show every extreme that they name: A passage's first passage_len tokens are live, the rest padding. `hard_ids`: A query's filled slots come first, from 8 to 32 of them; the rest hold -1. Slots may repeat a passage or name the positive.
All inputs are finite; a program needn't handle non-finite values.
Results may differ from the reference program's by a relative error of at most 0.017.
Values may be sent and summed in bfloat16 or wider, within the bound.
No kernel may reach another device: no remote copies, remote signals or barrier semaphores. Data moves between devices by JAX's collectives and lax.ppermute only.
A program may use at most 64 MiB of HBM per device.

```python
import jax
import jax.numpy as jnp
from jax import lax

H = 768
DIM = 128
QTOK = 32
PTOK = 128
NHARD = 32
QUERY_DEV = 8
POOL = 64
QUERIES = 256
PASSAGES = 512
N_GROUP = 4
N_DP = 8


def draw_passage_len(key, part):
    index = jnp.arange(PASSAGES, dtype=jnp.int32)
    lowest = PTOK // 8 + (PTOK - PTOK // 8) * index // (PASSAGES - 1)
    highest = jnp.minimum(PTOK, 2 * lowest)
    raw = jax.random.randint(key, (PASSAGES,), 0, 1 << 20, dtype=jnp.int32)
    drawn = lowest + raw % (highest + 1 - lowest)
    drawn = jnp.where(index == 0, PTOK // 8, drawn)
    return jnp.where(index == PASSAGES - 1, PTOK, drawn).astype(jnp.int32)


def draw_hard_ids(key, part):
    index = jnp.arange(QUERIES, dtype=jnp.int32)
    member = index // QUERY_DEV % N_GROUP
    fewest = NHARD // 4
    filled = fewest + (NHARD - fewest) * member // max(N_GROUP - 1, 1)
    picked = jax.random.randint(jax.random.fold_in(key, 7), (QUERIES, NHARD), 0, POOL, dtype=jnp.int32)
    slot = jnp.arange(NHARD, dtype=jnp.int32)
    return jnp.where(slot[None, :] < filled[:, None], picked, -1).astype(jnp.int32)


def touch_ends(values, stream_key, least, largest):
    place = [jax.random.randint(jax.random.fold_in(stream_key, axis), (), 0, length) for axis, length in enumerate(values.shape)]
    longest = values.shape.index(max(values.shape))
    beside = place[:longest] + [(place[longest] + 1) % values.shape[longest]] + place[longest + 1:]
    return values.at[tuple(place)].set(least).at[tuple(beside)].set(largest)


def shard_levels(own_key, dims, shards, least, largest):
    def one(position, parts):
        draws = jax.random.uniform(jax.random.fold_in(jax.random.fold_in(own_key, 6), position), (parts,), jnp.float32, least / len(shards), largest / len(shards))
        return jnp.repeat(jnp.exp(draws), dims[position] // parts).reshape((-1,) + (1,) * (len(dims) - position - 1))

    loudness = one(*shards[0])
    for cut in shards[1:]:
        loudness = loudness * one(*cut)
    return loudness


def noise(own_key, dims, width, reach, pieces=(), held_as=jnp.bfloat16):
    values = jax.random.normal(own_key, dims, jnp.float32) * width
    if len(pieces) > 0:
        values = shard_levels(own_key, dims, pieces, -0.22, 0.18) * values
    return jnp.clip(values, min=-reach, max=reach).astype(held_as)


def setup_inputs(seed: int = 0) -> dict:
    streams_of = jax.random.split(jax.random.key(seed), 7)
    query_hidden = noise(streams_of[0], (QUERIES, QTOK, H), 1.0, 6.0, ((0, 32),))
    passage_hidden = noise(streams_of[1], (PASSAGES, PTOK, H), 1.0, 6.0, ((0, 32),))
    projection = noise(streams_of[2], (H, DIM), H ** -0.5, 0.21875)
    positive = touch_ends(jax.random.randint(streams_of[3], (QUERIES,), 0, POOL), jax.random.fold_in(streams_of[3], 1), 0, POOL - 1).astype(jnp.int32)
    hard_ids = draw_hard_ids(jax.random.fold_in(streams_of[6], 71), 0)
    passage_len = draw_passage_len(jax.random.fold_in(streams_of[6], 71), 0)
    return {"query_hidden": query_hidden, "passage_hidden": passage_hidden, "projection": projection, "positive": positive, "hard_ids": hard_ids, "passage_len": passage_len}


smooth_temp = 0.1
norm_eps = 1e-06

def normalize(projected):
    return projected * lax.rsqrt(lax.optimization_barrier(jnp.sum(projected * projected, axis=-1, keepdims=True)) + norm_eps)

def contract_last(left, right):
    return lax.dot_general(left, right, (((1,), (1,)), ((), ())), preferred_element_type=jnp.float32)

def contract_first(left, right):
    return lax.dot_general(left, right, (((0,), (0,)), ((), ())), preferred_element_type=jnp.float32)

def smooth_scores(query_rows, passage_rows, usable):
    similar = contract_last(query_rows, passage_rows)
    similar = similar.reshape(similar.shape[0], usable.shape[0], usable.shape[1])
    summed = lax.optimization_barrier(jnp.sum(jnp.where(usable[None], jnp.exp(similar / smooth_temp), 0.0), axis=-1))
    return smooth_temp * jnp.log(summed)

def token_grads(query_rows, passage_rows, usable, smooth, weights):
    similar = contract_last(query_rows, passage_rows)
    similar = similar.reshape(similar.shape[0], usable.shape[0], usable.shape[1])
    shares = jnp.where(usable[None], jnp.exp(similar / smooth_temp - smooth[:, :, None] / smooth_temp), 0.0)
    coefficient = (weights[:, :, None] * shares).astype(jnp.bfloat16)
    coefficient = coefficient.reshape(query_rows.shape[0], passage_rows.shape[0])
    query_part = jnp.dot(coefficient, passage_rows, preferred_element_type=jnp.float32)
    passage_part = contract_first(coefficient, query_rows)
    return (query_part, passage_part)

def hard_counts(hard_ids, pool_size):
    columns = jnp.arange(pool_size, dtype=jnp.int32)
    return lax.optimization_barrier(jnp.sum((hard_ids[:, :, None] == columns[None, None, :]).astype(jnp.float32), axis=1))

def finish_loss(scores, positive, counts, hard_mean, boost):
    columns = jnp.arange(scores.shape[1], dtype=jnp.int32)
    chosen = positive[:, None] == columns[None, :]
    pos_score = lax.optimization_barrier(jnp.sum(jnp.where(chosen, scores, 0.0), axis=1, keepdims=True))
    reweight = 1.0 + jnp.where(chosen, 0.0, boost * counts * jnp.exp(scores - jnp.log(hard_mean)))
    weighted = reweight * jnp.exp(scores - pos_score)
    partition = lax.optimization_barrier(jnp.sum(weighted, axis=1, keepdims=True))
    losses = jnp.log(partition[:, 0])
    score_grad = weighted / partition - chosen.astype(jnp.float32)
    return (losses, score_grad)

def reference(query_hidden, passage_hidden, projection, positive, hard_ids, passage_len):
    query_flat = query_hidden.reshape(QUERIES * QTOK, H)
    passage_flat = passage_hidden.reshape(PASSAGES * PTOK, H)
    query_pre = jnp.dot(query_flat, projection, preferred_element_type=jnp.float32)
    passage_pre = jnp.dot(passage_flat, projection, preferred_element_type=jnp.float32)
    query_embed = normalize(query_pre).astype(jnp.bfloat16)
    passage_embed = normalize(passage_pre).astype(jnp.bfloat16)
    usable = jnp.arange(PTOK, dtype=jnp.int32)[None, :] < passage_len[:, None]
    block_rows = QUERY_DEV * QTOK
    query_pools = query_embed.reshape(N_DP, N_GROUP, block_rows, DIM)
    passage_pools = passage_embed.reshape(N_DP, POOL * PTOK, DIM)
    usable_pools = usable.reshape(N_DP, POOL, PTOK)

    def forward_pool(members):
        query_blocks, passage_rows, usable_rows = members
        return lax.map(lambda query_block: smooth_scores(query_block, passage_rows, usable_rows), query_blocks)
    smooth = lax.map(forward_pool, (query_pools, passage_pools, usable_pools))
    scores = lax.optimization_barrier(jnp.sum(smooth.reshape(QUERIES, QTOK, POOL), axis=1))
    counts = hard_counts(hard_ids, POOL)
    hard_mean = jnp.sum(counts * jnp.exp(scores)) / (QUERIES * NHARD)
    losses, score_grad = finish_loss(scores, positive, counts, hard_mean, POOL / NHARD)
    weights = jnp.repeat(score_grad, QTOK, axis=0).reshape(N_DP, N_GROUP, block_rows, POOL)
    smooth_pools = smooth.reshape(N_DP, N_GROUP, block_rows, POOL)

    def backward_pool(members):
        query_blocks, passage_rows, usable_rows, smooth_blocks, weight_blocks = members

        def step_block(running, inner):
            query_part, passage_part = token_grads(inner[0], passage_rows, usable_rows, inner[1], inner[2])
            rounded = lax.optimization_barrier(passage_part.astype(jnp.bfloat16))
            return (running + rounded.astype(jnp.float32), query_part)
        initial = jnp.zeros((POOL * PTOK, DIM), jnp.float32)
        return lax.scan(step_block, initial, (query_blocks, smooth_blocks, weight_blocks))
    passage_grad, query_grad = lax.map(backward_pool, (query_pools, passage_pools, usable_pools, smooth_pools, weights))
    query_grad = query_grad.reshape(QUERIES * QTOK, DIM)
    passage_grad = passage_grad.reshape(PASSAGES * PTOK, DIM)
    query_back = jax.vjp(normalize, query_pre)[1](query_grad)[0].astype(jnp.bfloat16)
    passage_back = jax.vjp(normalize, passage_pre)[1](passage_grad)[0].astype(jnp.bfloat16)
    grad_query = contract_last(query_back, projection).astype(jnp.bfloat16).reshape(QUERIES, QTOK, H)
    grad_passage = contract_last(passage_back, projection).astype(jnp.bfloat16).reshape(PASSAGES, PTOK, H)
    grad_proj = contract_first(query_flat, query_back) + contract_first(passage_flat, passage_back)
    return (losses, grad_proj, grad_query, grad_passage)
```

```python
import jax
import jax.numpy as jnp
from jax import lax
from jax.sharding import PartitionSpec as P

smooth_temp = 0.1
norm_eps = 1e-06


def normalize(projected):
    return projected * lax.rsqrt(jnp.sum(projected * projected, axis=-1, keepdims=True) + norm_eps)


def contract_last(left, right):
    return lax.dot_general(
        left, right, (((1,), (1,)), ((), ())), preferred_element_type=jnp.float32
    )


def contract_first(left, right):
    return lax.dot_general(
        left, right, (((0,), (0,)), ((), ())), preferred_element_type=jnp.float32
    )


def smooth_scores(query_rows, passage_rows, usable):
    similar = contract_last(query_rows, passage_rows)
    similar = similar.reshape(similar.shape[0], usable.shape[0], usable.shape[1])
    summed = jnp.sum(jnp.where(usable[None], jnp.exp(similar / smooth_temp), 0.0), axis=-1)
    return smooth_temp * jnp.log(summed)


def token_grads(query_rows, passage_rows, usable, smooth, weights):
    similar = contract_last(query_rows, passage_rows)
    similar = similar.reshape(similar.shape[0], usable.shape[0], usable.shape[1])
    shares = jnp.where(
        usable[None], jnp.exp(similar / smooth_temp - smooth[:, :, None] / smooth_temp), 0.0
    )
    coefficient = (weights[:, :, None] * shares).astype(jnp.bfloat16)
    coefficient = coefficient.reshape(query_rows.shape[0], passage_rows.shape[0])
    query_part = jnp.dot(coefficient, passage_rows, preferred_element_type=jnp.float32)
    passage_part = contract_first(coefficient, query_rows)
    return (query_part, passage_part)


def sum_everywhere(value):
    axes = ("dp", "group")
    devices = lax.axis_size(axes)
    rows = jnp.broadcast_to(value.reshape(1, 1, 1), (devices, 8, 128))
    return jnp.sum(lax.all_to_all(rows, axes, 0, 0, tiled=True)[:, 0, 0])


def sum_rows_everywhere(value):
    axes = ("dp", "group")
    devices = lax.axis_size(axes)
    rows, columns = value.shape
    parts = value.astype(jnp.bfloat16).reshape(devices, rows // devices, columns)
    parts = lax.all_to_all(parts, axes, 0, 0, tiled=True)
    own = jnp.sum(parts.astype(jnp.float32), axis=0).astype(jnp.bfloat16)
    copies = jnp.broadcast_to(own[None], parts.shape)
    return lax.all_to_all(copies, axes, 0, 0, tiled=True).reshape(rows, columns).astype(jnp.float32)


def hard_counts(hard_ids, pool_size):
    columns = jnp.arange(pool_size, dtype=jnp.int32)
    return jnp.sum((hard_ids[:, :, None] == columns[None, None, :]).astype(jnp.float32), axis=1)


def finish_loss(scores, positive, hard_ids, total_slots):
    counts = hard_counts(hard_ids, scores.shape[1])
    boost = scores.shape[1] / hard_ids.shape[1]
    hard_total = sum_everywhere(jnp.sum(counts * jnp.exp(scores)))
    hard_mean = hard_total / total_slots
    columns = jnp.arange(scores.shape[1], dtype=jnp.int32)
    chosen = positive[:, None] == columns[None, :]
    pos_score = jnp.sum(jnp.where(chosen, scores, 0.0), axis=1, keepdims=True)
    reweight = 1.0 + jnp.where(chosen, 0.0, boost * counts * jnp.exp(scores - jnp.log(hard_mean)))
    weighted = reweight * jnp.exp(scores - pos_score)
    partition = jnp.sum(weighted, axis=1, keepdims=True)
    losses = jnp.log(partition[:, 0])
    score_grad = weighted / partition - chosen.astype(jnp.float32)
    return (losses, score_grad)


def local(query_hidden, passage_hidden, projection, positive, hard_ids, passage_len):
    query_count = query_hidden.shape[0]
    query_len = query_hidden.shape[1]
    hidden_width = query_hidden.shape[2]
    passage_count = passage_hidden.shape[0]
    passage_tokens = passage_hidden.shape[1]
    embed_width = projection.shape[1]
    groups = lax.axis_size("group")
    total_slots = query_count * groups * lax.axis_size("dp") * hard_ids.shape[1]
    block_rows = query_count * query_len
    query_flat = query_hidden.reshape(block_rows, hidden_width)
    passage_flat = passage_hidden.reshape(passage_count * passage_tokens, hidden_width)
    query_pre = jnp.dot(query_flat, projection, preferred_element_type=jnp.float32)
    passage_pre = jnp.dot(passage_flat, projection, preferred_element_type=jnp.float32)
    query_embed = normalize(query_pre).astype(jnp.bfloat16)
    passage_embed = normalize(passage_pre).astype(jnp.bfloat16)
    token_index = jnp.arange(passage_tokens, dtype=jnp.int32)
    gathered = lax.all_gather(query_embed, "group", axis=0, tiled=True)
    query_blocks = gathered.reshape(groups, block_rows, embed_width)
    usable = token_index[None, :] < passage_len[:, None]
    smooth_blocks = lax.map(
        lambda query_block: smooth_scores(query_block, passage_embed, usable), query_blocks
    )
    local_scores = jnp.sum(
        smooth_blocks.reshape(groups * query_count, query_len, passage_count), axis=1
    )
    scores = lax.all_to_all(local_scores, "group", split_axis=0, concat_axis=1, tiled=True)
    losses, score_grad = finish_loss(scores, positive, hard_ids, total_slots)
    returned = lax.all_to_all(score_grad, "group", split_axis=1, concat_axis=0, tiled=True)
    weight_blocks = jnp.repeat(returned, query_len, axis=0).reshape(
        groups, block_rows, passage_count
    )

    def backward_block(running, members):
        query_part, passage_part = token_grads(
            members[0], passage_embed, usable, members[1], members[2]
        )
        rounded = lax.optimization_barrier(passage_part.astype(jnp.bfloat16))
        return (running + rounded.astype(jnp.float32), query_part)

    initial = jnp.zeros((passage_count * passage_tokens, embed_width), jnp.float32)
    passage_grad, query_parts = lax.scan(
        backward_block, initial, (query_blocks, smooth_blocks, weight_blocks)
    )
    query_grad = lax.psum_scatter(
        query_parts.reshape(groups * block_rows, embed_width).astype(jnp.bfloat16),
        "group",
        scatter_dimension=0,
        tiled=True,
    ).astype(jnp.float32)
    query_back = jax.vjp(normalize, query_pre)[1](query_grad)[0].astype(jnp.bfloat16)
    passage_back = jax.vjp(normalize, passage_pre)[1](passage_grad)[0].astype(jnp.bfloat16)
    grad_query = (
        contract_last(query_back, projection)
        .astype(jnp.bfloat16)
        .reshape(query_count, query_len, hidden_width)
    )
    grad_passage = (
        contract_last(passage_back, projection)
        .astype(jnp.bfloat16)
        .reshape(passage_count, passage_tokens, hidden_width)
    )
    local_weight = contract_first(query_flat, query_back) + contract_first(
        passage_flat, passage_back
    )
    grad_proj = sum_rows_everywhere(local_weight)
    return (losses, grad_proj, grad_query, grad_passage)


def solution(mesh):
    in_specs = (
        P(("dp", "group"), None, None),
        P(("dp", "group"), None, None),
        P(),
        P(("dp", "group")),
        P(("dp", "group"), None),
        P(("dp", "group")),
    )
    out_specs = (
        P(("dp", "group")),
        P(),
        P(("dp", "group"), None, None),
        P(("dp", "group"), None, None),
    )
    return jax.shard_map(local, mesh=mesh, in_specs=in_specs, out_specs=out_specs, check_vma=False)
```

```python
import functools

import jax
import jax.numpy as jnp
from jax import lax
from jax.experimental import pallas as pl
from jax.experimental.pallas import tpu as pltpu
from jax.sharding import PartitionSpec as P

smooth_temp = 0.1
norm_eps = 1e-06
center = 0.375
lanes = 128
axes = ("dp", "group")
f32 = jnp.float32
bf16 = jnp.bfloat16


def dot(left, right, left_dim, right_dim):
    return lax.dot_general(
        left, right, (((left_dim,), (right_dim,)), ((), ())), preferred_element_type=f32
    )


def split_parts(value):
    high = value.astype(bf16)
    rest = value - high.astype(f32)
    middle = rest.astype(bf16)
    low = (rest - middle.astype(f32)).astype(bf16)
    return (high, middle, low)


def exact_dot(value, picks):
    return sum(dot(part, picks, 1, 0) for part in split_parts(value))


def normalize(projected):
    return projected * lax.rsqrt(jnp.sum(projected * projected, axis=-1, keepdims=True) + norm_eps)


def normalize_back(projected, grad):
    inverse = lax.rsqrt(jnp.sum(projected * projected, axis=-1, keepdims=True) + norm_eps)
    along = jnp.sum(projected * grad, axis=-1, keepdims=True)
    return grad * inverse - projected * (inverse * inverse * inverse * along)


def iota(shape, dim):
    return lax.broadcasted_iota(jnp.int32, shape, dim)


def params(megabytes):
    return pltpu.CompilerParams(vmem_limit_bytes=megabytes * 2**20)


def cost(flops, nbytes, exps=0):
    return pl.CostEstimate(flops=int(flops), bytes_accessed=int(nbytes), transcendentals=int(exps))


VMEM = pl.BlockSpec(memory_space=pltpu.VMEM)
SMEM = pl.BlockSpec(memory_space=pltpu.SMEM)


def query_kernel(hidden, projection, hard_ids, positive, pre_out, packed_out):
    rows = hidden.shape[0]
    count, slots = hard_ids.shape
    pre = dot(hidden[...], projection[...], 1, 0)
    pre_out[...] = pre
    packed_out[:rows, :] = normalize(pre).astype(bf16)
    row = iota((count, lanes), 0)
    column = iota((count, lanes), 1)
    marks = jnp.full((count, lanes), -1.0, f32)
    for k in range(count):
        marks = jnp.where((row == k) & (column == slots), positive[k].astype(f32), marks)
    ids = jnp.concatenate(
        [hard_ids[...].astype(f32), jnp.full((count, lanes - slots), -1.0, f32)], axis=1
    )
    marks = jnp.where(column < slots, ids, marks)
    extra = packed_out.shape[0] - rows
    marks = jnp.concatenate([marks, jnp.full((extra - count, lanes), -1.0, f32)], axis=0)
    packed_out[rows:, :] = marks.astype(bf16)


def passage_kernel(hidden, projection, pre_out, embed_out):
    pre = dot(hidden[...], projection[...], 1, 0)
    pre_out[...] = pre
    embed_out[...] = normalize(pre).astype(bf16)


def token_picks(groups, count, length, width, rows_first):
    me = lax.axis_index("group")
    tokens = groups * count * length
    shape = (tokens, width) if rows_first else (width, tokens)
    token = iota(shape, 0 if rows_first else 1)
    query = iota(shape, 1 if rows_first else 0)
    member = jnp.bitwise_xor(token // (count * length), me)
    owner = member * count + (token % (count * length)) // length
    return jnp.where(owner == query, 1.0, 0.0).astype(bf16)


def forward_kernel(dims, lens, *refs):
    groups, count, length, passages, tokens, slots, step = dims
    packed = refs[:groups]
    embed, shares_out, inverse_out, stats_out, packet_out, queries, summed, marks = refs[groups:]
    rows = count * length
    at = pl.program_id(0)
    me = lax.axis_index("group")

    @pl.when(at == 0)
    def _():
        marks[...] = jnp.full(marks.shape, -1.0, f32)
        for k in range(groups):
            queries[k] = packed[k][:rows, :]
            member = jnp.bitwise_xor(me, k)
            start = pl.multiple_of(member * count, count)
            marks[pl.ds(start, count), :] = packed[k][rows:, :].astype(f32)[:count]

    def one(k, _):
        for p in range(step):
            part = embed[p * tokens : (p + 1) * tokens, :]
            similar = dot(part, queries[k], 1, 1)
            alive = iota(similar.shape, 0) < lens[at * step + p]
            grown = jnp.where(alive, jnp.exp(similar * (1.0 / smooth_temp)), 0.0)
            column = pl.multiple_of(k * rows, rows) if groups > 4 else k * rows
            shares_out[p * tokens : (p + 1) * tokens, pl.ds(column, rows)] = grown.astype(bf16)
            summed[pl.ds(at * step + p, 1), pl.ds(column, rows)] = jnp.sum(
                grown, axis=0, keepdims=True
            )
        return 0

    if groups > 4:
        lax.fori_loop(0, groups, one, 0)
    else:
        for k in range(groups):
            one(k, 0)

    @pl.when(at == pl.num_programs(0) - 1)
    def _():
        total = summed[...]
        inverse_out[...] = 1.0 / total
        width = marks.shape[0]
        scores = exact_dot(
            smooth_temp * jnp.log(total), token_picks(groups, count, length, width, True)
        )
        marks_t = marks[...].T
        ids = marks_t[:slots, :]
        first = me * passages
        counts = jnp.concatenate(
            [
                jnp.sum(
                    jnp.where(ids == (first + p).astype(f32), 1.0, 0.0), axis=0, keepdims=True
                )
                for p in range(passages)
            ],
            axis=0,
        )
        here = (iota((passages, width), 0) + first).astype(f32)
        chosen = here == marks_t[slots : slots + 1, :]
        grown = jnp.exp(scores - center * length)
        boost = groups * passages / slots
        boosted = jnp.where(chosen, 0.0, boost * counts)
        stats_out[:passages, :] = grown
        stats_out[passages : 2 * passages, :] = boosted
        stats_out[2 * passages :, :] = jnp.where(chosen, 1.0, 0.0)
        plain = jnp.sum(grown, axis=0, keepdims=True)
        hard = jnp.sum(boosted * grown * grown, axis=0, keepdims=True)
        kept = jnp.sum(jnp.where(chosen, scores, 0.0), axis=0, keepdims=True)
        sums = jnp.sum(counts * grown, axis=0, keepdims=True)
        sums = jnp.broadcast_to(jnp.sum(sums, axis=1, keepdims=True), sums.shape)
        packet = jnp.concatenate([plain, hard, kept, sums] * 2, axis=0)
        for k in range(packet_out.shape[0] // 8):
            packet_out[k * 8 : k * 8 + 8, :] = packet


def query_grad_kernel(dims, packets, stats, inverse, shares, embed, *refs):
    groups, count, length, passages, tokens, slots, step = dims
    parts_out = refs[:groups]
    weights_out, losses_out, weights, running = refs[groups:]
    rows = count * length
    at = pl.program_id(0)

    @pl.when(at == 0)
    def _():
        width = stats.shape[1]
        devices = packets.shape[0] // 8
        got = packets[...].reshape(devices, 8, width)
        dp = lax.axis_index("dp")
        ours = iota(got.shape, 0) // groups == dp
        pool = jnp.sum(jnp.where(ours, got, 0.0), axis=0)
        every = jnp.sum(got, axis=0)
        hard_mean = every[3:4, :] * (1.0 / (devices * count * slots))
        partition = pool[0:1, :] + pool[1:2, :] / hard_mean
        losses_out[...] = jnp.broadcast_to(
            jnp.log(partition) - (pool[2:3, :] - center * length), losses_out.shape
        )
        grown = stats[:passages, :]
        boosted = stats[passages : 2 * passages, :]
        chosen = stats[2 * passages :, :]
        grad = grown * (1.0 + boosted * grown / hard_mean) / partition - chosen
        spread = exact_dot(grad, token_picks(groups, count, length, width, False))
        found = (spread * inverse[...]).astype(bf16)
        for p in range(passages):
            weights[p] = found[p : p + 1, :]
        weights_out[...] = weights[...]
        running[...] = jnp.zeros(running.shape, f32)

    coefficient = jnp.concatenate(
        [
            shares[p * tokens : (p + 1) * tokens, :] * weights[at * step + p]
            for p in range(step)
        ],
        axis=0,
    )
    running[...] += dot(embed[...].T, coefficient, 1, 0)

    @pl.when(at == pl.num_programs(0) - 1)
    def _():
        for k in range(groups):
            parts_out[k][...] = running[:, k * rows : (k + 1) * rows].astype(bf16)


def passage_grad_kernel(dims, weights, shares, pre, hidden, *refs):
    groups, count, length, passages, tokens, slots, step = dims
    packed = refs[:groups]
    back_out, weight_out, queries = refs[groups:]
    rows = count * length
    at = pl.program_id(0)

    @pl.when(at == 0)
    def _():
        for k in range(groups):
            queries[k * rows : (k + 1) * rows, :] = packed[k][:rows, :]
        weight_out[...] = jnp.zeros(weight_out.shape, f32)

    coefficient = jnp.concatenate(
        [
            shares[p * tokens : (p + 1) * tokens, :] * weights[at * step + p]
            for p in range(step)
        ],
        axis=0,
    )
    grad = dot(coefficient, queries[...], 1, 0)
    back = normalize_back(pre[...], grad).astype(bf16)
    back_out[...] = back
    weight_out[...] += dot(back.T, hidden[...], 1, 0)


def query_back_kernel(pre, hidden, weight, *refs):
    parts = refs[:-2]
    back_out, weight_out = refs[-2:]
    grad = sum(part[...].astype(f32) for part in parts).T
    back = normalize_back(pre[...], grad).astype(bf16)
    back_out[...] = back
    total = weight[...] + dot(back.T, hidden[...], 1, 0)
    weight_out[...] = total.T.astype(bf16)


def sum_kernel(parts, copies_out):
    devices = copies_out.shape[0]
    total = parts[0].astype(f32)
    for k in range(1, devices):
        total += parts[k].astype(f32)
    total = total.astype(bf16)
    for k in range(devices):
        copies_out[k] = total


def local(query_hidden, passage_hidden, projection, positive, hard_ids, passage_len):
    count, length, width = query_hidden.shape
    passages, tokens, _ = passage_hidden.shape
    depth = projection.shape[1]
    slots = hard_ids.shape[1]
    groups = lax.axis_size("group")
    devices = lax.axis_size(axes)
    rows = count * length
    all_rows = groups * rows
    passage_rows = passages * tokens
    pool_width = -(-groups * count // lanes) * lanes
    step = 4 if passages % 4 == 0 else 1
    steps = passages // step
    step_rows = step * tokens
    dims = (groups, count, length, passages, tokens, slots, step)
    query_flat = query_hidden.reshape(rows, width)
    passage_flat = passage_hidden.reshape(passage_rows, width)
    shape = jax.ShapeDtypeStruct

    query_pre, packed = pl.pallas_call(
        query_kernel,
        out_shape=(shape((rows, depth), f32), shape((rows + 16, depth), bf16)),
        in_specs=[VMEM, VMEM, VMEM, SMEM],
        out_specs=(VMEM, VMEM),
        compiler_params=params(16),
        cost_estimate=cost(2 * rows * width * depth, rows * width * 2),
        name="query_embed",
    )(query_flat, projection, hard_ids, positive)

    def swap(value, k):
        return lax.ppermute(value, "group", [(i, i ^ k) for i in range(groups)])

    blocks = [packed] + [swap(packed, k) for k in range(1, groups)]

    def by_rows(columns):
        return pl.BlockSpec((step_rows, columns), lambda i: (i, 0))

    def whole(*dims_):
        return pl.BlockSpec(dims_, lambda i: (0,) * len(dims_))

    passage_pre, passage_embed = pl.pallas_call(
        passage_kernel,
        out_shape=(shape((passage_rows, depth), f32), shape((passage_rows, depth), bf16)),
        grid=(steps,),
        in_specs=[by_rows(width), whole(width, depth)],
        out_specs=(by_rows(depth), by_rows(depth)),
        compiler_params=params(16),
        cost_estimate=cost(2 * passage_rows * width * depth, passage_rows * (width * 2 + depth * 6)),
        name="passage_embed",
    )(passage_flat, projection)

    shares, inverse, stats, packets = pl.pallas_call(
        functools.partial(forward_kernel, dims),
        out_shape=(
            shape((passage_rows, all_rows), bf16),
            shape((passages, all_rows), f32),
            shape((3 * passages, pool_width), f32),
            shape((devices * 8, pool_width), f32),
        ),
        grid=(steps,),
        in_specs=[SMEM] + [whole(*packed.shape)] * groups + [by_rows(depth)],
        out_specs=(
            by_rows(all_rows),
            whole(passages, all_rows),
            whole(3 * passages, pool_width),
            whole(devices * 8, pool_width),
        ),
        scratch_shapes=[
            pltpu.VMEM((groups, rows, depth), bf16),
            pltpu.VMEM((passages, all_rows), f32),
            pltpu.VMEM((pool_width, lanes), f32),
        ],
        compiler_params=params(32),
        cost_estimate=cost(
            2 * passage_rows * all_rows * depth,
            passage_rows * all_rows * 2,
            passage_rows * all_rows,
        ),
        name="forward",
    )(passage_len, *blocks, passage_embed)

    packets = lax.all_to_all(packets, axes, 0, 0, tiled=True)

    outs = pl.pallas_call(
        functools.partial(query_grad_kernel, dims),
        out_shape=(
            *[shape((depth, rows), bf16)] * groups,
            shape((passages, 1, all_rows), bf16),
            shape((8, pool_width), f32),
        ),
        grid=(steps,),
        in_specs=[
            whole(*packets.shape),
            whole(*stats.shape),
            whole(*inverse.shape),
            by_rows(all_rows),
            by_rows(depth),
        ],
        out_specs=(
            *[whole(depth, rows)] * groups,
            whole(passages, 1, all_rows),
            whole(8, pool_width),
        ),
        scratch_shapes=[
            pltpu.VMEM((passages, 1, all_rows), bf16),
            pltpu.VMEM((depth, all_rows), f32),
        ],
        compiler_params=params(32),
        cost_estimate=cost(2 * passage_rows * all_rows * depth, passage_rows * all_rows * 2),
        name="query_grad",
    )(packets, stats, inverse, shares, passage_embed)
    parts = outs[:groups]
    weights, losses = outs[groups:]
    parts = [parts[0]] + [swap(parts[k], k) for k in range(1, groups)]

    passage_back, weight = pl.pallas_call(
        functools.partial(passage_grad_kernel, dims),
        out_shape=(shape((passage_rows, depth), bf16), shape((depth, width), f32)),
        grid=(steps,),
        in_specs=[
            whole(passages, 1, all_rows),
            by_rows(all_rows),
            by_rows(depth),
            by_rows(width),
        ]
        + [whole(*packed.shape)] * groups,
        out_specs=(by_rows(depth), whole(depth, width)),
        scratch_shapes=[pltpu.VMEM((all_rows, depth), bf16)],
        compiler_params=params(32),
        cost_estimate=cost(
            2 * passage_rows * (all_rows + width) * depth,
            passage_rows * (all_rows * 2 + width * 2 + depth * 6),
        ),
        name="passage_grad",
    )(weights, shares, passage_pre, passage_flat, *blocks)

    query_back, weight = pl.pallas_call(
        query_back_kernel,
        out_shape=(shape((rows, depth), bf16), shape((width, depth), bf16)),
        in_specs=[VMEM] * (3 + groups),
        out_specs=(VMEM, VMEM),
        compiler_params=params(16),
        cost_estimate=cost(2 * rows * width * depth, width * depth * 6 + rows * width * 2),
        name="query_back",
    )(query_pre, query_flat, weight, *parts)

    weight = weight.reshape(devices, width // devices, depth)
    weight = lax.all_to_all(weight, axes, 0, 0, tiled=True)
    copies = pl.pallas_call(
        sum_kernel,
        out_shape=shape(weight.shape, bf16),
        in_specs=[VMEM],
        out_specs=VMEM,
        compiler_params=params(16),
        name="sum_parts",
    )(weight)
    copies = lax.all_to_all(copies, axes, 0, 0, tiled=True)
    grad_proj = copies.reshape(width, depth).astype(f32)

    grad_query = dot(query_back, projection, 1, 1).astype(bf16).reshape(query_hidden.shape)
    grad_passage = dot(passage_back, projection, 1, 1).astype(bf16).reshape(passage_hidden.shape)
    own = lax.axis_index("group") * count
    return (lax.dynamic_slice(losses[0], (own,), (count,)), grad_proj, grad_query, grad_passage)


def solution(mesh):
    in_specs = (
        P(axes, None, None),
        P(axes, None, None),
        P(),
        P(axes),
        P(axes, None),
        P(axes),
    )
    out_specs = (P(axes), P(), P(axes, None, None), P(axes, None, None))
    return jax.shard_map(local, mesh=mesh, in_specs=in_specs, out_specs=out_specs, check_vma=False)
```

```python
import functools

import jax
import jax.numpy as jnp
from jax import lax
from jax.experimental import pallas as pl
from jax.experimental.pallas import tpu as pltpu
from jax.sharding import PartitionSpec as P

smooth_temp = 0.1
norm_eps = 1e-06
center = 0.375
lanes = 128
axes = ("dp", "group")
f32 = jnp.float32
bf16 = jnp.bfloat16


def dot(left, right, left_dim, right_dim):
    return lax.dot_general(
        left, right, (((left_dim,), (right_dim,)), ((), ())), preferred_element_type=f32
    )


def split_parts(value):
    high = value.astype(bf16)
    rest = value - high.astype(f32)
    middle = rest.astype(bf16)
    low = (rest - middle.astype(f32)).astype(bf16)
    return (high, middle, low)


def exact_dot(value, picks):
    return sum(dot(part, picks, 1, 0) for part in split_parts(value))


def normalize(projected):
    return projected * lax.rsqrt(jnp.sum(projected * projected, axis=-1, keepdims=True) + norm_eps)


def normalize_back(projected, grad):
    inverse = lax.rsqrt(jnp.sum(projected * projected, axis=-1, keepdims=True) + norm_eps)
    along = jnp.sum(projected * grad, axis=-1, keepdims=True)
    return grad * inverse - projected * (inverse * inverse * inverse * along)


def iota(shape, dim):
    return lax.broadcasted_iota(jnp.int32, shape, dim)


def params(megabytes):
    return pltpu.CompilerParams(vmem_limit_bytes=megabytes * 2**20)


def cost(flops, nbytes, exps=0):
    return pl.CostEstimate(flops=int(flops), bytes_accessed=int(nbytes), transcendentals=int(exps))


VMEM = pl.BlockSpec(memory_space=pltpu.VMEM)
SMEM = pl.BlockSpec(memory_space=pltpu.SMEM)
HBM = pl.BlockSpec(memory_space=pltpu.HBM)


def in_hbm(*values):
    return [pltpu.with_memory_space_constraint(value, pltpu.HBM) for value in values]


def query_kernel(
    hidden_hbm, projection_hbm, ids_hbm, positive_hbm, pre_out, packed_out, hidden, projection, hard_ids, positive, sems
):
    copies = [
        pltpu.make_async_copy(source, target, sems.at[k])
        for k, (source, target) in enumerate(
            [
                (projection_hbm, projection),
                (hidden_hbm, hidden),
                (ids_hbm, hard_ids),
                (positive_hbm, positive),
            ]
        )
    ]
    for copy in copies:
        copy.start()
    for copy in copies[2:]:
        copy.wait()
    rows = hidden.shape[0]
    count, slots = hard_ids.shape
    row = iota((count, lanes), 0)
    column = iota((count, lanes), 1)
    marks = jnp.full((count, lanes), -1.0, f32)
    for k in range(count):
        marks = jnp.where((row == k) & (column == slots), positive[k].astype(f32), marks)
    ids = jnp.concatenate(
        [hard_ids[...].astype(f32), jnp.full((count, lanes - slots), -1.0, f32)], axis=1
    )
    marks = jnp.where(column < slots, ids, marks)
    extra = packed_out.shape[0] - rows
    marks = jnp.concatenate([marks, jnp.full((extra - count, lanes), -1.0, f32)], axis=0)
    packed_out[rows:, :] = marks.astype(bf16)
    for copy in copies[:2]:
        copy.wait()
    pre = dot(hidden[...], projection[...], 1, 0)
    pre_out[...] = pre
    packed_out[:rows, :] = normalize(pre).astype(bf16)


def passage_kernel(step, hidden, projection_hbm, pre_out, embed_out, projection, sem):
    copy = pltpu.make_async_copy(projection_hbm, projection, sem)
    copy.start()
    copy.wait()
    for start in range(0, hidden.shape[0], step):
        part = slice(start, start + step)
        pre = dot(hidden[part, :], projection[...], 1, 0)
        pre_out[part, :] = pre
        embed_out[part, :] = normalize(pre).astype(bf16)


def token_picks(groups, count, length, width, rows_first):
    me = lax.axis_index("group")
    tokens = groups * count * length
    shape = (tokens, width) if rows_first else (width, tokens)
    token = iota(shape, 0 if rows_first else 1)
    query = iota(shape, 1 if rows_first else 0)
    member = jnp.bitwise_xor(token // (count * length), me)
    owner = member * count + (token % (count * length)) // length
    return jnp.where(owner == query, 1.0, 0.0).astype(bf16)


def forward_kernel(dims, lens, *refs):
    groups, count, length, passages, tokens, slots, step = dims
    packed = refs[:groups]
    embed, shares_out, inverse_out, stats_out, packet_out, summed, marks = refs[groups:]
    rows = count * length
    me = lax.axis_index("group")
    marks[...] = jnp.full(marks.shape, -1.0, f32)
    for k in range(groups):
        member = jnp.bitwise_xor(me, k)
        start = pl.multiple_of(member * count, count)
        marks[pl.ds(start, count), :] = packed[k][rows:, :].astype(f32)[:count]

    @pl.loop(0, passages // step, unroll=True)
    def _(at):
        start = pl.multiple_of(at * (step * tokens), step * tokens)
        part = embed[pl.ds(start, step * tokens), :]
        for k in range(groups):
            similar = dot(part, packed[k][:rows, :], 1, 1)
            for p in range(step):
                piece = similar[p * tokens : (p + 1) * tokens, :]
                alive = iota(piece.shape, 0) < lens[at * step + p]
                grown = jnp.where(alive, jnp.exp(piece * (1.0 / smooth_temp)), 0.0)
                shares_out[pl.ds(start + p * tokens, tokens), k * rows : (k + 1) * rows] = (
                    grown.astype(bf16)
                )
                summed[pl.ds(at * step + p, 1), k * rows : (k + 1) * rows] = jnp.sum(
                    grown, axis=0, keepdims=True
                )

    total = summed[...]
    inverse_out[...] = 1.0 / total
    width = marks.shape[0]
    scores = exact_dot(
        smooth_temp * jnp.log(total), token_picks(groups, count, length, width, True)
    )
    marks_t = marks[...].T
    ids = marks_t[:slots, :]
    first = me * passages
    counts = jnp.concatenate(
        [
            jnp.sum(jnp.where(ids == (first + p).astype(f32), 1.0, 0.0), axis=0, keepdims=True)
            for p in range(passages)
        ],
        axis=0,
    )
    here = (iota((passages, width), 0) + first).astype(f32)
    chosen = here == marks_t[slots : slots + 1, :]
    grown = jnp.exp(scores - center * length)
    boost = groups * passages / slots
    boosted = jnp.where(chosen, 0.0, boost * counts)
    stats_out[:passages, :] = grown
    stats_out[passages : 2 * passages, :] = boosted
    stats_out[2 * passages :, :] = jnp.where(chosen, 1.0, 0.0)
    plain = jnp.sum(grown, axis=0, keepdims=True)
    hard = jnp.sum(boosted * grown * grown, axis=0, keepdims=True)
    kept = jnp.sum(jnp.where(chosen, scores, 0.0), axis=0, keepdims=True)
    sums = jnp.sum(counts * grown, axis=0, keepdims=True)
    sums = jnp.broadcast_to(jnp.sum(sums, axis=1, keepdims=True), sums.shape)
    queries = groups * count
    if packet_out.shape[1] == 1:
        lane = iota(plain.shape, 1)
        packet = jnp.where(lane < queries, plain, sums)
        packet = jnp.where(lane // queries == 1, pltpu.roll(hard, queries, 1), packet)
        packet = jnp.where(lane // queries == 2, pltpu.roll(kept, 2 * queries, 1), packet)
    else:
        packet = jnp.concatenate([plain, hard, kept, sums] * 2, axis=0)
    for k in range(packet_out.shape[0]):
        packet_out[k] = packet


def query_grad_kernel(dims, packets, stats, inverse, shares, embed, *refs):
    groups, count, length, passages, tokens, slots, step = dims
    parts_out = refs[:groups]
    weights, losses_out, running = refs[groups:]
    rows = count * length
    width = stats.shape[1]
    devices = packets.shape[0]
    dp = lax.axis_index("dp")
    pool = packets[pl.ds(dp * groups, groups)].sum(axis=0)
    every = packets[...].sum(axis=0)
    queries = groups * count
    if packets.shape[1] == 1:
        plain, hard, kept = pool, pltpu.roll(pool, width - queries, 1), pltpu.roll(pool, width - 2 * queries, 1)
        sums = every[:, 3 * queries : 3 * queries + 1]
    else:
        plain, hard, kept, sums = pool[0:1, :], pool[1:2, :], pool[2:3, :], every[3:4, 0:1]
    hard_mean = sums * (1.0 / (devices * count * slots))
    partition = jnp.where(iota(plain.shape, 1) < queries, plain + hard / hard_mean, 1.0)
    losses_out[...] = jnp.broadcast_to(
        jnp.log(partition) - (kept - center * length), losses_out.shape
    )
    grown = stats[:passages, :]
    boosted = stats[passages : 2 * passages, :]
    chosen = stats[2 * passages :, :]
    grad = grown * (1.0 + boosted * grown / hard_mean) / partition - chosen
    spread = exact_dot(grad, token_picks(groups, count, length, width, False))
    found = (spread * inverse[...]).astype(bf16)
    for p in range(passages):
        weights[p] = found[p : p + 1, :]
    running[...] = jnp.zeros(running.shape, f32)

    @pl.loop(0, passages // step, unroll=True)
    def _(at):
        start = pl.multiple_of(at * (step * tokens), step * tokens)
        running[...] += dot(
            embed[pl.ds(start, step * tokens), :].T,
            coefficients(dims, shares, weights, at),
            1,
            0,
        )

    for k in range(groups):
        parts_out[k][...] = running[:, k * rows : (k + 1) * rows].astype(bf16)


def coefficients(dims, shares, weights, at):
    passages, tokens, _, step = dims[3:]
    start = pl.multiple_of(at * (step * tokens), step * tokens)
    return jnp.concatenate(
        [
            shares[pl.ds(start + p * tokens, tokens), :] * weights[at * step + p]
            for p in range(step)
        ],
        axis=0,
    )


def passage_grad_kernel(dims, weights, shares, pre, hidden, query_pre, query_hidden, *refs):
    groups, count, length, passages, tokens, slots, step = dims
    packed = refs[:groups]
    back_out, weight_out, pre_out, hidden_out, queries, running = refs[groups:]
    rows = count * length
    for k in range(groups):
        queries[k * rows : (k + 1) * rows, :] = packed[k][:rows, :]
    running[...] = jnp.zeros(running.shape, f32)

    @pl.loop(0, passages // step, unroll=True)
    def _(at):
        part = pl.ds(pl.multiple_of(at * (step * tokens), step * tokens), step * tokens)
        grad = dot(coefficients(dims, shares, weights, at), queries[...], 1, 0)
        back = normalize_back(pre[part, :], grad).astype(bf16)
        back_out[part, :] = back
        running[...] += dot(back.T, hidden[part, :], 1, 0)

    weight_out[...] = running[...].T
    pre_out[...] = query_pre[...].T
    hidden_out[...] = query_hidden[...].T


def query_back_kernel(pre, hidden, weight, *refs):
    parts = refs[:-2]
    back_out, weight_out = refs[-2:]
    grad = sum(part[...].astype(f32) for part in parts)
    projected = pre[...]
    inverse = lax.rsqrt(jnp.sum(projected * projected, axis=0, keepdims=True) + norm_eps)
    along = jnp.sum(projected * grad, axis=0, keepdims=True)
    back = (grad * inverse - projected * (inverse * inverse * inverse * along)).astype(bf16)
    back_out[...] = back
    weight_out[...] = (weight[...] + dot(hidden[...], back, 1, 1)).astype(bf16)


def sum_kernel(parts, copies_out):
    devices = copies_out.shape[0]
    total = parts[0].astype(f32)
    for k in range(1, devices):
        total += parts[k].astype(f32)
    total = total.astype(bf16)
    for k in range(devices):
        copies_out[k] = total


def local(query_hidden, passage_hidden, projection, positive, hard_ids, passage_len):
    count, length, width = query_hidden.shape
    passages, tokens, _ = passage_hidden.shape
    depth = projection.shape[1]
    slots = hard_ids.shape[1]
    groups = lax.axis_size("group")
    devices = lax.axis_size(axes)
    rows = count * length
    all_rows = groups * rows
    passage_rows = passages * tokens
    pool_width = -(-groups * count // lanes) * lanes
    packet_rows = 1 if 3 * groups * count < lanes else 8
    step = 4 if groups <= 4 else 1
    dims = (groups, count, length, passages, tokens, slots, step)
    query_flat = query_hidden.reshape(rows, width)
    passage_flat = passage_hidden.reshape(passage_rows, width)
    shape = jax.ShapeDtypeStruct

    query_pre, packed = pl.pallas_call(
        query_kernel,
        out_shape=(shape((rows, depth), f32), shape((rows + 16, depth), bf16)),
        in_specs=[HBM] * 4,
        out_specs=(VMEM, VMEM),
        scratch_shapes=[
            pltpu.VMEM((rows, width), bf16),
            pltpu.VMEM((width, depth), bf16),
            pltpu.VMEM((count, slots), jnp.int32),
            pltpu.SMEM((count,), jnp.int32),
            pltpu.SemaphoreType.DMA((4,)),
        ],
        compiler_params=params(16),
        cost_estimate=cost(2 * rows * width * depth, rows * width * 2),
        name="query_embed",
    )(*in_hbm(query_flat, projection, hard_ids, positive))

    def swap(value, k):
        return lax.ppermute(value, "group", [(i, i ^ k) for i in range(groups)])

    blocks = [packed] + [swap(packed, k) for k in range(1, groups)]

    passage_pre, passage_embed = pl.pallas_call(
        functools.partial(passage_kernel, 4 * tokens),
        out_shape=(shape((passage_rows, depth), f32), shape((passage_rows, depth), bf16)),
        in_specs=[VMEM, HBM],
        out_specs=(VMEM, VMEM),
        scratch_shapes=[pltpu.VMEM((width, depth), bf16), pltpu.SemaphoreType.DMA],
        compiler_params=params(16),
        cost_estimate=cost(2 * passage_rows * width * depth, passage_rows * (width * 2 + depth * 6)),
        name="passage_embed",
    )(passage_flat, *in_hbm(projection))

    shares, inverse, stats, packets = pl.pallas_call(
        functools.partial(forward_kernel, dims),
        out_shape=(
            shape((passage_rows, all_rows), bf16),
            shape((passages, all_rows), f32),
            shape((3 * passages, pool_width), f32),
            shape((devices, packet_rows, pool_width), f32),
        ),
        in_specs=[SMEM] + [VMEM] * (groups + 1),
        out_specs=(VMEM, VMEM, VMEM, VMEM),
        scratch_shapes=[
            pltpu.VMEM((passages, all_rows), f32),
            pltpu.VMEM((pool_width, lanes), f32),
        ],
        compiler_params=params(32),
        cost_estimate=cost(
            2 * passage_rows * all_rows * depth,
            passage_rows * all_rows * 2,
            passage_rows * all_rows,
        ),
        name="forward",
    )(passage_len, *blocks, passage_embed)

    packets = lax.all_to_all(packets, axes, 0, 0, tiled=True)

    outs = pl.pallas_call(
        functools.partial(query_grad_kernel, dims),
        out_shape=(
            *[shape((depth, rows), bf16)] * groups,
            shape((passages, 1, all_rows), bf16),
            shape((8, pool_width), f32),
        ),
        in_specs=[VMEM] * 5,
        out_specs=(VMEM,) * (groups + 2),
        scratch_shapes=[pltpu.VMEM((depth, all_rows), f32)],
        compiler_params=params(32),
        cost_estimate=cost(2 * passage_rows * all_rows * depth, passage_rows * all_rows * 2),
        name="query_grad",
    )(packets, stats, inverse, shares, passage_embed)
    parts = outs[:groups]
    weights, losses = outs[groups:]
    parts = [parts[0]] + [swap(parts[k], k) for k in range(1, groups)]

    passage_back, weight, pre_t, hidden_t = pl.pallas_call(
        functools.partial(passage_grad_kernel, dims),
        out_shape=(
            shape((passage_rows, depth), bf16),
            shape((width, depth), f32),
            shape((depth, rows), f32),
            shape((width, rows), bf16),
        ),
        in_specs=[VMEM] * (6 + groups),
        out_specs=(VMEM,) * 4,
        scratch_shapes=[pltpu.VMEM((all_rows, depth), bf16), pltpu.VMEM((depth, width), f32)],
        compiler_params=params(32),
        cost_estimate=cost(
            2 * passage_rows * (all_rows + width) * depth,
            passage_rows * (all_rows * 2 + width * 2 + depth * 6),
        ),
        name="passage_grad",
    )(weights, shares, passage_pre, passage_flat, query_pre, query_flat, *blocks)

    query_back, weight = pl.pallas_call(
        query_back_kernel,
        out_shape=(shape((depth, rows), bf16), shape((width, depth), bf16)),
        in_specs=[VMEM] * (3 + groups),
        out_specs=(VMEM, VMEM),
        compiler_params=params(16),
        cost_estimate=cost(2 * rows * width * depth, width * depth * 6 + rows * width * 2),
        name="query_back",
    )(pre_t, hidden_t, weight, *parts)

    weight = weight.reshape(devices, width // devices, depth)
    weight = lax.all_to_all(weight, axes, 0, 0, tiled=True)
    copies = pl.pallas_call(
        sum_kernel,
        out_shape=shape(weight.shape, bf16),
        in_specs=[VMEM],
        out_specs=VMEM,
        compiler_params=params(16),
        name="sum_parts",
    )(weight)
    copies = lax.all_to_all(copies, axes, 0, 0, tiled=True)
    grad_proj = copies.reshape(width, depth).astype(f32)

    grad_query = dot(query_back, projection, 0, 1).astype(bf16).reshape(query_hidden.shape)
    grad_passage = dot(passage_back, projection, 1, 1).astype(bf16).reshape(passage_hidden.shape)
    own = lax.axis_index("group") * count
    return (lax.dynamic_slice(losses[0], (own,), (count,)), grad_proj, grad_query, grad_passage)


def solution(mesh):
    in_specs = (
        P(axes, None, None),
        P(axes, None, None),
        P(),
        P(axes),
        P(axes, None),
        P(axes),
    )
    out_specs = (P(axes), P(), P(axes, None, None), P(axes, None, None))
    return jax.shard_map(local, mesh=mesh, in_specs=in_specs, out_specs=out_specs, check_vma=False)
```

```python
import functools

import jax
import jax.numpy as jnp
from jax import lax
from jax.experimental import pallas as pl
from jax.experimental.pallas import tpu as pltpu
from jax.sharding import PartitionSpec as P

smooth_temp = 0.1
norm_eps = 1e-06
center = 0.375
lanes = 128
near = 2
axes = ("dp", "group")
f32 = jnp.float32
bf16 = jnp.bfloat16


def dot(left, right, left_dim, right_dim):
    return lax.dot_general(
        left, right, (((left_dim,), (right_dim,)), ((), ())), preferred_element_type=f32
    )


def split_parts(value):
    high = value.astype(bf16)
    rest = value - high.astype(f32)
    middle = rest.astype(bf16)
    low = (rest - middle.astype(f32)).astype(bf16)
    return (high, middle, low)


def exact_dot(value, picks):
    return sum(dot(part, picks, 1, 0) for part in split_parts(value))


def normalize(projected):
    return projected * lax.rsqrt(jnp.sum(projected * projected, axis=-1, keepdims=True) + norm_eps)


def normalize_back(projected, grad):
    inverse = lax.rsqrt(jnp.sum(projected * projected, axis=-1, keepdims=True) + norm_eps)
    along = jnp.sum(projected * grad, axis=-1, keepdims=True)
    return grad * inverse - projected * (inverse * inverse * inverse * along)


def iota(shape, dim):
    return lax.broadcasted_iota(jnp.int32, shape, dim)


def params(megabytes):
    return pltpu.CompilerParams(vmem_limit_bytes=megabytes * 2**20)


def cost(flops, nbytes, exps=0):
    return pl.CostEstimate(flops=int(flops), bytes_accessed=int(nbytes), transcendentals=int(exps))


VMEM = pl.BlockSpec(memory_space=pltpu.VMEM)
HBM = pl.BlockSpec(memory_space=pltpu.HBM)


def in_hbm(*values):
    return [pltpu.with_memory_space_constraint(value, pltpu.HBM) for value in values]


def query_kernel(
    hidden_hbm,
    projection_hbm,
    ids_hbm,
    positive_hbm,
    lens_hbm,
    pre_out,
    packed_out,
    projection,
    lens_out,
    hidden,
    hard_ids,
    positive,
    lens,
    sems,
):
    copies = [
        pltpu.make_async_copy(source, target, sems.at[k])
        for k, (source, target) in enumerate(
            [
                (projection_hbm, projection),
                (hidden_hbm, hidden),
                (ids_hbm, hard_ids),
                (positive_hbm, positive),
                (lens_hbm, lens),
            ]
        )
    ]
    for copy in copies:
        copy.start()
    for copy in copies[2:]:
        copy.wait()
    rows = hidden.shape[0]
    count, slots = hard_ids.shape
    row = iota((count, lanes), 0)
    column = iota((count, lanes), 1)
    marks = jnp.full((count, lanes), -1.0, f32)
    for k in range(count):
        marks = jnp.where((row == k) & (column == slots), positive[k].astype(f32), marks)
    ids = jnp.concatenate(
        [hard_ids[...].astype(f32), jnp.full((count, lanes - slots), -1.0, f32)], axis=1
    )
    marks = jnp.where(column < slots, ids, marks)
    extra = packed_out.shape[0] - rows
    marks = jnp.concatenate([marks, jnp.full((extra - count, lanes), -1.0, f32)], axis=0)
    packed_out[rows:, :] = marks.astype(bf16)
    for p in range(lens_out.shape[0]):
        lens_out[p : p + 1, :] = jnp.full((1, lanes), lens[p], jnp.int32)
    for copy in copies[:2]:
        copy.wait()
    pre = dot(hidden[...], projection[...], 1, 0)
    pre_out[...] = pre
    packed_out[:rows, :] = normalize(pre).astype(bf16)


def parted(index, size):
    if size & (size - 1) == 0:
        return lax.shift_right_logical(index, size.bit_length() - 1)
    return index // size


def token_picks(groups, count, length, width, rows_first):
    me = lax.axis_index("group")
    tokens = groups * count * length
    shape = (tokens, width) if rows_first else (width, tokens)
    token = iota(shape, 0 if rows_first else 1)
    query = iota(shape, 1 if rows_first else 0)
    owner = jnp.bitwise_xor(parted(token, length), me * count)
    return jnp.where(owner == query, 1.0, 0.0).astype(bf16)


def forward_step(dims, at, lens, part, packed, shares_out, summed):
    groups, count, length, passages, tokens, slots, step = dims
    rows = count * length
    for k, block in enumerate(packed):
        columns = slice(k * rows, (k + 1) * rows)
        similar = dot(part, block[:rows, :], 1, 1)
        for p in range(step):
            piece = similar[p * tokens : (p + 1) * tokens, :]
            live = jnp.concatenate([lens[at * step + p : at * step + p + 1, :]] * (rows // lanes), axis=1)
            grown = jnp.exp(piece * (1.0 / smooth_temp))
            grown = jnp.where(iota(piece.shape, 0) < live, grown, 0.0)
            start = (at * step + p) * tokens
            shares_out[start : start + tokens, columns] = grown.astype(bf16)
            summed[at * step + p : at * step + p + 1, columns] = jnp.sum(
                grown, axis=0, keepdims=True
            )


def near_kernel(dims, lens, hidden, projection, *refs):
    groups, count, length, passages, tokens, slots, step = dims
    packed = refs[:near]
    pre_out, embed_out, shares_out, summed_out = refs[near:]
    for at in range(passages // step):
        part = slice(at * step * tokens, (at + 1) * step * tokens)
        pre = dot(hidden[part, :], projection[...], 1, 0)
        pre_out[part, :] = pre
        embed = normalize(pre).astype(bf16)
        embed_out[part, :] = embed
        forward_step(dims, at, lens, embed, packed, shares_out, summed_out)


def far_kernel(dims, lens, *refs):
    groups, count, length, passages, tokens, slots, step = dims
    packed = refs[:groups]
    embed, summed_near, shares_out, inverse_out, stats_out, packet_out, summed, marks = refs[groups:]
    rows = count * length
    me = lax.axis_index("group")
    marks[...] = jnp.full(marks.shape, -1.0, f32)
    for k in range(groups):
        member = jnp.bitwise_xor(me, k)
        start = pl.multiple_of(member * count, count)
        marks[pl.ds(start, count), :] = packed[k][rows:, :].astype(f32)[:count]
    for at in range(passages // step):
        part = embed[at * step * tokens : (at + 1) * step * tokens, :]
        forward_step(dims, at, lens, part, packed[near:], shares_out, summed)
    total = jnp.concatenate([summed_near[...], summed[...]], axis=1)
    inverse_out[...] = 1.0 / total
    width = marks.shape[0]
    scores = exact_dot(
        smooth_temp * jnp.log(total), token_picks(groups, count, length, width, True)
    )
    marks_t = marks[...].T
    ids = marks_t[:slots, :]
    first = me * passages
    counts = jnp.concatenate(
        [
            jnp.sum(jnp.where(ids == (first + p).astype(f32), 1.0, 0.0), axis=0, keepdims=True)
            for p in range(passages)
        ],
        axis=0,
    )
    here = (iota((passages, width), 0) + first).astype(f32)
    chosen = here == marks_t[slots : slots + 1, :]
    grown = jnp.exp(scores - center * length)
    boost = groups * passages / slots
    boosted = jnp.where(chosen, 0.0, boost * counts)
    stats_out[:passages, :] = grown
    stats_out[passages : 2 * passages, :] = boosted
    stats_out[2 * passages :, :] = jnp.where(chosen, 1.0, 0.0)
    plain = jnp.sum(grown, axis=0, keepdims=True)
    hard = jnp.sum(boosted * grown * grown, axis=0, keepdims=True)
    kept = jnp.sum(jnp.where(chosen, scores, 0.0), axis=0, keepdims=True)
    sums = jnp.sum(counts * grown, axis=0, keepdims=True)
    sums = jnp.broadcast_to(jnp.sum(sums, axis=1, keepdims=True), sums.shape)
    queries = groups * count
    if packet_out.shape[1] == 1:
        lane = iota(plain.shape, 1)
        packet = jnp.where(lane < queries, plain, sums)
        packet = jnp.where(lane // queries == 1, pltpu.roll(hard, queries, 1), packet)
        packet = jnp.where(lane // queries == 2, pltpu.roll(kept, 2 * queries, 1), packet)
    else:
        packet = jnp.concatenate([plain, hard, kept, sums] * 2, axis=0)
    for k in range(packet_out.shape[0]):
        packet_out[k] = packet


def far_grad_kernel(
    dims,
    packets,
    stats,
    inverse,
    shares,
    embed,
    *refs,
):
    groups, count, length, passages, tokens, slots, step = dims
    parts_out = refs[: groups - near]
    weights, losses_out, running = refs[groups - near :]
    rows = count * length
    width = stats.shape[1]
    devices = packets.shape[0]
    dp = lax.axis_index("dp")
    pool = packets[pl.ds(dp * groups, groups)].sum(axis=0)
    every = packets[...].sum(axis=0)
    queries = groups * count
    if packets.shape[1] == 1:
        plain, hard, kept = pool, pltpu.roll(pool, width - queries, 1), pltpu.roll(pool, width - 2 * queries, 1)
        sums = every[:, 3 * queries : 3 * queries + 1]
    else:
        plain, hard, kept, sums = pool[0:1, :], pool[1:2, :], pool[2:3, :], every[3:4, 0:1]
    hard_mean = sums * (1.0 / (devices * count * slots))
    partition = jnp.where(iota(plain.shape, 1) < queries, plain + hard / hard_mean, 1.0)
    losses_out[...] = jnp.broadcast_to(
        jnp.log(partition) - (kept - center * length), losses_out.shape
    )
    grown = stats[:passages, :]
    boosted = stats[passages : 2 * passages, :]
    chosen = stats[2 * passages :, :]
    grad = grown * (1.0 + boosted * grown / hard_mean) / partition - chosen
    spread = exact_dot(grad, token_picks(groups, count, length, width, False))
    found = (spread * inverse[...]).astype(bf16)
    for p in range(passages):
        weights[p] = found[p : p + 1, :]
    query_grads(dims, shares, slice(near * rows, groups * rows), embed, weights, running)
    for k, out in enumerate(parts_out):
        out[...] = running[:, k * rows : (k + 1) * rows].astype(bf16)


def near_grad_kernel(dims, weights, shares, embed, *refs):
    rows = dims[1] * dims[2]
    parts_out, running = refs[:near], refs[near]
    query_grads(dims, shares, slice(0, near * rows), embed, weights, running)
    for k, out in enumerate(parts_out):
        out[...] = running[:, k * rows : (k + 1) * rows].astype(bf16)


def query_grads(dims, shares, columns, embed, weights, running):
    groups, count, length, passages, tokens, slots, step = dims
    for at in range(passages // step):
        part = embed[at * step * tokens : (at + 1) * step * tokens, :].T
        terms = dot(part, coefficients(dims, shares, columns, weights, at), 1, 0)
        if at == 0:
            running[...] = terms
        else:
            running[...] += terms


def halves(dims, shares_near, shares_far):
    groups, count, length = dims[:3]
    cut = near * count * length
    return [(shares_near, slice(0, cut)), (shares_far, slice(cut, groups * count * length))]


def coefficients(dims, shares, columns, weights, at):
    passages, tokens, _, step = dims[3:]
    start = at * step * tokens
    return jnp.concatenate(
        [
            shares[start + p * tokens : start + (p + 1) * tokens, :]
            * weights[at * step + p, :, columns]
            for p in range(step)
        ],
        axis=0,
    )


def passage_grad_kernel(
    dims, weights, shares_near, shares_far, pre, hidden, query_pre, query_hidden, *refs
):
    groups, count, length, passages, tokens, slots, step = dims
    packed = refs[:groups]
    back_out, weight_out, pre_out, hidden_out, queries, running = refs[groups:]
    rows = count * length
    for k in range(groups):
        queries[k * rows : (k + 1) * rows, :] = packed[k][:rows, :]
    for at in range(passages // step):
        part = slice(at * step * tokens, (at + 1) * step * tokens)
        grad = sum(
            dot(coefficients(dims, shares, columns, weights, at), queries[columns, :], 1, 0)
            for shares, columns in halves(dims, shares_near, shares_far)
        )
        back = normalize_back(pre[part, :], grad).astype(bf16)
        back_out[part, :] = back
        terms = dot(back.T, hidden[part, :], 1, 0)
        if at == 0:
            running[...] = terms
        else:
            running[...] += terms
    weight_out[...] = running[...].T
    pre_out[...] = query_pre[...].T
    hidden_out[...] = query_hidden[...].T


def normalize_back_columns(projected, grad):
    inverse = lax.rsqrt(jnp.sum(projected * projected, axis=0, keepdims=True) + norm_eps)
    along = jnp.sum(projected * grad, axis=0, keepdims=True)
    return grad * inverse - projected * (inverse * inverse * inverse * along)


def query_back_kernel(pre, hidden, weight, *refs):
    parts = refs[:-2]
    back_out, weight_out = refs[-2:]
    grad = sum(part[...].astype(f32) for part in parts)
    back = normalize_back_columns(pre[...], grad).astype(bf16)
    back_out[...] = back
    weight_out[...] = (weight[...] + dot(hidden[...], back, 1, 1)).astype(bf16)


def sum_kernel(parts, copies_out):
    devices = copies_out.shape[0]
    total = parts[0].astype(f32)
    for k in range(1, devices):
        total += parts[k].astype(f32)
    total = total.astype(bf16)
    for k in range(devices):
        copies_out[k] = total


def local(query_hidden, passage_hidden, projection, positive, hard_ids, passage_len):
    count, length, width = query_hidden.shape
    passages, tokens, _ = passage_hidden.shape
    depth = projection.shape[1]
    slots = hard_ids.shape[1]
    groups = lax.axis_size("group")
    devices = lax.axis_size(axes)
    rows = count * length
    all_rows = groups * rows
    passage_rows = passages * tokens
    pool_width = -(-groups * count // lanes) * lanes
    packet_rows = 1 if 3 * groups * count < lanes else 8
    step = 4 if groups <= 4 else 1
    dims = (groups, count, length, passages, tokens, slots, step)
    query_flat = query_hidden.reshape(rows, width)
    passage_flat = passage_hidden.reshape(passage_rows, width)
    shape = jax.ShapeDtypeStruct

    query_pre, packed, projection_near, lens = pl.pallas_call(
        query_kernel,
        out_shape=(
            shape((rows, depth), f32),
            shape((rows + 16, depth), bf16),
            shape((width, depth), bf16),
            shape((passages, lanes), jnp.int32),
        ),
        in_specs=[HBM] * 5,
        out_specs=(VMEM,) * 4,
        scratch_shapes=[
            pltpu.VMEM((rows, width), bf16),
            pltpu.VMEM((count, slots), jnp.int32),
            pltpu.SMEM((count,), jnp.int32),
            pltpu.SMEM((passages,), jnp.int32),
            pltpu.SemaphoreType.DMA((5,)),
        ],
        compiler_params=params(16),
        cost_estimate=cost(2e10, rows * width * 2),
        name="query_embed",
    )(*in_hbm(query_flat, projection, hard_ids, positive, passage_len))

    def swap(value, k):
        return lax.ppermute(value, "group", [(i, i ^ k) for i in range(groups)])

    blocks = [packed] + [swap(packed, k) for k in range(1, groups)]

    passage_pre, passage_embed, shares_near, summed_near = pl.pallas_call(
        functools.partial(near_kernel, dims),
        out_shape=(
            shape((passage_rows, depth), f32),
            shape((passage_rows, depth), bf16),
            shape((passage_rows, near * rows), bf16),
            shape((passages, near * rows), f32),
        ),
        in_specs=[VMEM] * (near + 3),
        out_specs=(VMEM,) * 4,
        compiler_params=params(32),
        cost_estimate=cost(
            2 * passage_rows * (width + near * rows) * depth,
            passage_rows * (width + near * rows + 3 * depth) * 2,
            passage_rows * near * rows,
        ),
        name="forward_near",
    )(lens, passage_flat, projection_near, *blocks[:near])

    far_rows = all_rows - near * rows
    shares_far, inverse, stats, packets = pl.pallas_call(
        functools.partial(far_kernel, dims),
        out_shape=(
            shape((passage_rows, far_rows), bf16),
            shape((passages, all_rows), f32),
            shape((3 * passages, pool_width), f32),
            shape((devices, packet_rows, pool_width), f32),
        ),
        in_specs=[VMEM] * (groups + 3),
        out_specs=(VMEM, VMEM, VMEM, VMEM),
        scratch_shapes=[
            pltpu.VMEM((passages, far_rows), f32),
            pltpu.VMEM((pool_width, lanes), f32),
        ],
        compiler_params=params(32),
        cost_estimate=cost(
            2 * passage_rows * far_rows * depth, passage_rows * far_rows * 2, passage_rows * far_rows
        ),
        name="forward_far",
    )(lens, *blocks, passage_embed, summed_near)

    packets = lax.all_to_all(packets, axes, 0, 0, tiled=True)

    *far_parts, weights, losses = pl.pallas_call(
        functools.partial(far_grad_kernel, dims),
        out_shape=(
            *[shape((depth, rows), bf16)] * (groups - near),
            shape((passages, 1, all_rows), bf16),
            shape((8, pool_width), f32),
        ),
        in_specs=[VMEM] * 5,
        out_specs=(VMEM,) * (groups - near + 2),
        scratch_shapes=[pltpu.VMEM((depth, far_rows), f32)],
        compiler_params=params(32),
        cost_estimate=cost(2 * passage_rows * far_rows * depth, passage_rows * far_rows * 2),
        name="query_grad_far",
    )(packets, stats, inverse, shares_far, passage_embed)
    near_parts = pl.pallas_call(
        functools.partial(near_grad_kernel, dims),
        out_shape=(shape((depth, rows), bf16),) * near,
        in_specs=[VMEM] * 3,
        out_specs=(VMEM,) * near,
        scratch_shapes=[pltpu.VMEM((depth, near * rows), f32)],
        compiler_params=params(32),
        cost_estimate=cost(4e9, passage_rows * near * rows * 2),
        name="query_grad_near",
    )(weights, shares_near, passage_embed)
    parts = [*near_parts, *far_parts]
    parts = [parts[0]] + [swap(parts[k], k) for k in range(1, groups)]

    passage_back, weight, pre_t, hidden_t = pl.pallas_call(
        functools.partial(passage_grad_kernel, dims),
        out_shape=(
            shape((passage_rows, depth), bf16),
            shape((width, depth), f32),
            shape((depth, rows), f32),
            shape((width, rows), bf16),
        ),
        in_specs=[VMEM] * (7 + groups),
        out_specs=(VMEM,) * 4,
        scratch_shapes=[pltpu.VMEM((all_rows, depth), bf16), pltpu.VMEM((depth, width), f32)],
        compiler_params=params(32),
        cost_estimate=cost(
            2 * passage_rows * (all_rows + width) * depth,
            passage_rows * (all_rows * 2 + width * 2 + depth * 6),
        ),
        name="passage_grad",
    )(weights, shares_near, shares_far, passage_pre, passage_flat, query_pre, query_flat, *blocks)

    query_back, weight = pl.pallas_call(
        query_back_kernel,
        out_shape=(shape((depth, rows), bf16), shape((width, depth), bf16)),
        in_specs=[VMEM] * (3 + groups),
        out_specs=(VMEM, VMEM),
        compiler_params=params(16),
        cost_estimate=cost(2 * rows * width * depth, width * depth * 6 + rows * width * 2),
        name="query_back",
    )(pre_t, hidden_t, weight, *parts)

    weight = weight.reshape(devices, width // devices, depth)
    weight = lax.all_to_all(weight, axes, 0, 0, tiled=True)
    grad_passage = dot(passage_back, projection, 1, 1).astype(bf16).reshape(passage_hidden.shape)
    weight, grad_passage = lax.optimization_barrier((weight, grad_passage))
    copies = pl.pallas_call(
        sum_kernel,
        out_shape=shape(weight.shape, bf16),
        in_specs=[VMEM],
        out_specs=VMEM,
        compiler_params=params(16),
        name="sum_parts",
    )(weight)
    copies = lax.all_to_all(copies, axes, 0, 0, tiled=True)
    grad_proj = copies.reshape(width, depth).astype(f32)

    grad_query = dot(query_back, projection, 0, 1).astype(bf16).reshape(query_hidden.shape)
    own = lax.axis_index("group") * count
    return (lax.dynamic_slice(losses[0], (own,), (count,)), grad_proj, grad_query, grad_passage)


def solution(mesh):
    in_specs = (
        P(axes, None, None),
        P(axes, None, None),
        P(),
        P(axes),
        P(axes, None),
        P(axes),
    )
    out_specs = (P(axes), P(), P(axes, None, None), P(axes, None, None))
    return jax.shard_map(local, mesh=mesh, in_specs=in_specs, out_specs=out_specs, check_vma=False)
```

```python
import functools

import jax
import jax.numpy as jnp
from jax import lax
from jax.experimental import pallas as pl
from jax.experimental.pallas import tpu as pltpu
from jax.sharding import PartitionSpec as P

smooth_temp = 0.1
norm_eps = 1e-06
center = 0.375
lanes = 128
near = 2
axes = ("dp", "group")
f32 = jnp.float32
bf16 = jnp.bfloat16


def dot(left, right, left_dim, right_dim):
    return lax.dot_general(
        left, right, (((left_dim,), (right_dim,)), ((), ())), preferred_element_type=f32
    )


def exact_dot(value, picks):
    high = value.astype(bf16)
    rest = value - high.astype(f32)
    middle = rest.astype(bf16)
    low = (rest - middle.astype(f32)).astype(bf16)
    rows = value.shape[0]
    got = dot(jnp.concatenate([high, middle, low], axis=0), picks, 1, 0)
    return got[:rows] + got[rows : 2 * rows] + got[2 * rows :]


def normalize(projected):
    return projected * lax.rsqrt(jnp.sum(projected * projected, axis=-1, keepdims=True) + norm_eps)


def normalize_back(projected, grad):
    inverse = lax.rsqrt(jnp.sum(projected * projected, axis=-1, keepdims=True) + norm_eps)
    along = jnp.sum(projected * grad, axis=-1, keepdims=True)
    return grad * inverse - projected * (inverse * inverse * inverse * along)


def iota(shape, dim):
    return lax.broadcasted_iota(jnp.int32, shape, dim)


def params(megabytes):
    return pltpu.CompilerParams(vmem_limit_bytes=megabytes * 2**20)


def cost(flops, nbytes, exps=0):
    return pl.CostEstimate(flops=int(flops), bytes_accessed=int(nbytes), transcendentals=int(exps))


VMEM = pl.BlockSpec(memory_space=pltpu.VMEM)
HBM = pl.BlockSpec(memory_space=pltpu.HBM)


def in_hbm(*values):
    return [pltpu.with_memory_space_constraint(value, pltpu.HBM) for value in values]


def query_kernel(
    hidden_hbm,
    projection_hbm,
    ids_hbm,
    positive_hbm,
    lens_hbm,
    pre_out,
    packed_out,
    projection,
    lens_out,
    hidden,
    hard_ids,
    positive,
    lens,
    sems,
):
    copies = [
        pltpu.make_async_copy(source, target, sems.at[k])
        for k, (source, target) in enumerate(
            [
                (projection_hbm, projection),
                (hidden_hbm, hidden),
                (ids_hbm, hard_ids),
                (positive_hbm, positive),
                (lens_hbm, lens),
            ]
        )
    ]
    for copy in copies:
        copy.start()
    for copy in copies[2:]:
        copy.wait()
    rows = hidden.shape[0]
    count, slots = hard_ids.shape
    row = iota((count, lanes), 0)
    column = iota((count, lanes), 1)
    marks = jnp.full((count, lanes), -1.0, f32)
    for k in range(count):
        marks = jnp.where((row == k) & (column == slots), positive[k].astype(f32), marks)
    ids = jnp.concatenate(
        [hard_ids[...].astype(f32), jnp.full((count, lanes - slots), -1.0, f32)], axis=1
    )
    marks = jnp.where(column < slots, ids, marks)
    extra = packed_out.shape[0] - rows
    marks = jnp.concatenate([marks, jnp.full((extra - count, lanes), -1.0, f32)], axis=0)
    packed_out[rows:, :] = marks.astype(bf16)
    for p in range(lens_out.shape[0]):
        lens_out[p : p + 1, :] = jnp.full((1, lanes), lens[p], jnp.int32)
    for copy in copies[:2]:
        copy.wait()
    pre = dot(hidden[...], projection[...], 1, 0)
    pre_out[...] = pre
    packed_out[:rows, :] = normalize(pre).astype(bf16)


def parted(index, size):
    if size & (size - 1) == 0:
        return lax.shift_right_logical(index, size.bit_length() - 1)
    return index // size


def token_picks(groups, count, length, width, rows_first):
    me = lax.axis_index("group")
    tokens = groups * count * length
    shape = (tokens, width) if rows_first else (width, tokens)
    token = iota(shape, 0 if rows_first else 1)
    query = iota(shape, 1 if rows_first else 0)
    owner = jnp.bitwise_xor(parted(token, length), me * count)
    return jnp.where(owner == query, 1.0, 0.0).astype(bf16)


def forward_step(dims, at, lens, part, packed, shares_out, summed):
    groups, count, length, passages, tokens, slots, step = dims
    rows = count * length
    for k, block in enumerate(packed):
        columns = slice(k * rows, (k + 1) * rows)
        similar = dot(part, block[:rows, :], 1, 1)
        for p in range(step):
            piece = similar[p * tokens : (p + 1) * tokens, :]
            live = jnp.concatenate([lens[at * step + p : at * step + p + 1, :]] * (rows // lanes), axis=1)
            grown = jnp.exp(piece * (1.0 / smooth_temp))
            grown = jnp.where(iota(piece.shape, 0) < live, grown, 0.0)
            start = (at * step + p) * tokens
            shares_out[start : start + tokens, columns] = grown.astype(bf16)
            summed[at * step + p : at * step + p + 1, columns] = jnp.sum(
                grown, axis=0, keepdims=True
            )


def near_kernel(dims, lens, hidden, projection, *refs):
    groups, count, length, passages, tokens, slots, step = dims
    packed = refs[:near]
    pre_out, embed_out, shares_out, summed_out, gather_out, spread_out = refs[near:]
    gather_out[...] = token_picks(groups, count, length, gather_out.shape[1], True)
    spread_out[...] = token_picks(groups, count, length, gather_out.shape[1], False)
    for at in range(passages // step):
        part = slice(at * step * tokens, (at + 1) * step * tokens)
        pre = dot(hidden[part, :], projection[...], 1, 0)
        pre_out[part, :] = pre
        embed = normalize(pre).astype(bf16)
        embed_out[part, :] = embed
        forward_step(dims, at, lens, embed, packed, shares_out, summed_out)


def far_kernel(dims, lens, *refs):
    groups, count, length, passages, tokens, slots, step = dims
    packed = refs[:groups]
    embed, summed_near, gather, *refs = refs[groups:]
    shares_out, inverse_out, stats_out, packet_out, summed, marks = refs
    rows = count * length
    me = lax.axis_index("group")
    marks[...] = jnp.full(marks.shape, -1.0, f32)
    for k in range(groups):
        member = jnp.bitwise_xor(me, k)
        start = pl.multiple_of(member * count, count)
        marks[pl.ds(start, count), :] = packed[k][rows:, :].astype(f32)[:count]
    for at in range(passages // step):
        part = embed[at * step * tokens : (at + 1) * step * tokens, :]
        forward_step(dims, at, lens, part, packed[near:], shares_out, summed)
    total = jnp.concatenate([summed_near[...], summed[...]], axis=1)
    inverse_out[...] = 1.0 / total
    width = marks.shape[0]
    scores = exact_dot(smooth_temp * jnp.log(total), gather[...])
    marks_t = marks[...].T
    ids = marks_t[:slots, :]
    first = me * passages
    counts = jnp.concatenate(
        [
            jnp.sum(jnp.where(ids == (first + p).astype(f32), 1.0, 0.0), axis=0, keepdims=True)
            for p in range(passages)
        ],
        axis=0,
    )
    here = (iota((passages, width), 0) + first).astype(f32)
    chosen = here == marks_t[slots : slots + 1, :]
    grown = jnp.exp(scores - center * length)
    boost = groups * passages / slots
    boosted = jnp.where(chosen, 0.0, boost * counts)
    stats_out[:passages, :] = grown
    stats_out[passages : 2 * passages, :] = boosted
    stats_out[2 * passages :, :] = jnp.where(chosen, 1.0, 0.0)
    plain = jnp.sum(grown, axis=0, keepdims=True)
    hard = jnp.sum(boosted * grown * grown, axis=0, keepdims=True)
    kept = jnp.sum(jnp.where(chosen, scores, 0.0), axis=0, keepdims=True)
    sums = jnp.sum(counts * grown, axis=0, keepdims=True)
    sums = jnp.broadcast_to(jnp.sum(sums, axis=1, keepdims=True), sums.shape)
    queries = groups * count
    if packet_out.shape[1] == 1:
        lane = iota(plain.shape, 1)
        packet = jnp.where(lane < queries, plain, sums)
        packet = jnp.where(lane // queries == 1, pltpu.roll(hard, queries, 1), packet)
        packet = jnp.where(lane // queries == 2, pltpu.roll(kept, 2 * queries, 1), packet)
    else:
        packet = jnp.concatenate([plain, hard, kept, sums] * 2, axis=0)
    for k in range(packet_out.shape[0]):
        packet_out[k] = packet


def far_grad_kernel(
    dims,
    packets,
    stats,
    inverse,
    spread,
    shares,
    embed,
    *refs,
):
    groups, count, length, passages, tokens, slots, step = dims
    parts_out = refs[: groups - near]
    weights, losses_out, running = refs[groups - near :]
    rows = count * length
    width = stats.shape[1]
    devices = packets.shape[0]
    dp = lax.axis_index("dp")
    pool = packets[pl.ds(dp * groups, groups)].sum(axis=0)
    every = packets[...].sum(axis=0)
    queries = groups * count
    if packets.shape[1] == 1:
        plain, hard, kept = pool, pltpu.roll(pool, width - queries, 1), pltpu.roll(pool, width - 2 * queries, 1)
        sums = every[:, 3 * queries : 3 * queries + 1]
    else:
        plain, hard, kept, sums = pool[0:1, :], pool[1:2, :], pool[2:3, :], every[3:4, 0:1]
    hard_mean = sums * (1.0 / (devices * count * slots))
    partition = jnp.where(iota(plain.shape, 1) < queries, plain + hard / hard_mean, 1.0)
    losses_out[...] = jnp.broadcast_to(
        jnp.log(partition) - (kept - center * length), losses_out.shape
    )
    grown = stats[:passages, :]
    boosted = stats[passages : 2 * passages, :]
    chosen = stats[2 * passages :, :]
    grad = grown * (1.0 + boosted * grown / hard_mean) / partition - chosen
    found = (exact_dot(grad, spread[...]) * inverse[...]).astype(bf16)
    for p in range(passages):
        weights[p] = found[p : p + 1, :]
    query_grads(dims, shares, slice(near * rows, groups * rows), embed, weights, running)
    for k, out in enumerate(parts_out):
        out[...] = running[:, k * rows : (k + 1) * rows].astype(bf16)


def near_grad_kernel(dims, weights, shares, embed, *refs):
    rows = dims[1] * dims[2]
    parts_out, running = refs[:near], refs[near]
    query_grads(dims, shares, slice(0, near * rows), embed, weights, running)
    for k, out in enumerate(parts_out):
        out[...] = running[:, k * rows : (k + 1) * rows].astype(bf16)


def query_grads(dims, shares, columns, embed, weights, running):
    groups, count, length, passages, tokens, slots, step = dims
    for at in range(passages // step):
        part = embed[at * step * tokens : (at + 1) * step * tokens, :].T
        terms = dot(part, coefficients(dims, shares, columns, weights, at), 1, 0)
        if at == 0:
            running[...] = terms
        else:
            running[...] += terms


def halves(dims, shares_near, shares_far):
    groups, count, length = dims[:3]
    cut = near * count * length
    return [(shares_near, slice(0, cut)), (shares_far, slice(cut, groups * count * length))]


def coefficients(dims, shares, columns, weights, at):
    passages, tokens, _, step = dims[3:]
    start = at * step * tokens
    return jnp.concatenate(
        [
            shares[start + p * tokens : start + (p + 1) * tokens, :]
            * weights[at * step + p, :, columns]
            for p in range(step)
        ],
        axis=0,
    )


def passage_grad_kernel(
    dims, weights, shares_near, shares_far, pre, hidden, query_pre, query_hidden, *refs
):
    groups, count, length, passages, tokens, slots, step = dims
    packed = refs[:groups]
    back_out, weight_out, pre_out, hidden_out, queries, running = refs[groups:]
    rows = count * length
    for k in range(groups):
        queries[k * rows : (k + 1) * rows, :] = packed[k][:rows, :]
    for at in range(passages // step):
        part = slice(at * step * tokens, (at + 1) * step * tokens)
        grad = sum(
            dot(coefficients(dims, shares, columns, weights, at), queries[columns, :], 1, 0)
            for shares, columns in halves(dims, shares_near, shares_far)
        )
        back = normalize_back(pre[part, :], grad).astype(bf16)
        back_out[part, :] = back
        terms = dot(back.T, hidden[part, :], 1, 0)
        if at == 0:
            running[...] = terms
        else:
            running[...] += terms
    weight_out[...] = running[...].T
    pre_out[...] = query_pre[...].T
    hidden_out[...] = query_hidden[...].T


def normalize_back_columns(projected, grad):
    inverse = lax.rsqrt(jnp.sum(projected * projected, axis=0, keepdims=True) + norm_eps)
    along = jnp.sum(projected * grad, axis=0, keepdims=True)
    return grad * inverse - projected * (inverse * inverse * inverse * along)


def query_back_kernel(pre, hidden, weight, *refs):
    parts = refs[:-2]
    back_out, weight_out = refs[-2:]
    grad = sum(part[...].astype(f32) for part in parts)
    back = normalize_back_columns(pre[...], grad).astype(bf16)
    back_out[...] = back
    weight_out[...] = (weight[...] + dot(hidden[...], back, 1, 1)).astype(bf16)


def sum_kernel(parts, copies_out):
    devices = copies_out.shape[0]
    total = parts[0].astype(f32)
    for k in range(1, devices):
        total += parts[k].astype(f32)
    total = total.astype(bf16)
    for k in range(devices):
        copies_out[k] = total


def local(query_hidden, passage_hidden, projection, positive, hard_ids, passage_len):
    count, length, width = query_hidden.shape
    passages, tokens, _ = passage_hidden.shape
    depth = projection.shape[1]
    slots = hard_ids.shape[1]
    groups = lax.axis_size("group")
    devices = lax.axis_size(axes)
    rows = count * length
    all_rows = groups * rows
    passage_rows = passages * tokens
    pool_width = -(-groups * count // lanes) * lanes
    packet_rows = 1 if 3 * groups * count < lanes else 8
    step = 4 if groups <= 4 else 1
    dims = (groups, count, length, passages, tokens, slots, step)
    query_flat = query_hidden.reshape(rows, width)
    passage_flat = passage_hidden.reshape(passage_rows, width)
    shape = jax.ShapeDtypeStruct

    query_pre, packed, projection_near, lens = pl.pallas_call(
        query_kernel,
        out_shape=(
            shape((rows, depth), f32),
            shape((rows + 16, depth), bf16),
            shape((width, depth), bf16),
            shape((passages, lanes), jnp.int32),
        ),
        in_specs=[HBM] * 5,
        out_specs=(VMEM,) * 4,
        scratch_shapes=[
            pltpu.VMEM((rows, width), bf16),
            pltpu.VMEM((count, slots), jnp.int32),
            pltpu.SMEM((count,), jnp.int32),
            pltpu.SMEM((passages,), jnp.int32),
            pltpu.SemaphoreType.DMA((5,)),
        ],
        compiler_params=params(16),
        cost_estimate=cost(2e10, rows * width * 2),
        name="query_embed",
    )(*in_hbm(query_flat, projection, hard_ids, positive, passage_len))

    def swap(value, k):
        return lax.ppermute(value, "group", [(i, i ^ k) for i in range(groups)])

    blocks = [packed] + [swap(packed, k) for k in range(1, groups)]

    passage_pre, passage_embed, shares_near, summed_near, gather, spread = pl.pallas_call(
        functools.partial(near_kernel, dims),
        out_shape=(
            shape((passage_rows, depth), f32),
            shape((passage_rows, depth), bf16),
            shape((passage_rows, near * rows), bf16),
            shape((passages, near * rows), f32),
            shape((all_rows, pool_width), bf16),
            shape((pool_width, all_rows), bf16),
        ),
        in_specs=[VMEM] * (near + 3),
        out_specs=(VMEM,) * 6,
        compiler_params=params(32),
        cost_estimate=cost(
            2 * passage_rows * (width + near * rows) * depth,
            passage_rows * (width + near * rows + 3 * depth) * 2,
            passage_rows * near * rows,
        ),
        name="forward_near",
    )(lens, passage_flat, projection_near, *blocks[:near])

    far_rows = all_rows - near * rows
    shares_far, inverse, stats, packets = pl.pallas_call(
        functools.partial(far_kernel, dims),
        out_shape=(
            shape((passage_rows, far_rows), bf16),
            shape((passages, all_rows), f32),
            shape((3 * passages, pool_width), f32),
            shape((devices, packet_rows, pool_width), f32),
        ),
        in_specs=[VMEM] * (groups + 4),
        out_specs=(VMEM, VMEM, VMEM, VMEM),
        scratch_shapes=[
            pltpu.VMEM((passages, far_rows), f32),
            pltpu.VMEM((pool_width, lanes), f32),
        ],
        compiler_params=params(32),
        cost_estimate=cost(
            2 * passage_rows * far_rows * depth, passage_rows * far_rows * 2, passage_rows * far_rows
        ),
        name="forward_far",
    )(lens, *blocks, passage_embed, summed_near, gather)

    packets = lax.all_to_all(packets, axes, 0, 0, tiled=True)

    *far_parts, weights, losses = pl.pallas_call(
        functools.partial(far_grad_kernel, dims),
        out_shape=(
            *[shape((depth, rows), bf16)] * (groups - near),
            shape((passages, 1, all_rows), bf16),
            shape((8, pool_width), f32),
        ),
        in_specs=[VMEM] * 6,
        out_specs=(VMEM,) * (groups - near + 2),
        scratch_shapes=[pltpu.VMEM((depth, far_rows), f32)],
        compiler_params=params(32),
        cost_estimate=cost(2 * passage_rows * far_rows * depth, passage_rows * far_rows * 2),
        name="query_grad_far",
    )(packets, stats, inverse, spread, shares_far, passage_embed)
    near_parts = pl.pallas_call(
        functools.partial(near_grad_kernel, dims),
        out_shape=(shape((depth, rows), bf16),) * near,
        in_specs=[VMEM] * 3,
        out_specs=(VMEM,) * near,
        scratch_shapes=[pltpu.VMEM((depth, near * rows), f32)],
        compiler_params=params(32),
        cost_estimate=cost(4e9, passage_rows * near * rows * 2),
        name="query_grad_near",
    )(weights, shares_near, passage_embed)
    parts = [*near_parts, *far_parts]
    parts = [swap(parts[k], k) for k in range(groups - 1, 0, -1)] + [parts[0]]

    passage_back, weight, pre_t, hidden_t = pl.pallas_call(
        functools.partial(passage_grad_kernel, dims),
        out_shape=(
            shape((passage_rows, depth), bf16),
            shape((width, depth), f32),
            shape((depth, rows), f32),
            shape((width, rows), bf16),
        ),
        in_specs=[VMEM] * (7 + groups),
        out_specs=(VMEM,) * 4,
        scratch_shapes=[pltpu.VMEM((all_rows, depth), bf16), pltpu.VMEM((depth, width), f32)],
        compiler_params=params(32),
        cost_estimate=cost(
            2 * passage_rows * (all_rows + width) * depth,
            passage_rows * (all_rows * 2 + width * 2 + depth * 6),
        ),
        name="passage_grad",
    )(weights, shares_near, shares_far, passage_pre, passage_flat, query_pre, query_flat, *blocks)

    query_back, weight = pl.pallas_call(
        query_back_kernel,
        out_shape=(shape((depth, rows), bf16), shape((width, depth), bf16)),
        in_specs=[VMEM] * (3 + groups),
        out_specs=(VMEM, VMEM),
        compiler_params=params(16),
        cost_estimate=cost(2 * rows * width * depth, width * depth * 6 + rows * width * 2),
        name="query_back",
    )(pre_t, hidden_t, weight, *parts)

    weight = weight.reshape(devices, width // devices, depth)
    weight = lax.all_to_all(weight, axes, 0, 0, tiled=True)
    grad_passage = dot(passage_back, projection, 1, 1).astype(bf16).reshape(passage_hidden.shape)
    weight, grad_passage = lax.optimization_barrier((weight, grad_passage))
    copies = pl.pallas_call(
        sum_kernel,
        out_shape=shape(weight.shape, bf16),
        in_specs=[VMEM],
        out_specs=VMEM,
        compiler_params=params(16),
        name="sum_parts",
    )(weight)
    copies = lax.all_to_all(copies, axes, 0, 0, tiled=True)
    grad_proj = copies.reshape(width, depth).astype(f32)

    grad_query = dot(query_back, projection, 0, 1).astype(bf16).reshape(query_hidden.shape)
    own = lax.axis_index("group") * count
    return (lax.dynamic_slice(losses[0], (own,), (count,)), grad_proj, grad_query, grad_passage)


def solution(mesh):
    in_specs = (
        P(axes, None, None),
        P(axes, None, None),
        P(),
        P(axes),
        P(axes, None),
        P(axes),
    )
    out_specs = (P(axes), P(), P(axes, None, None), P(axes, None, None))
    return jax.shard_map(local, mesh=mesh, in_specs=in_specs, out_specs=out_specs, check_vma=False)
```

```python
import functools

import jax
import jax.numpy as jnp
from jax import lax
from jax.experimental import pallas as pl
from jax.experimental.pallas import tpu as pltpu
from jax.sharding import PartitionSpec as P

smooth_temp = 0.1
norm_eps = 1e-06
center = 0.375
lanes = 128
cores = 2
axes = ("dp", "group")
f32 = jnp.float32
bf16 = jnp.bfloat16


def dot(left, right, left_dim, right_dim):
    return lax.dot_general(
        left, right, (((left_dim,), (right_dim,)), ((), ())), preferred_element_type=f32
    )


def exact_dot(value, picks):
    high = value.astype(bf16)
    rest = value - high.astype(f32)
    middle = rest.astype(bf16)
    low = (rest - middle.astype(f32)).astype(bf16)
    rows = value.shape[0]
    got = dot(jnp.concatenate([high, middle, low], axis=0), picks, 1, 0)
    return got[:rows] + got[rows : 2 * rows] + got[2 * rows :]


def normalize(projected):
    return projected * lax.rsqrt(jnp.sum(projected * projected, axis=-1, keepdims=True) + norm_eps)


def normalize_back(projected, grad):
    inverse = lax.rsqrt(jnp.sum(projected * projected, axis=-1, keepdims=True) + norm_eps)
    along = jnp.sum(projected * grad, axis=-1, keepdims=True)
    return grad * inverse - projected * (inverse * inverse * inverse * along)


def iota(shape, dim):
    return lax.broadcasted_iota(jnp.int32, shape, dim)


def params(megabytes):
    return pltpu.CompilerParams(vmem_limit_bytes=megabytes * 2**20)


def cost(flops, nbytes, exps=0):
    return pl.CostEstimate(flops=int(flops), bytes_accessed=int(nbytes), transcendentals=int(exps))


VMEM = pl.BlockSpec(memory_space=pltpu.VMEM)
HBM = pl.BlockSpec(memory_space=pltpu.HBM)


def in_hbm(*values):
    return [pltpu.with_memory_space_constraint(value, pltpu.HBM) for value in values]


def query_kernel(
    hidden_hbm,
    projection_hbm,
    ids_hbm,
    positive_hbm,
    lens_hbm,
    pre_out,
    packed_out,
    projection,
    lens_out,
    hidden,
    hard_ids,
    positive,
    lens,
    sems,
):
    copies = [
        pltpu.make_async_copy(source, target, sems.at[k])
        for k, (source, target) in enumerate(
            [
                (projection_hbm, projection),
                (hidden_hbm, hidden),
                (ids_hbm, hard_ids),
                (positive_hbm, positive),
                (lens_hbm, lens),
            ]
        )
    ]
    for copy in copies:
        copy.start()
    for copy in copies[2:]:
        copy.wait()
    rows = hidden.shape[0]
    count, slots = hard_ids.shape
    row = iota((count, lanes), 0)
    column = iota((count, lanes), 1)
    marks = jnp.full((count, lanes), -1.0, f32)
    for k in range(count):
        marks = jnp.where((row == k) & (column == slots), positive[k].astype(f32), marks)
    ids = jnp.concatenate(
        [hard_ids[...].astype(f32), jnp.full((count, lanes - slots), -1.0, f32)], axis=1
    )
    marks = jnp.where(column < slots, ids, marks)
    extra = packed_out.shape[0] - rows
    marks = jnp.concatenate([marks, jnp.full((extra - count, lanes), -1.0, f32)], axis=0)
    packed_out[rows:, :] = marks.astype(bf16)
    for p in range(lens_out.shape[0]):
        lens_out[p : p + 1, :] = jnp.full((1, lanes), lens[p], jnp.int32)
    for copy in copies[:2]:
        copy.wait()
    pre = dot(hidden[...], projection[...], 1, 0)
    pre_out[...] = pre
    packed_out[:rows, :] = normalize(pre).astype(bf16)


def parted(index, size):
    if size & (size - 1) == 0:
        return lax.shift_right_logical(index, size.bit_length() - 1)
    return index // size


def token_picks(dims, width, rows_first):
    blocks, count, length = dims[:3]
    chip = lax.axis_index("group") // cores
    tokens = blocks * count * length
    shape = (tokens, width) if rows_first else (width, tokens)
    token = iota(shape, 0 if rows_first else 1)
    query = iota(shape, 1 if rows_first else 0)
    owner = jnp.bitwise_xor(parted(token, length), chip * count)
    return jnp.where(owner == query, 1.0, 0.0).astype(bf16)


def passage_kernel(dims, lens, hidden, projection, pre_out, embed_out, gather_out, spread_out):
    blocks, count, length, passages, tokens, slots, step = dims
    for start in range(0, hidden.shape[0], step * tokens):
        part = slice(start, start + step * tokens)
        pre = dot(hidden[part, :], projection[...], 1, 0)
        pre_out[part, :] = pre
        embed_out[part, :] = normalize(pre).astype(bf16)
    embed_out[hidden.shape[0] :, :] = lens[...].astype(f32).astype(bf16)
    gather_out[...] = token_picks(dims, gather_out.shape[1], True)
    spread_out[...] = token_picks(dims, gather_out.shape[1], False)


def forward_part(dims, embed, queries, shares_out, summed, first):
    blocks, count, length, passages, tokens, slots, step = dims
    rows = count * length
    lens = embed[passages * tokens :, :].astype(f32).astype(jnp.int32)
    for at in range(passages // step):
        part = embed[at * step * tokens : (at + 1) * step * tokens, :]
        for k, block in enumerate(queries):
            columns = slice(k * rows, (k + 1) * rows)
            similar = dot(part, block[:rows, :], 1, 1)
            for p in range(step):
                row = at * step + p
                piece = similar[p * tokens : (p + 1) * tokens, :]
                live = jnp.concatenate([lens[row : row + 1, :]] * (rows // lanes), axis=1)
                grown = jnp.exp(piece * (1.0 / smooth_temp))
                grown = jnp.where(iota(piece.shape, 0) < live, grown, 0.0)
                shares_out[row * tokens : (row + 1) * tokens, columns] = grown.astype(bf16)
                summed[first + row : first + row + 1, columns] = jnp.sum(
                    grown, axis=0, keepdims=True
                )


def forward_kernel(dims, embed, *refs):
    forward_part(dims, embed, refs[:-2], refs[-2], refs[-1], 0)


def far_kernel(dims, *refs):
    blocks, count, length, passages, tokens, slots, step = dims
    packed = refs[:blocks]
    embed_other, summed_near, summed_far, gather, *refs = refs[blocks:]
    shares_other, inverse_out, stats_out, packet_out, summed, marks = refs
    rows = count * length
    me = lax.axis_index("group")
    marks[...] = jnp.full(marks.shape, -1.0, f32)
    for k in range(blocks):
        start = pl.multiple_of(jnp.bitwise_xor(me // cores, k) * count, count)
        marks[pl.ds(start, count), :] = packed[k][rows:, :].astype(f32)[:count]
    forward_part(dims, embed_other, packed, shares_other, summed, passages)
    summed[:passages, :rows] = summed_near[...]
    summed[:passages, rows:] = summed_far[...]
    total = summed[...]
    inverse_out[...] = 1.0 / total
    width = marks.shape[0]
    scores = exact_dot(smooth_temp * jnp.log(total), gather[...])
    marks_t = marks[...].T
    ids = marks_t[:slots, :]
    pair = cores * passages
    first = [me * passages, jnp.bitwise_xor(me, 1) * passages]
    counts = jnp.concatenate(
        [
            jnp.sum(
                jnp.where(ids == (first[p // passages] + p % passages).astype(f32), 1.0, 0.0),
                axis=0,
                keepdims=True,
            )
            for p in range(pair)
        ],
        axis=0,
    )
    row = iota((pair, width), 0)
    here = jnp.where(row < passages, row + first[0], row - passages + first[1])
    chosen = here.astype(f32) == marks_t[slots : slots + 1, :]
    grown = jnp.exp(scores - center * length)
    boost = blocks * pair / slots
    boosted = jnp.where(chosen, 0.0, boost * counts)
    stats_out[:pair, :] = grown
    stats_out[pair : 2 * pair, :] = boosted
    stats_out[2 * pair :, :] = jnp.where(chosen, 1.0, 0.0)
    plain = jnp.sum(grown, axis=0, keepdims=True)
    hard = jnp.sum(boosted * grown * grown, axis=0, keepdims=True)
    kept = jnp.sum(jnp.where(chosen, scores, 0.0), axis=0, keepdims=True)
    sums = jnp.sum(counts * grown, axis=0, keepdims=True)
    sums = jnp.broadcast_to(jnp.sum(sums, axis=1, keepdims=True), sums.shape)
    queries = blocks * count
    if packet_out.shape[1] == 1:
        lane = iota(plain.shape, 1)
        packet = jnp.where(lane < queries, plain, sums)
        packet = jnp.where(lane // queries == 1, pltpu.roll(hard, queries, 1), packet)
        packet = jnp.where(lane // queries == 2, pltpu.roll(kept, 2 * queries, 1), packet)
    else:
        packet = jnp.concatenate([plain, hard, kept, sums] * 2, axis=0)
    for k in range(packet_out.shape[0]):
        packet_out[k] = packet


def coefficients(dims, shares, columns, weights, first, at):
    passages, tokens, _, step = dims[3:]
    parts = []
    for p in range(at * step, (at + 1) * step):
        parts.append(shares[p * tokens : (p + 1) * tokens, :] * weights[first + p, :, columns])
    return jnp.concatenate(parts, axis=0)


def query_grads(dims, sources, weights, running):
    blocks, count, length, passages, tokens, slots, step = dims
    for k, (embed, shares, columns, first) in enumerate(sources):
        for at in range(passages // step):
            part = embed[at * step * tokens : (at + 1) * step * tokens, :].T
            terms = dot(part, coefficients(dims, shares, columns, weights, first, at), 1, 0)
            if k == 0 and at == 0:
                running[...] = terms
            else:
                running[...] += terms


class Columns:
    def __init__(self, ref, columns):
        self.ref, self.columns = ref, columns

    def __getitem__(self, index):
        return self.ref[index[0], self.columns]


def far_grad_kernel(
    dims,
    packets,
    stats,
    inverse,
    spread,
    shares_far,
    shares_other,
    embed,
    embed_other,
    *refs,
):
    blocks, count, length, passages, tokens, slots, step = dims
    parts_out = refs[: blocks - 1]
    weights, losses_out, running = refs[blocks - 1 :]
    rows = count * length
    pair = cores * passages
    width = stats.shape[1]
    devices = packets.shape[0]
    groups = cores * blocks
    core = lax.axis_index("group") % cores
    pool = packets[pl.ds(lax.axis_index("dp") * groups, groups)]
    pool = jnp.where(iota(pool.shape, 0) % cores == core, pool, 0.0).sum(axis=0)
    every = packets[...].sum(axis=0)
    queries = blocks * count
    if packets.shape[1] == 1:
        plain = pool
        hard = pltpu.roll(pool, width - queries, 1)
        kept = pltpu.roll(pool, width - 2 * queries, 1)
        sums = every[:, 3 * queries : 3 * queries + 1]
    else:
        plain, hard, kept, sums = pool[0:1, :], pool[1:2, :], pool[2:3, :], every[3:4, 0:1]
    hard_mean = sums * (1.0 / (devices * count * slots))
    partition = jnp.where(iota(plain.shape, 1) < queries, plain + hard / hard_mean, 1.0)
    losses_out[...] = jnp.broadcast_to(
        jnp.log(partition) - (kept - center * length), losses_out.shape
    )
    grown = stats[:pair, :]
    boosted = stats[pair : 2 * pair, :]
    chosen = stats[2 * pair :, :]
    grad = grown * (1.0 + boosted * grown / hard_mean) / partition - chosen
    found = (exact_dot(grad, spread[...]) * inverse[...]).astype(bf16)
    for p in range(pair):
        weights[p] = found[p : p + 1, :]
    columns = slice(rows, blocks * rows)
    sources = [
        (embed, shares_far, columns, 0),
        (embed_other, Columns(shares_other, columns), columns, passages),
    ]
    query_grads(dims, sources, weights, running)
    for k, out in enumerate(parts_out):
        out[...] = running[:, k * rows : (k + 1) * rows].astype(bf16)


def other_grad_kernel(dims, weights, shares_other, *refs):
    blocks, count, length, passages, tokens, slots, step = dims
    packed = refs[:blocks]
    grad_out, queries = refs[blocks:]
    rows = count * length
    for k in range(blocks):
        queries[k * rows : (k + 1) * rows, :] = packed[k][:rows, :]
    columns = slice(0, blocks * rows)
    for at in range(passages // step):
        coefficient = coefficients(dims, shares_other, columns, weights, passages, at)
        grad = dot(coefficient, queries[...], 1, 0)
        grad_out[at * step * tokens : (at + 1) * step * tokens, :] = grad.astype(bf16)


def own_grad_kernel(
    dims,
    weights,
    shares_near,
    shares_far,
    shares_other,
    embed,
    embed_other,
    query_pre,
    query_hidden,
    *refs,
):
    blocks, count, length, passages, tokens, slots, step = dims
    packed = refs[:blocks]
    part_out, grad_out, pre_out, hidden_out, queries = refs[blocks:]
    rows = count * length
    for k in range(1, blocks):
        queries[(k - 1) * rows : k * rows, :] = packed[k][:rows, :]
    own, far = slice(0, rows), slice(rows, blocks * rows)
    for at in range(passages // step):
        part = slice(at * step * tokens, (at + 1) * step * tokens)
        near = coefficients(dims, shares_near, own, weights, 0, at)
        other = coefficients(dims, Columns(shares_other, own), own, weights, passages, at)
        terms = dot(embed[part, :].T, near, 1, 0) + dot(embed_other[part, :].T, other, 1, 0)
        if at == 0:
            part_out[...] = terms
        else:
            part_out[...] += terms
        grad_out[part, :] = dot(near, packed[0][:rows, :], 1, 0) + dot(
            coefficients(dims, shares_far, far, weights, 0, at), queries[...], 1, 0
        )
    pre_out[...] = query_pre[...].T
    hidden_out[...] = query_hidden[...].T


def passage_back_kernel(dims, grad, grad_other, pre, hidden, back_out, weight_out, running):
    blocks, count, length, passages, tokens, slots, step = dims
    for at in range(passages // step):
        part = slice(at * step * tokens, (at + 1) * step * tokens)
        total = grad[part, :] + grad_other[part, :].astype(f32)
        back = normalize_back(pre[part, :], total).astype(bf16)
        back_out[part, :] = back
        terms = dot(back.T, hidden[part, :], 1, 0)
        if at == 0:
            running[...] = terms
        else:
            running[...] += terms
    weight_out[...] = running[...].T


def normalize_back_columns(projected, grad):
    inverse = lax.rsqrt(jnp.sum(projected * projected, axis=0, keepdims=True) + norm_eps)
    along = jnp.sum(projected * grad, axis=0, keepdims=True)
    return grad * inverse - projected * (inverse * inverse * inverse * along)


def query_back_kernel(pre, hidden, weight, *refs):
    parts = refs[:-2]
    back_out, weight_out = refs[-2:]
    grad = sum(part[...].astype(f32) for part in parts)
    back = normalize_back_columns(pre[...], grad).astype(bf16)
    back_out[...] = back
    weight_out[...] = (weight[...] + dot(hidden[...], back, 1, 1)).astype(bf16)


def sum_kernel(parts, copies_out):
    devices = copies_out.shape[0]
    total = parts[0].astype(f32)
    for k in range(1, devices):
        total += parts[k].astype(f32)
    total = total.astype(bf16)
    for k in range(devices):
        copies_out[k] = total


def local(query_hidden, passage_hidden, projection, positive, hard_ids, passage_len):
    count, length, width = query_hidden.shape
    passages, tokens, _ = passage_hidden.shape
    depth = projection.shape[1]
    slots = hard_ids.shape[1]
    groups = lax.axis_size("group")
    devices = lax.axis_size(axes)
    blocks = groups // cores
    rows = count * length
    all_rows = blocks * rows
    far_rows = all_rows - rows
    passage_rows = passages * tokens
    pair = cores * passages
    pool_width = -(-blocks * count // lanes) * lanes
    packet_rows = 1 if 3 * blocks * count < lanes else 8
    step = 4 if blocks <= 2 else 1
    dims = (blocks, count, length, passages, tokens, slots, step)
    query_flat = query_hidden.reshape(rows, width)
    passage_flat = passage_hidden.reshape(passage_rows, width)
    shape = jax.ShapeDtypeStruct

    query_pre, packed, projection_near, lens = pl.pallas_call(
        query_kernel,
        out_shape=(
            shape((rows, depth), f32),
            shape((rows + 16, depth), bf16),
            shape((width, depth), bf16),
            shape((passages, lanes), jnp.int32),
        ),
        in_specs=[HBM] * 5,
        out_specs=(VMEM,) * 4,
        scratch_shapes=[
            pltpu.VMEM((rows, width), bf16),
            pltpu.VMEM((count, slots), jnp.int32),
            pltpu.SMEM((count,), jnp.int32),
            pltpu.SMEM((passages,), jnp.int32),
            pltpu.SemaphoreType.DMA((5,)),
        ],
        compiler_params=params(16),
        cost_estimate=cost(2e10, rows * width * 2),
        name="query_embed",
    )(*in_hbm(query_flat, projection, hard_ids, positive, passage_len))

    def swap(value, k):
        return lax.ppermute(value, "group", [(i, i ^ k) for i in range(groups)])

    queries = [packed] + [swap(packed, cores * k) for k in range(1, blocks)]

    passage_pre, embed, gather, spread = pl.pallas_call(
        functools.partial(passage_kernel, dims),
        out_shape=(
            shape((passage_rows, depth), f32),
            shape((passage_rows + passages, depth), bf16),
            shape((all_rows, pool_width), bf16),
            shape((pool_width, all_rows), bf16),
        ),
        in_specs=[VMEM] * 3,
        out_specs=(VMEM,) * 4,
        compiler_params=params(16),
        cost_estimate=cost(2 * passage_rows * width * depth, passage_rows * (width * 2 + depth * 6)),
        name="passage_embed",
    )(lens, passage_flat, projection_near)
    embed_other = swap(embed, 1)

    def forward_cost(passage_count, query_rows):
        pairs = passage_count * tokens * query_rows
        return cost(2 * pairs * depth, pairs * 2, pairs)

    def forward(name, blocks_of_queries, estimate):
        query_rows = len(blocks_of_queries) * rows
        return pl.pallas_call(
            functools.partial(forward_kernel, dims),
            out_shape=(shape((passage_rows, query_rows), bf16), shape((passages, query_rows), f32)),
            in_specs=[VMEM] * (1 + len(blocks_of_queries)),
            out_specs=(VMEM,) * 2,
            compiler_params=params(16),
            cost_estimate=estimate,
            name=name,
        )(embed, *blocks_of_queries)

    shares_near, summed_near = forward("forward_near", queries[:1], forward_cost(passages, rows))
    shares_far, summed_far = forward("forward_far", queries[1:], cost(1e10, 1e6))
    shares_other, inverse, stats, packets = pl.pallas_call(
        functools.partial(far_kernel, dims),
        out_shape=(
            shape((passage_rows, all_rows), bf16),
            shape((pair, all_rows), f32),
            shape((3 * pair, pool_width), f32),
            shape((devices, packet_rows, pool_width), f32),
        ),
        in_specs=[VMEM] * (blocks + 4),
        out_specs=(VMEM,) * 4,
        scratch_shapes=[
            pltpu.VMEM((pair, all_rows), f32),
            pltpu.VMEM((pool_width, lanes), f32),
        ],
        compiler_params=params(32),
        cost_estimate=forward_cost(passages, all_rows),
        name="forward_other",
    )(*queries, embed_other, summed_near, summed_far, gather)

    packets = lax.all_to_all(packets, axes, 0, 0, tiled=True)

    *far_parts, weights, losses = pl.pallas_call(
        functools.partial(far_grad_kernel, dims),
        out_shape=(
            *[shape((depth, rows), bf16)] * (blocks - 1),
            shape((pair, 1, all_rows), bf16),
            shape((8, pool_width), f32),
        ),
        in_specs=[VMEM] * 8,
        out_specs=(VMEM,) * (blocks + 1),
        scratch_shapes=[pltpu.VMEM((depth, far_rows), f32)],
        compiler_params=params(32),
        cost_estimate=forward_cost(pair, far_rows),
        name="query_grad_far",
    )(packets, stats, inverse, spread, shares_far, shares_other, embed, embed_other)
    far_parts = [swap(part, cores * (k + 1)) for k, part in enumerate(far_parts)]

    grad_other = pl.pallas_call(
        functools.partial(other_grad_kernel, dims),
        out_shape=shape((passage_rows, depth), bf16),
        in_specs=[VMEM] * (2 + blocks),
        out_specs=VMEM,
        scratch_shapes=[pltpu.VMEM((all_rows, depth), bf16)],
        compiler_params=params(32),
        cost_estimate=forward_cost(passages, all_rows),
        name="passage_grad_other",
    )(weights, shares_other, *queries)
    grad_other = swap(grad_other, 1)

    own_part, grad_own, pre_t, hidden_t = pl.pallas_call(
        functools.partial(own_grad_kernel, dims),
        out_shape=(
            shape((depth, rows), f32),
            shape((passage_rows, depth), f32),
            shape((depth, rows), f32),
            shape((width, rows), bf16),
        ),
        in_specs=[VMEM] * (8 + blocks),
        out_specs=(VMEM,) * 4,
        scratch_shapes=[pltpu.VMEM((far_rows, depth), bf16)],
        compiler_params=params(32),
        cost_estimate=forward_cost(pair, all_rows),
        name="own_grads",
    )(
        weights,
        shares_near,
        shares_far,
        shares_other,
        embed,
        embed_other,
        query_pre,
        query_flat,
        *queries,
    )

    passage_back, weight = pl.pallas_call(
        functools.partial(passage_back_kernel, dims),
        out_shape=(shape((passage_rows, depth), bf16), shape((width, depth), f32)),
        in_specs=[VMEM] * 4,
        out_specs=(VMEM,) * 2,
        scratch_shapes=[pltpu.VMEM((depth, width), f32)],
        compiler_params=params(32),
        cost_estimate=cost(2 * passage_rows * width * depth, passage_rows * width * 2),
        name="passage_back",
    )(grad_own, grad_other, passage_pre, passage_flat)

    parts = [*far_parts, own_part]
    query_back, weight = pl.pallas_call(
        query_back_kernel,
        out_shape=(shape((depth, rows), bf16), shape((width, depth), bf16)),
        in_specs=[VMEM] * (3 + blocks),
        out_specs=(VMEM, VMEM),
        compiler_params=params(16),
        cost_estimate=cost(2 * rows * width * depth, width * depth * 6 + rows * width * 2),
        name="query_back",
    )(pre_t, hidden_t, weight, *parts)

    weight = weight.reshape(devices, width // devices, depth)
    weight = lax.all_to_all(weight, axes, 0, 0, tiled=True)
    grad_passage = dot(passage_back, projection, 1, 1).astype(bf16).reshape(passage_hidden.shape)
    weight, grad_passage = lax.optimization_barrier((weight, grad_passage))
    copies = pl.pallas_call(
        sum_kernel,
        out_shape=shape(weight.shape, bf16),
        in_specs=[VMEM],
        out_specs=VMEM,
        compiler_params=params(16),
        name="sum_parts",
    )(weight)
    copies = lax.all_to_all(copies, axes, 0, 0, tiled=True)
    grad_proj = copies.reshape(width, depth).astype(f32)

    grad_query = dot(query_back, projection, 0, 1).astype(bf16).reshape(query_hidden.shape)
    own = lax.axis_index("group") // cores * count
    return (lax.dynamic_slice(losses[0], (own,), (count,)), grad_proj, grad_query, grad_passage)


def solution(mesh):
    in_specs = (
        P(axes, None, None),
        P(axes, None, None),
        P(),
        P(axes),
        P(axes, None),
        P(axes),
    )
    out_specs = (P(axes), P(), P(axes, None, None), P(axes, None, None))
    return jax.shard_map(local, mesh=mesh, in_specs=in_specs, out_specs=out_specs, check_vma=False)
```

```python
import functools

import jax
import jax.numpy as jnp
from jax import lax
from jax.experimental import pallas as pl
from jax.experimental.pallas import tpu as pltpu
from jax.sharding import PartitionSpec as P

smooth_temp = 0.1
norm_eps = 1e-06
center = 0.375
lanes = 128
cores = 2
axes = ("dp", "group")
f32 = jnp.float32
bf16 = jnp.bfloat16


def dot(left, right, left_dim, right_dim):
    return lax.dot_general(
        left, right, (((left_dim,), (right_dim,)), ((), ())), preferred_element_type=f32
    )


def exact_dot(value, picks):
    high = value.astype(bf16)
    rest = value - high.astype(f32)
    middle = rest.astype(bf16)
    low = (rest - middle.astype(f32)).astype(bf16)
    rows = value.shape[0]
    got = dot(jnp.concatenate([high, middle, low], axis=0), picks, 1, 0)
    return got[:rows] + got[rows : 2 * rows] + got[2 * rows :]


def normalize(projected):
    return projected * lax.rsqrt(jnp.sum(projected * projected, axis=-1, keepdims=True) + norm_eps)


def normalize_back(projected, grad):
    inverse = lax.rsqrt(jnp.sum(projected * projected, axis=-1, keepdims=True) + norm_eps)
    along = jnp.sum(projected * grad, axis=-1, keepdims=True)
    return grad * inverse - projected * (inverse * inverse * inverse * along)


def iota(shape, dim):
    return lax.broadcasted_iota(jnp.int32, shape, dim)


def params(megabytes):
    return pltpu.CompilerParams(vmem_limit_bytes=megabytes * 2**20)


def cost(flops, nbytes, exps=0):
    return pl.CostEstimate(flops=int(flops), bytes_accessed=int(nbytes), transcendentals=int(exps))


VMEM = pl.BlockSpec(memory_space=pltpu.VMEM)
HBM = pl.BlockSpec(memory_space=pltpu.HBM)


def in_hbm(*values):
    return [pltpu.with_memory_space_constraint(value, pltpu.HBM) for value in values]


def query_kernel(
    hidden_hbm,
    projection_hbm,
    ids_hbm,
    positive_hbm,
    lens_hbm,
    pre_out,
    packed_out,
    projection,
    lens_out,
    hidden,
    hard_ids,
    positive,
    lens,
    sems,
):
    copies = [
        pltpu.make_async_copy(source, target, sems.at[k])
        for k, (source, target) in enumerate(
            [
                (projection_hbm, projection),
                (hidden_hbm, hidden),
                (ids_hbm, hard_ids),
                (positive_hbm, positive),
                (lens_hbm, lens),
            ]
        )
    ]
    for copy in copies:
        copy.start()
    for copy in copies[2:]:
        copy.wait()
    rows = hidden.shape[0]
    count, slots = hard_ids.shape
    row = iota((count, lanes), 0)
    column = iota((count, lanes), 1)
    marks = jnp.full((count, lanes), -1.0, f32)
    for k in range(count):
        marks = jnp.where((row == k) & (column == slots), positive[k].astype(f32), marks)
    ids = jnp.concatenate(
        [hard_ids[...].astype(f32), jnp.full((count, lanes - slots), -1.0, f32)], axis=1
    )
    marks = jnp.where(column < slots, ids, marks)
    extra = packed_out.shape[0] - rows
    marks = jnp.concatenate([marks, jnp.full((extra - count, lanes), -1.0, f32)], axis=0)
    packed_out[rows:, :] = marks.astype(bf16)
    for p in range(lens_out.shape[0]):
        lens_out[p : p + 1, :] = jnp.full((1, lanes), lens[p], jnp.int32)
    for copy in copies[:2]:
        copy.wait()
    pre = dot(hidden[...], projection[...], 1, 0)
    pre_out[...] = pre
    packed_out[:rows, :] = normalize(pre).astype(bf16)


def parted(index, size):
    if size & (size - 1) == 0:
        return lax.shift_right_logical(index, size.bit_length() - 1)
    return index // size


def token_picks(dims, width, rows_first):
    blocks, count, length = dims[:3]
    chip = lax.axis_index("group") // cores
    tokens = blocks * count * length
    shape = (tokens, width) if rows_first else (width, tokens)
    token = iota(shape, 0 if rows_first else 1)
    query = iota(shape, 1 if rows_first else 0)
    owner = jnp.bitwise_xor(parted(token, length), chip * count)
    return jnp.where(owner == query, 1.0, 0.0).astype(bf16)


def passage_kernel(dims, lens, hidden, projection, pre_out, embed_out, gather_out, spread_out):
    blocks, count, length, passages, tokens, slots, step = dims
    for start in range(0, hidden.shape[0], step * tokens):
        part = slice(start, start + step * tokens)
        pre = dot(hidden[part, :], projection[...], 1, 0)
        pre_out[part, :] = pre
        embed_out[part, :] = normalize(pre).astype(bf16)
    embed_out[hidden.shape[0] :, :] = lens[...].astype(f32).astype(bf16)
    gather_out[...] = token_picks(dims, gather_out.shape[1], True)
    spread_out[...] = token_picks(dims, gather_out.shape[1], False)


def forward_part(dims, embed, queries, shares_out, summed, first):
    blocks, count, length, passages, tokens, slots, step = dims
    rows = count * length
    lens = embed[passages * tokens :, :].astype(f32).astype(jnp.int32)
    for at in range(passages // step):
        part = embed[at * step * tokens : (at + 1) * step * tokens, :]
        for k, block in enumerate(queries):
            columns = slice(k * rows, (k + 1) * rows)
            similar = dot(part, block[:rows, :], 1, 1)
            for p in range(step):
                row = at * step + p
                piece = similar[p * tokens : (p + 1) * tokens, :]
                live = jnp.concatenate([lens[row : row + 1, :]] * (rows // lanes), axis=1)
                grown = jnp.exp(piece * (1.0 / smooth_temp))
                grown = jnp.where(iota(piece.shape, 0) < live, grown, 0.0)
                shares_out[row * tokens : (row + 1) * tokens, columns] = grown.astype(bf16)
                summed[first + row : first + row + 1, columns] = jnp.sum(
                    grown, axis=0, keepdims=True
                )


def forward_kernel(dims, embed, *refs):
    forward_part(dims, embed, refs[:-2], refs[-2], refs[-1], 0)


def far_kernel(dims, *refs):
    blocks, count, length, passages, tokens, slots, step = dims
    packed = refs[:blocks]
    embed_other, summed_near, summed_far, gather, *refs = refs[blocks:]
    shares_other, inverse_out, stats_out, packet_out, summed, marks = refs
    rows = count * length
    me = lax.axis_index("group")
    marks[...] = jnp.full(marks.shape, -1.0, f32)
    for k in range(blocks):
        start = pl.multiple_of(jnp.bitwise_xor(me // cores, k) * count, count)
        marks[pl.ds(start, count), :] = packed[k][rows:, :].astype(f32)[:count]
    forward_part(dims, embed_other, packed, shares_other, summed, passages)
    summed[:passages, :rows] = summed_near[...]
    summed[:passages, rows:] = summed_far[...]
    total = summed[...]
    inverse_out[...] = 1.0 / total
    width = marks.shape[0]
    scores = exact_dot(smooth_temp * jnp.log(total), gather[...])
    marks_t = marks[...].T
    ids = marks_t[:slots, :]
    pair = cores * passages
    first = [me * passages, jnp.bitwise_xor(me, 1) * passages]
    counts = jnp.concatenate(
        [
            jnp.sum(
                jnp.where(ids == (first[p // passages] + p % passages).astype(f32), 1.0, 0.0),
                axis=0,
                keepdims=True,
            )
            for p in range(pair)
        ],
        axis=0,
    )
    row = iota((pair, width), 0)
    here = jnp.where(row < passages, row + first[0], row - passages + first[1])
    chosen = here.astype(f32) == marks_t[slots : slots + 1, :]
    grown = jnp.exp(scores - center * length)
    boost = blocks * pair / slots
    boosted = jnp.where(chosen, 0.0, boost * counts)
    stats_out[:pair, :] = grown
    stats_out[pair : 2 * pair, :] = boosted
    stats_out[2 * pair :, :] = jnp.where(chosen, 1.0, 0.0)
    plain = jnp.sum(grown, axis=0, keepdims=True)
    hard = jnp.sum(boosted * grown * grown, axis=0, keepdims=True)
    kept = jnp.sum(jnp.where(chosen, scores, 0.0), axis=0, keepdims=True)
    sums = jnp.sum(counts * grown, axis=0, keepdims=True)
    sums = jnp.broadcast_to(jnp.sum(sums, axis=1, keepdims=True), sums.shape)
    queries = blocks * count
    if packet_out.shape[1] == 1:
        lane = iota(plain.shape, 1)
        packet = jnp.where(lane < queries, plain, sums)
        packet = jnp.where(lane // queries == 1, pltpu.roll(hard, queries, 1), packet)
        packet = jnp.where(lane // queries == 2, pltpu.roll(kept, 2 * queries, 1), packet)
    else:
        packet = jnp.concatenate([plain, hard, kept, sums] * 2, axis=0)
    for k in range(packet_out.shape[0]):
        packet_out[k] = packet


def coefficients(dims, shares, columns, weights, first, at):
    passages, tokens, _, step = dims[3:]
    parts = []
    for p in range(at * step, (at + 1) * step):
        parts.append(shares[p * tokens : (p + 1) * tokens, :] * weights[first + p, :, columns])
    return jnp.concatenate(parts, axis=0)


class Columns:
    def __init__(self, ref, columns):
        self.ref, self.columns = ref, columns

    def __getitem__(self, index):
        return self.ref[index[0], self.columns]


def far_grad_kernel(
    dims,
    packets,
    stats,
    inverse,
    spread,
    shares_far,
    shares_other,
    embed,
    embed_other,
    *refs,
):
    blocks, count, length, passages, tokens, slots, step = dims
    packed, refs = refs[:blocks], refs[blocks:]
    parts_out = refs[: blocks - 1]
    weights, losses_out, grad_out, running, all_queries = refs[blocks - 1 :]
    rows = count * length
    pair = cores * passages
    width = stats.shape[1]
    devices = packets.shape[0]
    groups = cores * blocks
    core = lax.axis_index("group") % cores
    pool = packets[pl.ds(lax.axis_index("dp") * groups, groups)]
    pool = jnp.where(iota(pool.shape, 0) % cores == core, pool, 0.0).sum(axis=0)
    every = packets[...].sum(axis=0)
    queries = blocks * count
    if packets.shape[1] == 1:
        plain = pool
        hard = pltpu.roll(pool, width - queries, 1)
        kept = pltpu.roll(pool, width - 2 * queries, 1)
        sums = every[:, 3 * queries : 3 * queries + 1]
    else:
        plain, hard, kept, sums = pool[0:1, :], pool[1:2, :], pool[2:3, :], every[3:4, 0:1]
    hard_mean = sums * (1.0 / (devices * count * slots))
    partition = jnp.where(iota(plain.shape, 1) < queries, plain + hard / hard_mean, 1.0)
    losses = jnp.broadcast_to(
        jnp.log(partition) - (kept - center * length), losses_out.shape
    )
    chip = lax.axis_index("group") // cores
    losses_out[...] = pltpu.roll(losses, width - chip * count, 1)
    grown = stats[:pair, :]
    boosted = stats[pair : 2 * pair, :]
    chosen = stats[2 * pair :, :]
    grad = grown * (1.0 + boosted * grown / hard_mean) / partition - chosen
    found = (exact_dot(grad, spread[...]) * inverse[...]).astype(bf16)
    for p in range(pair):
        weights[p] = found[p : p + 1, :]
    for k in range(blocks):
        all_queries[k * rows : (k + 1) * rows, :] = packed[k][:rows, :]
    everything, far = slice(0, blocks * rows), slice(rows, blocks * rows)
    for at in range(passages // step):
        part = slice(at * step * tokens, (at + 1) * step * tokens)
        other = coefficients(dims, shares_other, everything, weights, passages, at)
        own = coefficients(dims, shares_far, far, weights, 0, at)
        terms = dot(embed_other[part, :].T, other[:, rows:], 1, 0)
        terms += dot(embed[part, :].T, own, 1, 0)
        if at == 0:
            running[...] = terms
        else:
            running[...] += terms
        grad_out[part, :] = dot(other, all_queries[...], 1, 0).astype(bf16)
    for k, out in enumerate(parts_out):
        out[...] = running[:, k * rows : (k + 1) * rows].astype(bf16)


def own_grad_kernel(
    dims,
    weights,
    shares_near,
    shares_far,
    shares_other,
    embed,
    embed_other,
    query_pre,
    query_hidden,
    *refs,
):
    blocks, count, length, passages, tokens, slots, step = dims
    packed = refs[:blocks]
    part_out, grad_out, pre_out, hidden_out, queries = refs[blocks:]
    rows = count * length
    for k in range(1, blocks):
        queries[(k - 1) * rows : k * rows, :] = packed[k][:rows, :]
    own, far = slice(0, rows), slice(rows, blocks * rows)
    for at in range(passages // step):
        part = slice(at * step * tokens, (at + 1) * step * tokens)
        near = coefficients(dims, shares_near, own, weights, 0, at)
        other = coefficients(dims, Columns(shares_other, own), own, weights, passages, at)
        terms = dot(embed[part, :].T, near, 1, 0) + dot(embed_other[part, :].T, other, 1, 0)
        if at == 0:
            part_out[...] = terms
        else:
            part_out[...] += terms
        grad_out[part, :] = dot(near, packed[0][:rows, :], 1, 0) + dot(
            coefficients(dims, shares_far, far, weights, 0, at), queries[...], 1, 0
        )
    pre_out[...] = query_pre[...].T
    hidden_out[...] = query_hidden[...].T


def passage_back_kernel(
    dims,
    grad,
    grad_other,
    pre,
    hidden,
    projection,
    weight_out,
    grad_hidden_hbm,
    running,
    grad_hidden,
    sems,
):
    blocks, count, length, passages, tokens, slots, step = dims
    copies = []
    for at in range(passages // step):
        part = slice(at * step * tokens, (at + 1) * step * tokens)
        total = grad[part, :] + grad_other[part, :].astype(f32)
        back = normalize_back(pre[part, :], total).astype(bf16)
        grad_hidden[part, :] = dot(back, projection[...], 1, 1).astype(bf16)
        rows = pl.ds(at * step * tokens, step * tokens)
        copy = pltpu.make_async_copy(grad_hidden.at[rows], grad_hidden_hbm.at[rows], sems.at[at])
        copy.start()
        copies.append(copy)
        terms = dot(back.T, hidden[part, :], 1, 0)
        if at == 0:
            running[...] = terms
        else:
            running[...] += terms
    weight_out[...] = running[...].T
    for copy in copies:
        copy.wait()


def normalize_back_columns(projected, grad):
    inverse = lax.rsqrt(jnp.sum(projected * projected, axis=0, keepdims=True) + norm_eps)
    along = jnp.sum(projected * grad, axis=0, keepdims=True)
    return grad * inverse - projected * (inverse * inverse * inverse * along)


def query_back_kernel(pre, hidden, weight, *refs):
    parts = refs[:-2]
    back_out, weight_out = refs[-2:]
    grad = sum(part[...].astype(f32) for part in parts)
    back = normalize_back_columns(pre[...], grad).astype(bf16)
    back_out[...] = back
    weight_out[...] = (weight[...] + dot(hidden[...], back, 1, 1)).astype(bf16)


def sum_kernel(parts, copies_out):
    devices = copies_out.shape[0]
    total = parts[0].astype(f32)
    for k in range(1, devices):
        total += parts[k].astype(f32)
    total = total.astype(bf16)
    for k in range(devices):
        copies_out[k] = total


def final_kernel(copies, back, projection, losses, grad_proj_out, grad_query_out, losses_out):
    grad_proj_out[...] = copies[...].astype(f32)
    grad_query_out[...] = dot(back[...].T, projection[...], 1, 1).astype(bf16)
    losses_out[...] = losses[0, : losses_out.shape[0]]


def local(query_hidden, passage_hidden, projection, positive, hard_ids, passage_len):
    count, length, width = query_hidden.shape
    passages, tokens, _ = passage_hidden.shape
    depth = projection.shape[1]
    slots = hard_ids.shape[1]
    groups = lax.axis_size("group")
    devices = lax.axis_size(axes)
    blocks = groups // cores
    rows = count * length
    all_rows = blocks * rows
    far_rows = all_rows - rows
    passage_rows = passages * tokens
    pair = cores * passages
    pool_width = -(-blocks * count // lanes) * lanes
    packet_rows = 1 if 3 * blocks * count < lanes else 8
    step = 4 if blocks <= 2 else 1
    dims = (blocks, count, length, passages, tokens, slots, step)
    query_flat = query_hidden.reshape(rows, width)
    passage_flat = passage_hidden.reshape(passage_rows, width)
    shape = jax.ShapeDtypeStruct

    query_pre, packed, projection_near, lens = pl.pallas_call(
        query_kernel,
        out_shape=(
            shape((rows, depth), f32),
            shape((rows + 16, depth), bf16),
            shape((width, depth), bf16),
            shape((passages, lanes), jnp.int32),
        ),
        in_specs=[HBM] * 5,
        out_specs=(VMEM,) * 4,
        scratch_shapes=[
            pltpu.VMEM((rows, width), bf16),
            pltpu.VMEM((count, slots), jnp.int32),
            pltpu.SMEM((count,), jnp.int32),
            pltpu.SMEM((passages,), jnp.int32),
            pltpu.SemaphoreType.DMA((5,)),
        ],
        compiler_params=params(16),
        cost_estimate=cost(2e10, rows * width * 2),
        name="query_embed",
    )(*in_hbm(query_flat, projection, hard_ids, positive, passage_len))

    def swap(value, k):
        return lax.ppermute(value, "group", [(i, i ^ k) for i in range(groups)])

    queries = [packed] + [swap(packed, cores * k) for k in range(1, blocks)]

    passage_pre, embed, gather, spread = pl.pallas_call(
        functools.partial(passage_kernel, dims),
        out_shape=(
            shape((passage_rows, depth), f32),
            shape((passage_rows + passages, depth), bf16),
            shape((all_rows, pool_width), bf16),
            shape((pool_width, all_rows), bf16),
        ),
        in_specs=[VMEM] * 3,
        out_specs=(VMEM,) * 4,
        compiler_params=params(16),
        cost_estimate=cost(2 * passage_rows * width * depth, passage_rows * (width * 2 + depth * 6)),
        name="passage_embed",
    )(lens, passage_flat, projection_near)
    embed_other = swap(embed, 1)

    def forward_cost(passage_count, query_rows):
        pairs = passage_count * tokens * query_rows
        return cost(2 * pairs * depth, pairs * 2, pairs)

    def forward(name, blocks_of_queries, estimate):
        query_rows = len(blocks_of_queries) * rows
        return pl.pallas_call(
            functools.partial(forward_kernel, dims),
            out_shape=(shape((passage_rows, query_rows), bf16), shape((passages, query_rows), f32)),
            in_specs=[VMEM] * (1 + len(blocks_of_queries)),
            out_specs=(VMEM,) * 2,
            compiler_params=params(16),
            cost_estimate=estimate,
            name=name,
        )(embed, *blocks_of_queries)

    shares_near, summed_near = forward("forward_near", queries[:1], forward_cost(passages, rows))
    shares_far, summed_far = forward("forward_far", queries[1:], cost(1e10, 1e6))
    shares_other, inverse, stats, packets = pl.pallas_call(
        functools.partial(far_kernel, dims),
        out_shape=(
            shape((passage_rows, all_rows), bf16),
            shape((pair, all_rows), f32),
            shape((3 * pair, pool_width), f32),
            shape((devices, packet_rows, pool_width), f32),
        ),
        in_specs=[VMEM] * (blocks + 4),
        out_specs=(VMEM,) * 4,
        scratch_shapes=[
            pltpu.VMEM((pair, all_rows), f32),
            pltpu.VMEM((pool_width, lanes), f32),
        ],
        compiler_params=params(32),
        cost_estimate=forward_cost(passages, all_rows),
        name="forward_other",
    )(*queries, embed_other, summed_near, summed_far, gather)

    packets = lax.all_to_all(packets, axes, 0, 0, tiled=True)

    *far_parts, weights, losses, grad_other = pl.pallas_call(
        functools.partial(far_grad_kernel, dims),
        out_shape=(
            *[shape((depth, rows), bf16)] * (blocks - 1),
            shape((pair, 1, all_rows), bf16),
            shape((8, pool_width), f32),
            shape((passage_rows, depth), bf16),
        ),
        in_specs=[VMEM] * (8 + blocks),
        out_specs=(VMEM,) * (blocks + 2),
        scratch_shapes=[
            pltpu.VMEM((depth, far_rows), f32),
            pltpu.VMEM((all_rows, depth), bf16),
        ],
        compiler_params=params(32),
        cost_estimate=forward_cost(pair, all_rows),
        name="far_grads",
    )(packets, stats, inverse, spread, shares_far, shares_other, embed, embed_other, *queries)
    grad_other = swap(grad_other, 1)
    far_parts = [swap(part, cores * (k + 1)) for k, part in enumerate(far_parts)]

    own_part, grad_own, pre_t, hidden_t = pl.pallas_call(
        functools.partial(own_grad_kernel, dims),
        out_shape=(
            shape((depth, rows), f32),
            shape((passage_rows, depth), f32),
            shape((depth, rows), f32),
            shape((width, rows), bf16),
        ),
        in_specs=[VMEM] * (8 + blocks),
        out_specs=(VMEM,) * 4,
        scratch_shapes=[pltpu.VMEM((far_rows, depth), bf16)],
        compiler_params=params(32),
        cost_estimate=forward_cost(pair, all_rows),
        name="own_grads",
    )(
        weights,
        shares_near,
        shares_far,
        shares_other,
        embed,
        embed_other,
        query_pre,
        query_flat,
        *queries,
    )

    weight, grad_passage = pl.pallas_call(
        functools.partial(passage_back_kernel, dims),
        out_shape=(shape((width, depth), f32), shape((passage_rows, width), bf16)),
        in_specs=[VMEM] * 5,
        out_specs=(VMEM, HBM),
        scratch_shapes=[
            pltpu.VMEM((depth, width), f32),
            pltpu.VMEM((passage_rows, width), bf16),
            pltpu.SemaphoreType.DMA((passages // step,)),
        ],
        compiler_params=params(32),
        cost_estimate=cost(4 * passage_rows * width * depth, passage_rows * width * 4),
        name="passage_back",
    )(grad_own, grad_other, passage_pre, passage_flat, projection_near)

    parts = [*far_parts, own_part]
    query_back, weight = pl.pallas_call(
        query_back_kernel,
        out_shape=(shape((depth, rows), bf16), shape((width, depth), bf16)),
        in_specs=[VMEM] * (3 + blocks),
        out_specs=(VMEM, VMEM),
        compiler_params=params(16),
        cost_estimate=cost(2 * rows * width * depth, width * depth * 6 + rows * width * 2),
        name="query_back",
    )(pre_t, hidden_t, weight, *parts)

    weight = weight.reshape(devices, width // devices, depth)
    weight = lax.all_to_all(weight, axes, 0, 0, tiled=True)
    copies = pl.pallas_call(
        sum_kernel,
        out_shape=shape(weight.shape, bf16),
        in_specs=[VMEM],
        out_specs=VMEM,
        compiler_params=params(16),
        name="sum_parts",
    )(weight)
    copies = lax.all_to_all(copies, axes, 0, 0, tiled=True)
    grad_proj, grad_query, losses = pl.pallas_call(
        final_kernel,
        out_shape=(shape((width, depth), f32), shape((rows, width), bf16), shape((count,), f32)),
        in_specs=[VMEM] * 4,
        out_specs=(VMEM,) * 3,
        compiler_params=params(16),
        cost_estimate=cost(2 * rows * width * depth, rows * width * 4),
        name="outputs",
    )(copies.reshape(width, depth), query_back, projection_near, losses)
    return (
        losses,
        grad_proj,
        grad_query.reshape(query_hidden.shape),
        grad_passage.reshape(passage_hidden.shape),
    )


def solution(mesh):
    in_specs = (
        P(axes, None, None),
        P(axes, None, None),
        P(),
        P(axes),
        P(axes, None),
        P(axes),
    )
    out_specs = (P(axes), P(), P(axes, None, None), P(axes, None, None))
    return jax.shard_map(local, mesh=mesh, in_specs=in_specs, out_specs=out_specs, check_vma=False)
```

```python
import functools

import jax
import jax.numpy as jnp
from jax import lax
from jax.experimental import pallas as pl
from jax.experimental.pallas import tpu as pltpu
from jax.sharding import PartitionSpec as P

smooth_temp = 0.1
norm_eps = 1e-06
center = 0.375
lanes = 128
cores = 2
axes = ("dp", "group")
f32 = jnp.float32
bf16 = jnp.bfloat16


def dot(left, right, left_dim, right_dim):
    return lax.dot_general(
        left, right, (((left_dim,), (right_dim,)), ((), ())), preferred_element_type=f32
    )


def exact_dot(value, picks):
    high = value.astype(bf16)
    rest = value - high.astype(f32)
    middle = rest.astype(bf16)
    low = (rest - middle.astype(f32)).astype(bf16)
    rows = value.shape[0]
    got = dot(jnp.concatenate([high, middle, low], axis=0), picks, 1, 0)
    return got[:rows] + got[rows : 2 * rows] + got[2 * rows :]


def normalize(projected):
    return projected * lax.rsqrt(jnp.sum(projected * projected, axis=-1, keepdims=True) + norm_eps)


def normalize_back(projected, grad):
    inverse = lax.rsqrt(jnp.sum(projected * projected, axis=-1, keepdims=True) + norm_eps)
    along = jnp.sum(projected * grad, axis=-1, keepdims=True)
    return grad * inverse - projected * (inverse * inverse * inverse * along)


def iota(shape, dim):
    return lax.broadcasted_iota(jnp.int32, shape, dim)


def params(megabytes):
    return pltpu.CompilerParams(vmem_limit_bytes=megabytes * 2**20)


def cost(flops, nbytes, exps=0):
    return pl.CostEstimate(flops=int(flops), bytes_accessed=int(nbytes), transcendentals=int(exps))


VMEM = pl.BlockSpec(memory_space=pltpu.VMEM)
HBM = pl.BlockSpec(memory_space=pltpu.HBM)


def in_hbm(*values):
    return [pltpu.with_memory_space_constraint(value, pltpu.HBM) for value in values]


def query_kernel(
    hidden_hbm,
    projection_hbm,
    ids_hbm,
    positive_hbm,
    pre_out,
    packed_out,
    projection,
    hidden,
    hard_ids,
    positive,
    sems,
):
    copies = [
        pltpu.make_async_copy(source, target, sems.at[k])
        for k, (source, target) in enumerate(
            [
                (projection_hbm, projection),
                (hidden_hbm, hidden),
                (ids_hbm, hard_ids),
                (positive_hbm, positive),
            ]
        )
    ]
    for copy in copies:
        copy.start()
    for copy in copies[2:]:
        copy.wait()
    rows = hidden.shape[0]
    count, slots = hard_ids.shape
    row = iota((count, lanes), 0)
    column = iota((count, lanes), 1)
    marks = jnp.full((count, lanes), -1.0, f32)
    for k in range(count):
        marks = jnp.where((row == k) & (column == slots), positive[k].astype(f32), marks)
    ids = jnp.concatenate(
        [hard_ids[...].astype(f32), jnp.full((count, lanes - slots), -1.0, f32)], axis=1
    )
    marks = jnp.where(column < slots, ids, marks)
    extra = packed_out.shape[0] - rows
    marks = jnp.concatenate([marks, jnp.full((extra - count, lanes), -1.0, f32)], axis=0)
    packed_out[rows:, :] = marks.astype(bf16)
    for copy in copies[:2]:
        copy.wait()
    pre = dot(hidden[...], projection[...], 1, 0)
    pre_out[...] = pre
    packed_out[:rows, :] = normalize(pre).astype(bf16)


def parted(index, size):
    if size & (size - 1) == 0:
        return lax.shift_right_logical(index, size.bit_length() - 1)
    return index // size


def token_picks(dims, width, rows_first):
    blocks, count, length = dims[:3]
    chip = lax.axis_index("group") // cores
    tokens = blocks * count * length
    shape = (tokens, width) if rows_first else (width, tokens)
    token = iota(shape, 0 if rows_first else 1)
    query = iota(shape, 1 if rows_first else 0)
    owner = jnp.bitwise_xor(parted(token, length), chip * count)
    return jnp.where(owner == query, 1.0, 0.0).astype(bf16)


def passage_kernel(dims, lens, hidden, projection, pre_out, embed_out):
    blocks, count, length, passages, tokens, slots, step = dims
    for start in range(0, hidden.shape[0], step * tokens):
        part = slice(start, start + step * tokens)
        pre = dot(hidden[part, :], projection[...], 1, 0)
        pre_out[part, :] = pre
        embed_out[part, :] = normalize(pre).astype(bf16)
    row = jnp.broadcast_to(lens[...].astype(f32).reshape(1, passages), (passages, passages))
    own = iota(row.shape, 0) == iota(row.shape, 1)
    column = jnp.sum(jnp.where(own, row, 0.0), axis=1, keepdims=True)
    embed_out[hidden.shape[0] :, :] = jnp.broadcast_to(column, (passages, lanes)).astype(bf16)


def forward_part(dims, embed, queries, shares_out, summed, first):
    blocks, count, length, passages, tokens, slots, step = dims
    rows = count * length
    lens = embed[passages * tokens :, :].astype(f32).astype(jnp.int32)
    for at in range(passages // step):
        part = embed[at * step * tokens : (at + 1) * step * tokens, :]
        for k, block in enumerate(queries):
            columns = slice(k * rows, (k + 1) * rows)
            similar = dot(part, block[:rows, :], 1, 1)
            for p in range(step):
                row = at * step + p
                piece = similar[p * tokens : (p + 1) * tokens, :]
                live = jnp.concatenate([lens[row : row + 1, :]] * (rows // lanes), axis=1)
                grown = jnp.exp(piece * (1.0 / smooth_temp))
                grown = jnp.where(iota(piece.shape, 0) < live, grown, 0.0)
                shares_out[row * tokens : (row + 1) * tokens, columns] = grown.astype(bf16)
                summed[first + row : first + row + 1, columns] = jnp.sum(
                    grown, axis=0, keepdims=True
                )


def near_kernel(dims, embed, packed, shares_out, summed_out, gather_out, spread_out):
    forward_part(dims, embed, [packed], shares_out, summed_out, 0)
    gather_out[...] = token_picks(dims, gather_out.shape[1], True)
    spread_out[...] = token_picks(dims, gather_out.shape[1], False)


def other_kernel(dims, embed, packed, shares_out, summed_out):
    forward_part(dims, embed, [packed], shares_out, summed_out, 0)


def far_kernel(dims, *refs):
    blocks, count, length, passages, tokens, slots, step = dims
    packed = refs[:blocks]
    embed, embed_other, summed_near, summed_other, gather, *refs = refs[blocks:]
    shares_far, shares_other, inverse_out, stats_out, packet_out, summed, summed_far, marks = refs
    rows = count * length
    me = lax.axis_index("group")
    marks[...] = jnp.full(marks.shape, -1.0, f32)
    for k in range(blocks):
        start = pl.multiple_of(jnp.bitwise_xor(me // cores, k) * count, count)
        marks[pl.ds(start, count), :] = packed[k][rows:, :].astype(f32)[:count]
    forward_part(dims, embed, packed[1:], shares_far, summed_far, 0)
    forward_part(dims, embed_other, packed[1:], shares_other, summed_far, passages)
    summed[:passages, :rows] = summed_near[...]
    summed[passages:, :rows] = summed_other[...]
    summed[:, rows:] = summed_far[...]
    total = summed[...]
    inverse_out[...] = 1.0 / total
    width = marks.shape[0]
    scores = exact_dot(smooth_temp * jnp.log(total), gather[...])
    marks_t = marks[...].T
    pair = cores * passages
    row = iota((pair, width), 0)
    other = jnp.bitwise_xor(me, 1)
    here = jnp.where(row < passages, row + me * passages, row + (other - 1) * passages)
    here = here.astype(f32)
    chosen = here == marks_t[slots : slots + 1, :]
    counts = jnp.zeros((pair, width), f32)
    for k in range(slots):
        counts += jnp.where(here == marks_t[k : k + 1, :], 1.0, 0.0)
    grown = jnp.exp(scores - center * length)
    boost = blocks * pair / slots
    boosted = jnp.where(chosen, 0.0, boost * counts)
    stats_out[:pair, :] = grown
    stats_out[pair : 2 * pair, :] = boosted
    stats_out[2 * pair :, :] = jnp.where(chosen, 1.0, 0.0)
    plain = jnp.sum(grown, axis=0, keepdims=True)
    hard = jnp.sum(boosted * grown * grown, axis=0, keepdims=True)
    kept = jnp.sum(jnp.where(chosen, scores, 0.0), axis=0, keepdims=True)
    sums = jnp.sum(counts * grown, axis=0, keepdims=True)
    sums = jnp.broadcast_to(jnp.sum(sums, axis=1, keepdims=True), sums.shape)
    queries = blocks * count
    if packet_out.shape[1] == 1:
        lane = iota(plain.shape, 1)
        packet = jnp.where(lane < queries, plain, sums)
        packet = jnp.where(lane // queries == 1, pltpu.roll(hard, queries, 1), packet)
        packet = jnp.where(lane // queries == 2, pltpu.roll(kept, 2 * queries, 1), packet)
    else:
        packet = jnp.concatenate([plain, hard, kept, sums] * 2, axis=0)
    for k in range(packet_out.shape[0]):
        packet_out[k] = packet


def coefficients(dims, shares, columns, weights, first, at):
    passages, tokens, _, step = dims[3:]
    parts = []
    for p in range(at * step, (at + 1) * step):
        weight = weights[first + p : first + p + 1, columns]
        weight = jnp.broadcast_to(weight, (tokens, weight.shape[1])).astype(bf16)
        parts.append(shares[p * tokens : (p + 1) * tokens, :] * weight)
    return jnp.concatenate(parts, axis=0)


def far_grad_kernel(
    dims,
    packets,
    stats,
    inverse,
    spread,
    shares_far,
    shares_other_near,
    shares_other_far,
    embed,
    embed_other,
    *refs,
):
    blocks, count, length, passages, tokens, slots, step = dims
    packed, refs = refs[:blocks], refs[blocks:]
    parts_out = refs[: blocks - 1]
    weights, losses_out, grad_out, running, far_queries = refs[blocks - 1 :]
    rows = count * length
    pair = cores * passages
    width = stats.shape[1]
    devices = packets.shape[0]
    groups = cores * blocks
    core = lax.axis_index("group") % cores
    pool = packets[pl.ds(lax.axis_index("dp") * groups, groups)]
    pool = jnp.where(iota(pool.shape, 0) % cores == core, pool, 0.0).sum(axis=0)
    every = packets[...].sum(axis=0)
    queries = blocks * count
    if packets.shape[1] == 1:
        plain = pool
        hard = pltpu.roll(pool, width - queries, 1)
        kept = pltpu.roll(pool, width - 2 * queries, 1)
        sums = every[:, 3 * queries : 3 * queries + 1]
    else:
        plain, hard, kept, sums = pool[0:1, :], pool[1:2, :], pool[2:3, :], every[3:4, 0:1]
    hard_mean = sums * (1.0 / (devices * count * slots))
    partition = jnp.where(iota(plain.shape, 1) < queries, plain + hard / hard_mean, 1.0)
    losses = jnp.broadcast_to(
        jnp.log(partition) - (kept - center * length), losses_out.shape
    )
    chip = lax.axis_index("group") // cores
    losses_out[...] = pltpu.roll(losses, width - chip * count, 1)
    grown = stats[:pair, :]
    boosted = stats[pair : 2 * pair, :]
    chosen = stats[2 * pair :, :]
    grad = grown * (1.0 + boosted * grown / hard_mean) / partition - chosen
    found = exact_dot(grad, spread[...]) * inverse[...]
    weights[...] = found
    for k in range(1, blocks):
        far_queries[(k - 1) * rows : k * rows, :] = packed[k][:rows, :]
    near, far = slice(0, rows), slice(rows, blocks * rows)
    for at in range(passages // step):
        part = slice(at * step * tokens, (at + 1) * step * tokens)
        own = coefficients(dims, shares_far, far, weights, 0, at)
        other_near = coefficients(dims, shares_other_near, near, weights, passages, at)
        other_far = coefficients(dims, shares_other_far, far, weights, passages, at)
        terms = dot(embed[part, :].T, own, 1, 0) + dot(embed_other[part, :].T, other_far, 1, 0)
        if at == 0:
            running[...] = terms
        else:
            running[...] += terms
        grad = dot(other_near, packed[0][:rows, :], 1, 0) + dot(other_far, far_queries[...], 1, 0)
        grad_out[part, :] = grad.astype(bf16)
    for k, out in enumerate(parts_out):
        out[...] = running[:, k * rows : (k + 1) * rows].astype(bf16)


def own_grad_kernel(
    dims,
    weights,
    shares_near,
    shares_far,
    shares_other,
    embed,
    embed_other,
    query_pre,
    query_hidden,
    *refs,
):
    blocks, count, length, passages, tokens, slots, step = dims
    packed = refs[:blocks]
    part_out, grad_out, pre_out, hidden_out, queries = refs[blocks:]
    rows = count * length
    for k in range(1, blocks):
        queries[(k - 1) * rows : k * rows, :] = packed[k][:rows, :]
    own, far = slice(0, rows), slice(rows, blocks * rows)
    for at in range(passages // step):
        part = slice(at * step * tokens, (at + 1) * step * tokens)
        near = coefficients(dims, shares_near, own, weights, 0, at)
        other = coefficients(dims, shares_other, own, weights, passages, at)
        terms = dot(embed[part, :].T, near, 1, 0) + dot(embed_other[part, :].T, other, 1, 0)
        if at == 0:
            part_out[...] = terms
        else:
            part_out[...] += terms
        grad_out[part, :] = dot(near, packed[0][:rows, :], 1, 0) + dot(
            coefficients(dims, shares_far, far, weights, 0, at), queries[...], 1, 0
        )
    pre_out[...] = query_pre[...].T
    hidden_out[...] = query_hidden[...].T


def passage_back_kernel(
    dims,
    grad,
    grad_other,
    pre,
    hidden,
    projection,
    weight_out,
    grad_hidden_hbm,
    running,
    grad_hidden,
    sems,
):
    blocks, count, length, passages, tokens, slots, step = dims
    copies = []
    for at in range(passages // step):
        part = slice(at * step * tokens, (at + 1) * step * tokens)
        total = grad[part, :] + grad_other[part, :].astype(f32)
        back = normalize_back(pre[part, :], total).astype(bf16)
        grad_hidden[part, :] = dot(back, projection[...], 1, 1).astype(bf16)
        rows = pl.ds(at * step * tokens, step * tokens)
        copy = pltpu.make_async_copy(grad_hidden.at[rows], grad_hidden_hbm.at[rows], sems.at[at])
        copy.start()
        copies.append(copy)
        terms = dot(back.T, hidden[part, :], 1, 0)
        if at == 0:
            running[...] = terms
        else:
            running[...] += terms
    weight_out[...] = running[...].T
    for copy in copies:
        copy.wait()


def normalize_back_columns(projected, grad):
    inverse = lax.rsqrt(jnp.sum(projected * projected, axis=0, keepdims=True) + norm_eps)
    along = jnp.sum(projected * grad, axis=0, keepdims=True)
    return grad * inverse - projected * (inverse * inverse * inverse * along)


def query_back_kernel(pre, hidden, weight, *refs):
    parts = refs[:-2]
    back_out, weight_out = refs[-2:]
    grad = sum(part[...].astype(f32) for part in parts)
    back = normalize_back_columns(pre[...], grad).astype(bf16)
    back_out[...] = back
    weight_out[...] = (weight[...] + dot(hidden[...], back, 1, 1)).astype(bf16)


def sum_kernel(parts, copies_out):
    devices = copies_out.shape[0]
    total = parts[0].astype(f32)
    for k in range(1, devices):
        total += parts[k].astype(f32)
    total = total.astype(bf16)
    for k in range(devices):
        copies_out[k] = total


def final_kernel(copies, back, projection, losses, grad_proj_out, grad_query_out, losses_out):
    grad_proj_out[...] = copies[...].astype(f32)
    grad_query_out[...] = dot(back[...].T, projection[...], 1, 1).astype(bf16)
    losses_out[...] = losses[0, : losses_out.shape[0]]


def local(query_hidden, passage_hidden, projection, positive, hard_ids, passage_len):
    count, length, width = query_hidden.shape
    passages, tokens, _ = passage_hidden.shape
    depth = projection.shape[1]
    slots = hard_ids.shape[1]
    groups = lax.axis_size("group")
    devices = lax.axis_size(axes)
    blocks = groups // cores
    rows = count * length
    all_rows = blocks * rows
    far_rows = all_rows - rows
    passage_rows = passages * tokens
    pair = cores * passages
    pool_width = -(-blocks * count // lanes) * lanes
    packet_rows = 1 if 3 * blocks * count < lanes else 8
    step = 4 if blocks <= 2 else 1
    dims = (blocks, count, length, passages, tokens, slots, step)
    query_flat = query_hidden.reshape(rows, width)
    passage_flat = passage_hidden.reshape(passage_rows, width)
    shape = jax.ShapeDtypeStruct

    query_pre, packed, projection_near = pl.pallas_call(
        query_kernel,
        out_shape=(
            shape((rows, depth), f32),
            shape((rows + 16, depth), bf16),
            shape((width, depth), bf16),
        ),
        in_specs=[HBM] * 4,
        out_specs=(VMEM,) * 3,
        scratch_shapes=[
            pltpu.VMEM((rows, width), bf16),
            pltpu.VMEM((count, slots), jnp.int32),
            pltpu.SMEM((count,), jnp.int32),
            pltpu.SemaphoreType.DMA((4,)),
        ],
        compiler_params=params(16),
        cost_estimate=cost(2e10, rows * width * 2),
        name="query_embed",
    )(*in_hbm(query_flat, projection, hard_ids, positive))

    def swap(value, k):
        return lax.ppermute(value, "group", [(i, i ^ k) for i in range(groups)])

    queries = [packed] + [swap(packed, cores * k) for k in range(1, blocks)]

    passage_pre, embed = pl.pallas_call(
        functools.partial(passage_kernel, dims),
        out_shape=(
            shape((passage_rows, depth), f32),
            shape((passage_rows + passages, depth), bf16),
        ),
        in_specs=[VMEM] * 3,
        out_specs=(VMEM,) * 2,
        compiler_params=params(16),
        cost_estimate=cost(2 * passage_rows * width * depth, passage_rows * (width * 2 + depth * 6)),
        name="passage_embed",
    )(passage_len, passage_flat, projection_near)
    embed_other = swap(embed, 1)

    def forward_cost(passage_count, query_rows):
        pairs = passage_count * tokens * query_rows
        return cost(2 * pairs * depth, pairs * 2, pairs)

    shares_near, summed_near, gather, spread = pl.pallas_call(
        functools.partial(near_kernel, dims),
        out_shape=(
            shape((passage_rows, rows), bf16),
            shape((passages, rows), f32),
            shape((all_rows, pool_width), bf16),
            shape((pool_width, all_rows), bf16),
        ),
        in_specs=[VMEM] * 2,
        out_specs=(VMEM,) * 4,
        compiler_params=params(16),
        cost_estimate=cost(5e10, 1e6),
        name="forward_near",
    )(embed, packed)
    shares_other_near, summed_other = pl.pallas_call(
        functools.partial(other_kernel, dims),
        out_shape=(shape((passage_rows, rows), bf16), shape((passages, rows), f32)),
        in_specs=[VMEM] * 2,
        out_specs=(VMEM,) * 2,
        compiler_params=params(16),
        cost_estimate=forward_cost(passages, rows),
        name="forward_other",
    )(embed_other, packed)
    shares_far, shares_other_far, inverse, stats, packets = pl.pallas_call(
        functools.partial(far_kernel, dims),
        out_shape=(
            shape((passage_rows, far_rows), bf16),
            shape((passage_rows, far_rows), bf16),
            shape((pair, all_rows), f32),
            shape((3 * pair, pool_width), f32),
            shape((devices, packet_rows, pool_width), f32),
        ),
        in_specs=[VMEM] * (blocks + 5),
        out_specs=(VMEM,) * 5,
        scratch_shapes=[
            pltpu.VMEM((pair, all_rows), f32),
            pltpu.VMEM((pair, far_rows), f32),
            pltpu.VMEM((pool_width, lanes), f32),
        ],
        compiler_params=params(32),
        cost_estimate=forward_cost(pair, far_rows),
        name="forward_far",
    )(*queries, embed, embed_other, summed_near, summed_other, gather)

    packets = lax.all_to_all(packets, axes, 0, 0, tiled=True)

    *far_parts, weights, losses, grad_other = pl.pallas_call(
        functools.partial(far_grad_kernel, dims),
        out_shape=(
            *[shape((depth, rows), bf16)] * (blocks - 1),
            shape((pair, all_rows), f32),
            shape((8, pool_width), f32),
            shape((passage_rows, depth), bf16),
        ),
        in_specs=[VMEM] * (9 + blocks),
        out_specs=(VMEM,) * (blocks + 2),
        scratch_shapes=[
            pltpu.VMEM((depth, far_rows), f32),
            pltpu.VMEM((far_rows, depth), bf16),
        ],
        compiler_params=params(32),
        cost_estimate=forward_cost(pair, all_rows),
        name="far_grads",
    )(
        packets,
        stats,
        inverse,
        spread,
        shares_far,
        shares_other_near,
        shares_other_far,
        embed,
        embed_other,
        *queries,
    )
    grad_other = swap(grad_other, 1)
    far_parts = [swap(part, cores * (k + 1)) for k, part in enumerate(far_parts)]

    own_part, grad_own, pre_t, hidden_t = pl.pallas_call(
        functools.partial(own_grad_kernel, dims),
        out_shape=(
            shape((depth, rows), f32),
            shape((passage_rows, depth), f32),
            shape((depth, rows), f32),
            shape((width, rows), bf16),
        ),
        in_specs=[VMEM] * (8 + blocks),
        out_specs=(VMEM,) * 4,
        scratch_shapes=[pltpu.VMEM((far_rows, depth), bf16)],
        compiler_params=params(32),
        cost_estimate=forward_cost(pair, all_rows),
        name="own_grads",
    )(
        weights,
        shares_near,
        shares_far,
        shares_other_near,
        embed,
        embed_other,
        query_pre,
        query_flat,
        *queries,
    )

    weight, grad_passage = pl.pallas_call(
        functools.partial(passage_back_kernel, dims),
        out_shape=(shape((width, depth), f32), shape((passage_rows, width), bf16)),
        in_specs=[VMEM] * 5,
        out_specs=(VMEM, HBM),
        scratch_shapes=[
            pltpu.VMEM((depth, width), f32),
            pltpu.VMEM((passage_rows, width), bf16),
            pltpu.SemaphoreType.DMA((passages // step,)),
        ],
        compiler_params=params(32),
        cost_estimate=cost(4 * passage_rows * width * depth, passage_rows * width * 4),
        name="passage_back",
    )(grad_own, grad_other, passage_pre, passage_flat, projection_near)

    parts = [*far_parts, own_part]
    query_back, weight = pl.pallas_call(
        query_back_kernel,
        out_shape=(shape((depth, rows), bf16), shape((width, depth), bf16)),
        in_specs=[VMEM] * (3 + blocks),
        out_specs=(VMEM, VMEM),
        compiler_params=params(16),
        cost_estimate=cost(2 * rows * width * depth, width * depth * 6 + rows * width * 2),
        name="query_back",
    )(pre_t, hidden_t, weight, *parts)

    weight = weight.reshape(devices, width // devices, depth)
    weight = lax.all_to_all(weight, axes, 0, 0, tiled=True)
    copies = pl.pallas_call(
        sum_kernel,
        out_shape=shape(weight.shape, bf16),
        in_specs=[VMEM],
        out_specs=VMEM,
        compiler_params=params(16),
        name="sum_parts",
    )(weight)
    copies = lax.all_to_all(copies, axes, 0, 0, tiled=True)
    grad_proj, grad_query, losses = pl.pallas_call(
        final_kernel,
        out_shape=(shape((width, depth), f32), shape((rows, width), bf16), shape((count,), f32)),
        in_specs=[VMEM] * 4,
        out_specs=(VMEM,) * 3,
        compiler_params=params(16),
        cost_estimate=cost(2 * rows * width * depth, rows * width * 4),
        name="outputs",
    )(copies.reshape(width, depth), query_back, projection_near, losses)
    return (
        losses,
        grad_proj,
        grad_query.reshape(query_hidden.shape),
        grad_passage.reshape(passage_hidden.shape),
    )


def solution(mesh):
    in_specs = (
        P(axes, None, None),
        P(axes, None, None),
        P(),
        P(axes),
        P(axes, None),
        P(axes),
    )
    out_specs = (P(axes), P(), P(axes, None, None), P(axes, None, None))
    return jax.shard_map(local, mesh=mesh, in_specs=in_specs, out_specs=out_specs, check_vma=False)
```

```python
import functools

import jax
import jax.numpy as jnp
from jax import lax
from jax.experimental import pallas as pl
from jax.experimental.pallas import tpu as pltpu
from jax.sharding import PartitionSpec as P

smooth_temp = 0.1
norm_eps = 1e-06
center = 0.375
lanes = 128
cores = 2
padding = -30.0
axes = ("dp", "group")
f32 = jnp.float32
bf16 = jnp.bfloat16


def dot(left, right, left_dim, right_dim):
    return lax.dot_general(
        left, right, (((left_dim,), (right_dim,)), ((), ())), preferred_element_type=f32
    )


def exact_dot(value, picks):
    high = value.astype(bf16)
    rest = value - high.astype(f32)
    middle = rest.astype(bf16)
    low = (rest - middle.astype(f32)).astype(bf16)
    rows = value.shape[0]
    got = dot(jnp.concatenate([high, middle, low], axis=0), picks, 1, 0)
    return got[:rows] + got[rows : 2 * rows] + got[2 * rows :]


def normalize(projected):
    return projected * lax.rsqrt(jnp.sum(projected * projected, axis=-1, keepdims=True) + norm_eps)


def normalize_back(projected, grad):
    inverse = lax.rsqrt(jnp.sum(projected * projected, axis=-1, keepdims=True) + norm_eps)
    along = jnp.sum(projected * grad, axis=-1, keepdims=True)
    return grad * inverse - projected * (inverse * inverse * inverse * along)


def iota(shape, dim):
    return lax.broadcasted_iota(jnp.int32, shape, dim)


def params(megabytes):
    return pltpu.CompilerParams(vmem_limit_bytes=megabytes * 2**20)


def cost(flops, nbytes, exps=0):
    return pl.CostEstimate(flops=int(flops), bytes_accessed=int(nbytes), transcendentals=int(exps))


VMEM = pl.BlockSpec(memory_space=pltpu.VMEM)
HBM = pl.BlockSpec(memory_space=pltpu.HBM)


def in_hbm(*values):
    return [pltpu.with_memory_space_constraint(value, pltpu.HBM) for value in values]


def query_kernel(
    hidden_hbm,
    projection_hbm,
    ids_hbm,
    positive_hbm,
    pre_out,
    packed_out,
    projection,
    hidden,
    hard_ids,
    positive,
    sems,
):
    copies = [
        pltpu.make_async_copy(source, target, sems.at[k])
        for k, (source, target) in enumerate(
            [
                (projection_hbm, projection),
                (hidden_hbm, hidden),
                (ids_hbm, hard_ids),
                (positive_hbm, positive),
            ]
        )
    ]
    for copy in copies:
        copy.start()
    for copy in copies[2:]:
        copy.wait()
    rows = hidden.shape[0]
    count, slots = hard_ids.shape
    row = iota((count, lanes), 0)
    column = iota((count, lanes), 1)
    marks = jnp.full((count, lanes), -1.0, f32)
    for k in range(count):
        marks = jnp.where((row == k) & (column == slots), positive[k].astype(f32), marks)
    ids = jnp.concatenate(
        [hard_ids[...].astype(f32), jnp.full((count, lanes - slots), -1.0, f32)], axis=1
    )
    marks = jnp.where(column < slots, ids, marks)
    extra = packed_out.shape[0] - rows
    marks = jnp.concatenate([marks, jnp.full((extra - count, lanes), -1.0, f32)], axis=0)
    packed_out[rows:, :] = marks.astype(bf16)
    for copy in copies[:2]:
        copy.wait()
    pre = dot(hidden[...], projection[...], 1, 0)
    pre_out[...] = pre
    packed_out[:rows, :] = normalize(pre).astype(bf16)


def parted(index, size):
    if size & (size - 1) == 0:
        return lax.shift_right_logical(index, size.bit_length() - 1)
    return index // size


def owners(dims, token):
    chip = lax.axis_index("group") // cores
    return jnp.bitwise_xor(parted(token, dims[2]), chip * dims[1])


def token_picks(dims, width):
    blocks, count, length = dims[:3]
    shape = (blocks * count * length, width)
    return jnp.where(owners(dims, iota(shape, 0)) == iota(shape, 1), 1.0, 0.0).astype(bf16)


def passage_kernel(dims, lens, hidden, projection, pre_out, embed_out):
    blocks, count, length, passages, tokens, slots, step = dims
    for start in range(0, hidden.shape[0], step * tokens):
        part = slice(start, start + step * tokens)
        pre = dot(hidden[part, :], projection[...], 1, 0)
        pre_out[part, :] = pre
        embed_out[part, :] = normalize(pre).astype(bf16)
    row = jnp.broadcast_to(lens[...].astype(f32).reshape(1, passages), (passages, passages))
    own = iota(row.shape, 0) == iota(row.shape, 1)
    column = jnp.sum(jnp.where(own, row, 0.0), axis=1, keepdims=True)
    embed_out[hidden.shape[0] :, :] = jnp.broadcast_to(column, (passages, lanes)).astype(bf16)


def fill_bias(dims, embed, bias_out):
    passages, tokens = dims[3:5]
    lens = embed[passages * tokens :, :].astype(f32).astype(jnp.int32)
    for p in range(passages):
        live = iota((tokens, lanes), 0) < lens[p : p + 1, :]
        bias_out[p * tokens : (p + 1) * tokens, :] = jnp.where(live, 0.0, padding).astype(bf16)


def forward_part(dims, embed, bias, queries, shares_out, summed, first):
    blocks, count, length, passages, tokens, slots, step = dims
    rows = count * length
    once = jnp.where(iota((rows, lanes), 1) == 0, 1.0, 0.0).astype(bf16)
    for at in range(passages // step):
        part = slice(at * step * tokens, (at + 1) * step * tokens)
        left = jnp.concatenate([embed[part, :], bias[part, :]], axis=1)
        for k, block in enumerate(queries):
            columns = slice(k * rows, (k + 1) * rows)
            similar = dot(left, jnp.concatenate([block[:rows, :], once], axis=1), 1, 1)
            for p in range(step):
                row = at * step + p
                grown = jnp.exp(similar[p * tokens : (p + 1) * tokens, :] * (1.0 / smooth_temp))
                shares_out[row * tokens : (row + 1) * tokens, columns] = grown.astype(bf16)
                summed[first + row : first + row + 1, columns] = jnp.sum(
                    grown, axis=0, keepdims=True
                )


def near_kernel(dims, embed, packed, shares_out, summed_out, turned_out, bias_out, gather_out):
    fill_bias(dims, embed, bias_out)
    forward_part(dims, embed, bias_out, [packed], shares_out, summed_out, 0)
    turned_out[...] = embed[: turned_out.shape[1], :].T
    gather_out[...] = token_picks(dims, gather_out.shape[1])


def other_kernel(dims, embed, packed, shares_out, summed_out, turned_out, bias_out):
    fill_bias(dims, embed, bias_out)
    forward_part(dims, embed, bias_out, [packed], shares_out, summed_out, 0)
    turned_out[...] = embed[: turned_out.shape[1], :].T


def far_kernel(dims, *refs):
    blocks, count, length, passages, tokens, slots, step = dims
    packed = refs[:blocks]
    embed, embed_other, bias, bias_other, summed_near, summed_other, gather, *refs = refs[blocks:]
    shares_far, shares_other, inverse_out, stats_out, packet_out, summed, summed_far, marks = refs
    rows = count * length
    me = lax.axis_index("group")
    marks[...] = jnp.full(marks.shape, -1.0, f32)
    for k in range(blocks):
        start = pl.multiple_of(jnp.bitwise_xor(me // cores, k) * count, count)
        marks[pl.ds(start, count), :] = packed[k][rows:, :].astype(f32)[:count]
    forward_part(dims, embed, bias, packed[1:], shares_far, summed_far, 0)
    forward_part(dims, embed_other, bias_other, packed[1:], shares_other, summed_far, passages)
    summed[:passages, :rows] = summed_near[...]
    summed[passages:, :rows] = summed_other[...]
    summed[:, rows:] = summed_far[...]
    total = summed[...]
    inverse_out[...] = 1.0 / total
    width = marks.shape[0]
    scores = exact_dot(smooth_temp * jnp.log(total), gather[...])
    marks_t = marks[...].T
    pair = cores * passages
    row = iota((pair, width), 0)
    other = jnp.bitwise_xor(me, 1)
    here = jnp.where(row < passages, row + me * passages, row + (other - 1) * passages)
    here = here.astype(f32)
    chosen = here == marks_t[slots : slots + 1, :]
    counts = jnp.zeros((pair, width), f32)
    for k in range(slots):
        counts += jnp.where(here == marks_t[k : k + 1, :], 1.0, 0.0)
    grown = jnp.exp(scores - center * length)
    boost = blocks * pair / slots
    boosted = jnp.where(chosen, 0.0, boost * counts)
    stats_out[:pair, :] = grown
    stats_out[pair : 2 * pair, :] = boosted
    stats_out[2 * pair :, :] = jnp.where(chosen, 1.0, 0.0)
    plain = jnp.sum(grown, axis=0, keepdims=True)
    hard = jnp.sum(boosted * grown * grown, axis=0, keepdims=True)
    kept = jnp.sum(jnp.where(chosen, scores, 0.0), axis=0, keepdims=True)
    sums = jnp.sum(counts * grown, axis=0, keepdims=True)
    sums = jnp.broadcast_to(jnp.sum(sums, axis=1, keepdims=True), sums.shape)
    queries = blocks * count
    if packet_out.shape[1] == 1:
        lane = iota(plain.shape, 1)
        packet = jnp.where(lane < queries, plain, sums)
        packet = jnp.where(lane // queries == 1, pltpu.roll(hard, queries, 1), packet)
        packet = jnp.where(lane // queries == 2, pltpu.roll(kept, 2 * queries, 1), packet)
    else:
        packet = jnp.concatenate([plain, hard, kept, sums] * 2, axis=0)
    for k in range(packet_out.shape[0]):
        packet_out[k] = packet


def coefficients(dims, shares, columns, weights, first, at):
    passages, tokens, _, step = dims[3:]
    parts = []
    for p in range(at * step, (at + 1) * step):
        weight = weights[first + p : first + p + 1, columns]
        weight = jnp.broadcast_to(weight, (tokens, weight.shape[1])).astype(bf16)
        parts.append(shares[p * tokens : (p + 1) * tokens, :] * weight)
    return jnp.concatenate(parts, axis=0)


def far_grad_kernel(
    dims,
    packets,
    stats,
    inverse,
    shares_far,
    shares_other_near,
    shares_other_far,
    embed_t,
    embed_other_t,
    *refs,
):
    blocks, count, length, passages, tokens, slots, step = dims
    packed, refs = refs[:blocks], refs[blocks:]
    parts_out = refs[: blocks - 1]
    weights, losses_out, grad_out, running, far_queries = refs[blocks - 1 :]
    rows = count * length
    pair = cores * passages
    width = stats.shape[1]
    devices = packets.shape[0]
    groups = cores * blocks
    core = lax.axis_index("group") % cores
    pool = packets[pl.ds(lax.axis_index("dp") * groups, groups)]
    pool = jnp.where(iota(pool.shape, 0) % cores == core, pool, 0.0).sum(axis=0)
    every = packets[...].sum(axis=0)
    queries = blocks * count
    if packets.shape[1] == 1:
        plain = pool
        hard = pltpu.roll(pool, width - queries, 1)
        kept = pltpu.roll(pool, width - 2 * queries, 1)
        sums = every[:, 3 * queries : 3 * queries + 1]
    else:
        plain, hard, kept, sums = pool[0:1, :], pool[1:2, :], pool[2:3, :], every[3:4, 0:1]
    hard_mean = sums * (1.0 / (devices * count * slots))
    partition = jnp.where(iota(plain.shape, 1) < queries, plain + hard / hard_mean, 1.0)
    losses = jnp.broadcast_to(
        jnp.log(partition) - (kept - center * length), losses_out.shape
    )
    chip = lax.axis_index("group") // cores
    losses_out[...] = pltpu.roll(losses, width - chip * count, 1)
    grown = stats[:pair, :]
    boosted = stats[pair : 2 * pair, :]
    chosen = stats[2 * pair :, :]
    grad = grown * (1.0 + boosted * grown / hard_mean) / partition - chosen
    spreaded = []
    for start in range(0, blocks * rows, lanes):
        owner = owners(dims, iota(grad.shape, 1) + start)
        spreaded.append(jnp.take_along_axis(grad, owner, axis=1))
    found = jnp.concatenate(spreaded, axis=1) * inverse[...]
    weights[...] = found
    for k in range(1, blocks):
        far_queries[(k - 1) * rows : k * rows, :] = packed[k][:rows, :]
    near, far = slice(0, rows), slice(rows, blocks * rows)
    for at in range(passages // step):
        part = slice(at * step * tokens, (at + 1) * step * tokens)
        own = coefficients(dims, shares_far, far, weights, 0, at)
        other_near = coefficients(dims, shares_other_near, near, weights, passages, at)
        other_far = coefficients(dims, shares_other_far, far, weights, passages, at)
        terms = dot(embed_t[:, part], own, 1, 0) + dot(embed_other_t[:, part], other_far, 1, 0)
        if at == 0:
            running[...] = terms
        else:
            running[...] += terms
        grad = dot(other_near, packed[0][:rows, :], 1, 0) + dot(other_far, far_queries[...], 1, 0)
        grad_out[part, :] = grad.astype(bf16)
    for k, out in enumerate(parts_out):
        out[...] = running[:, k * rows : (k + 1) * rows].astype(bf16)


def own_grad_kernel(
    dims,
    weights,
    shares_near,
    shares_far,
    shares_other,
    embed_t,
    embed_other_t,
    query_pre,
    query_hidden,
    *refs,
):
    blocks, count, length, passages, tokens, slots, step = dims
    packed = refs[:blocks]
    part_out, grad_out, pre_out, hidden_out, queries = refs[blocks:]
    rows = count * length
    for k in range(1, blocks):
        queries[(k - 1) * rows : k * rows, :] = packed[k][:rows, :]
    own, far = slice(0, rows), slice(rows, blocks * rows)
    for at in range(passages // step):
        part = slice(at * step * tokens, (at + 1) * step * tokens)
        near = coefficients(dims, shares_near, own, weights, 0, at)
        other = coefficients(dims, shares_other, own, weights, passages, at)
        terms = dot(embed_t[:, part], near, 1, 0) + dot(embed_other_t[:, part], other, 1, 0)
        if at == 0:
            part_out[...] = terms
        else:
            part_out[...] += terms
        grad_out[part, :] = dot(near, packed[0][:rows, :], 1, 0) + dot(
            coefficients(dims, shares_far, far, weights, 0, at), queries[...], 1, 0
        )
    pre_out[...] = query_pre[...].T
    hidden_out[...] = query_hidden[...].T


def passage_back_kernel(
    dims,
    grad,
    grad_other,
    pre,
    hidden,
    projection,
    weight_out,
    grad_hidden_hbm,
    backs,
    grad_hidden,
    sems,
):
    blocks, count, length, passages, tokens, slots, step = dims
    copies = []
    for at in range(passages // step):
        part = slice(at * step * tokens, (at + 1) * step * tokens)
        total = grad[part, :] + grad_other[part, :].astype(f32)
        back = normalize_back(pre[part, :], total).astype(bf16)
        grad_hidden[part, :] = dot(back, projection[...], 1, 1).astype(bf16)
        rows = pl.ds(at * step * tokens, step * tokens)
        copy = pltpu.make_async_copy(grad_hidden.at[rows], grad_hidden_hbm.at[rows], sems.at[at])
        copy.start()
        copies.append(copy)
        backs[:, part] = back.T
    weight_out[...] = dot(backs[...], hidden[...], 1, 0).T
    for copy in copies:
        copy.wait()


def normalize_back_columns(projected, grad):
    inverse = lax.rsqrt(jnp.sum(projected * projected, axis=0, keepdims=True) + norm_eps)
    along = jnp.sum(projected * grad, axis=0, keepdims=True)
    return grad * inverse - projected * (inverse * inverse * inverse * along)


def query_back_kernel(pre, hidden, weight, *refs):
    parts = refs[:-2]
    back_out, weight_out = refs[-2:]
    grad = sum(part[...].astype(f32) for part in parts)
    back = normalize_back_columns(pre[...], grad).astype(bf16)
    back_out[...] = back
    weight_out[...] = (weight[...] + dot(hidden[...], back, 1, 1)).astype(bf16)


def sum_kernel(parts, copies_out):
    devices = copies_out.shape[0]
    total = parts[0].astype(f32)
    for k in range(1, devices):
        total += parts[k].astype(f32)
    total = total.astype(bf16)
    for k in range(devices):
        copies_out[k] = total


def final_kernel(copies, back, projection, losses, grad_proj_out, grad_query_out, losses_out):
    grad_proj_out[...] = copies[...].astype(f32)
    grad_query_out[...] = dot(back[...].T, projection[...], 1, 1).astype(bf16)
    losses_out[...] = losses[0, : losses_out.shape[0]]


def local(query_hidden, passage_hidden, projection, positive, hard_ids, passage_len):
    count, length, width = query_hidden.shape
    passages, tokens, _ = passage_hidden.shape
    depth = projection.shape[1]
    slots = hard_ids.shape[1]
    groups = lax.axis_size("group")
    devices = lax.axis_size(axes)
    blocks = groups // cores
    rows = count * length
    all_rows = blocks * rows
    far_rows = all_rows - rows
    passage_rows = passages * tokens
    pair = cores * passages
    pool_width = -(-blocks * count // lanes) * lanes
    packet_rows = 1 if 3 * blocks * count < lanes else 8
    step = 4 if blocks <= 2 else 1
    dims = (blocks, count, length, passages, tokens, slots, step)
    query_flat = query_hidden.reshape(rows, width)
    passage_flat = passage_hidden.reshape(passage_rows, width)
    shape = jax.ShapeDtypeStruct

    query_pre, packed, projection_near = pl.pallas_call(
        query_kernel,
        out_shape=(
            shape((rows, depth), f32),
            shape((rows + 16, depth), bf16),
            shape((width, depth), bf16),
        ),
        in_specs=[HBM] * 4,
        out_specs=(VMEM,) * 3,
        scratch_shapes=[
            pltpu.VMEM((rows, width), bf16),
            pltpu.VMEM((count, slots), jnp.int32),
            pltpu.SMEM((count,), jnp.int32),
            pltpu.SemaphoreType.DMA((4,)),
        ],
        compiler_params=params(16),
        cost_estimate=cost(2e10, rows * width * 2),
        name="query_embed",
    )(*in_hbm(query_flat, projection, hard_ids, positive))

    def swap(value, k):
        return lax.ppermute(value, "group", [(i, i ^ k) for i in range(groups)])

    queries = [packed] + [swap(packed, cores * k) for k in range(1, blocks)]

    passage_pre, embed = pl.pallas_call(
        functools.partial(passage_kernel, dims),
        out_shape=(
            shape((passage_rows, depth), f32),
            shape((passage_rows + passages, depth), bf16),
        ),
        in_specs=[VMEM] * 3,
        out_specs=(VMEM,) * 2,
        compiler_params=params(16),
        cost_estimate=cost(2 * passage_rows * width * depth, passage_rows * (width * 2 + depth * 6)),
        name="passage_embed",
    )(passage_len, passage_flat, projection_near)
    embed_other = swap(embed, 1)

    def forward_cost(passage_count, query_rows):
        pairs = passage_count * tokens * query_rows
        return cost(2 * pairs * depth, pairs * 2, pairs)

    shares_near, summed_near, embed_t, bias, gather = pl.pallas_call(
        functools.partial(near_kernel, dims),
        out_shape=(
            shape((passage_rows, rows), bf16),
            shape((passages, rows), f32),
            shape((depth, passage_rows), bf16),
            shape((passage_rows, lanes), bf16),
            shape((all_rows, pool_width), bf16),
        ),
        in_specs=[VMEM] * 2,
        out_specs=(VMEM,) * 5,
        compiler_params=params(16),
        cost_estimate=cost(5e10, 1e6),
        name="forward_near",
    )(embed, packed)
    shares_other_near, summed_other, embed_other_t, bias_other = pl.pallas_call(
        functools.partial(other_kernel, dims),
        out_shape=(
            shape((passage_rows, rows), bf16),
            shape((passages, rows), f32),
            shape((depth, passage_rows), bf16),
            shape((passage_rows, lanes), bf16),
        ),
        in_specs=[VMEM] * 2,
        out_specs=(VMEM,) * 4,
        compiler_params=params(16),
        cost_estimate=forward_cost(passages, rows),
        name="forward_other",
    )(embed_other, packed)
    shares_far, shares_other_far, inverse, stats, packets = pl.pallas_call(
        functools.partial(far_kernel, dims),
        out_shape=(
            shape((passage_rows, far_rows), bf16),
            shape((passage_rows, far_rows), bf16),
            shape((pair, all_rows), f32),
            shape((3 * pair, pool_width), f32),
            shape((devices, packet_rows, pool_width), f32),
        ),
        in_specs=[VMEM] * (blocks + 7),
        out_specs=(VMEM,) * 5,
        scratch_shapes=[
            pltpu.VMEM((pair, all_rows), f32),
            pltpu.VMEM((pair, far_rows), f32),
            pltpu.VMEM((pool_width, lanes), f32),
        ],
        compiler_params=params(32),
        cost_estimate=forward_cost(pair, far_rows),
        name="forward_far",
    )(
        *queries,
        embed,
        embed_other,
        bias,
        bias_other,
        summed_near,
        summed_other,
        gather,
    )

    packets = lax.all_to_all(packets, axes, 0, 0, tiled=True)

    *far_parts, weights, losses, grad_other = pl.pallas_call(
        functools.partial(far_grad_kernel, dims),
        out_shape=(
            *[shape((depth, rows), bf16)] * (blocks - 1),
            shape((pair, all_rows), f32),
            shape((8, pool_width), f32),
            shape((passage_rows, depth), bf16),
        ),
        in_specs=[VMEM] * (8 + blocks),
        out_specs=(VMEM,) * (blocks + 2),
        scratch_shapes=[
            pltpu.VMEM((depth, far_rows), f32),
            pltpu.VMEM((far_rows, depth), bf16),
        ],
        compiler_params=params(32),
        cost_estimate=forward_cost(pair, all_rows),
        name="far_grads",
    )(
        packets,
        stats,
        inverse,
        shares_far,
        shares_other_near,
        shares_other_far,
        embed_t,
        embed_other_t,
        *queries,
    )
    grad_other = swap(grad_other, 1)
    far_parts = [swap(part, cores * (k + 1)) for k, part in enumerate(far_parts)]

    own_part, grad_own, pre_t, hidden_t = pl.pallas_call(
        functools.partial(own_grad_kernel, dims),
        out_shape=(
            shape((depth, rows), f32),
            shape((passage_rows, depth), f32),
            shape((depth, rows), f32),
            shape((width, rows), bf16),
        ),
        in_specs=[VMEM] * (8 + blocks),
        out_specs=(VMEM,) * 4,
        scratch_shapes=[pltpu.VMEM((far_rows, depth), bf16)],
        compiler_params=params(32),
        cost_estimate=forward_cost(pair, all_rows),
        name="own_grads",
    )(
        weights,
        shares_near,
        shares_far,
        shares_other_near,
        embed_t,
        embed_other_t,
        query_pre,
        query_flat,
        *queries,
    )

    weight, grad_passage = pl.pallas_call(
        functools.partial(passage_back_kernel, dims),
        out_shape=(shape((width, depth), f32), shape((passage_rows, width), bf16)),
        in_specs=[VMEM] * 5,
        out_specs=(VMEM, HBM),
        scratch_shapes=[
            pltpu.VMEM((depth, passage_rows), bf16),
            pltpu.VMEM((passage_rows, width), bf16),
            pltpu.SemaphoreType.DMA((passages // step,)),
        ],
        compiler_params=params(32),
        cost_estimate=cost(4 * passage_rows * width * depth, passage_rows * width * 4),
        name="passage_back",
    )(grad_own, grad_other, passage_pre, passage_flat, projection_near)

    parts = [*far_parts, own_part]
    query_back, weight = pl.pallas_call(
        query_back_kernel,
        out_shape=(shape((depth, rows), bf16), shape((width, depth), bf16)),
        in_specs=[VMEM] * (3 + blocks),
        out_specs=(VMEM, VMEM),
        compiler_params=params(16),
        cost_estimate=cost(2 * rows * width * depth, width * depth * 6 + rows * width * 2),
        name="query_back",
    )(pre_t, hidden_t, weight, *parts)

    weight = weight.reshape(devices, width // devices, depth)
    weight = lax.all_to_all(weight, axes, 0, 0, tiled=True)
    copies = pl.pallas_call(
        sum_kernel,
        out_shape=shape(weight.shape, bf16),
        in_specs=[VMEM],
        out_specs=VMEM,
        compiler_params=params(16),
        name="sum_parts",
    )(weight)
    copies = lax.all_to_all(copies, axes, 0, 0, tiled=True)
    grad_proj, grad_query, losses = pl.pallas_call(
        final_kernel,
        out_shape=(shape((width, depth), f32), shape((rows, width), bf16), shape((count,), f32)),
        in_specs=[VMEM] * 4,
        out_specs=(VMEM,) * 3,
        compiler_params=params(16),
        cost_estimate=cost(2 * rows * width * depth, rows * width * 4),
        name="outputs",
    )(copies.reshape(width, depth), query_back, projection_near, losses)
    return (
        losses,
        grad_proj,
        grad_query.reshape(query_hidden.shape),
        grad_passage.reshape(passage_hidden.shape),
    )


def solution(mesh):
    in_specs = (
        P(axes, None, None),
        P(axes, None, None),
        P(),
        P(axes),
        P(axes, None),
        P(axes),
    )
    out_specs = (P(axes), P(), P(axes, None, None), P(axes, None, None))
    return jax.shard_map(local, mesh=mesh, in_specs=in_specs, out_specs=out_specs, check_vma=False)
```

```python
import functools

import jax
import jax.numpy as jnp
from jax import lax
from jax.experimental import pallas as pl
from jax.experimental.pallas import tpu as pltpu
from jax.sharding import PartitionSpec as P

smooth_temp = 0.1
norm_eps = 1e-06
center = 0.375
lanes = 128
cores = 2
padding = -30.0
axes = ("dp", "group")
f32 = jnp.float32
bf16 = jnp.bfloat16


def dot(left, right, left_dim, right_dim):
    return lax.dot_general(
        left, right, (((left_dim,), (right_dim,)), ((), ())), preferred_element_type=f32
    )


def exact_dot(value, picks):
    high = value.astype(bf16)
    rest = value - high.astype(f32)
    middle = rest.astype(bf16)
    low = (rest - middle.astype(f32)).astype(bf16)
    rows = value.shape[0]
    got = dot(jnp.concatenate([high, middle, low], axis=0), picks, 1, 0)
    return got[:rows] + got[rows : 2 * rows] + got[2 * rows :]


def normalize(projected):
    return projected * lax.rsqrt(jnp.sum(projected * projected, axis=-1, keepdims=True) + norm_eps)


def normalize_back(projected, grad):
    inverse = lax.rsqrt(jnp.sum(projected * projected, axis=-1, keepdims=True) + norm_eps)
    along = jnp.sum(projected * grad, axis=-1, keepdims=True)
    return grad * inverse - projected * (inverse * inverse * inverse * along)


def iota(shape, dim):
    return lax.broadcasted_iota(jnp.int32, shape, dim)


def params(megabytes):
    return pltpu.CompilerParams(vmem_limit_bytes=megabytes * 2**20)


def cost(flops, nbytes, exps=0):
    return pl.CostEstimate(flops=int(flops), bytes_accessed=int(nbytes), transcendentals=int(exps))


VMEM = pl.BlockSpec(memory_space=pltpu.VMEM)
HBM = pl.BlockSpec(memory_space=pltpu.HBM)


def in_hbm(*values):
    return [pltpu.with_memory_space_constraint(value, pltpu.HBM) for value in values]


def query_kernel(
    hidden_hbm,
    projection_hbm,
    ids_hbm,
    positive_hbm,
    pre_out,
    packed_out,
    projection,
    hidden,
    hard_ids,
    positive,
    sems,
):
    copies = [
        pltpu.make_async_copy(source, target, sems.at[k])
        for k, (source, target) in enumerate(
            [
                (projection_hbm, projection),
                (hidden_hbm, hidden),
                (ids_hbm, hard_ids),
                (positive_hbm, positive),
            ]
        )
    ]
    for copy in copies:
        copy.start()
    for copy in copies[2:]:
        copy.wait()
    rows = hidden.shape[0]
    count, slots = hard_ids.shape
    row = iota((count, lanes), 0)
    column = iota((count, lanes), 1)
    marks = jnp.full((count, lanes), -1.0, f32)
    for k in range(count):
        marks = jnp.where((row == k) & (column == slots), positive[k].astype(f32), marks)
    ids = jnp.concatenate(
        [hard_ids[...].astype(f32), jnp.full((count, lanes - slots), -1.0, f32)], axis=1
    )
    marks = jnp.where(column < slots, ids, marks)
    extra = packed_out.shape[0] - rows
    marks = jnp.concatenate([marks, jnp.full((extra - count, lanes), -1.0, f32)], axis=0)
    packed_out[rows:, :] = marks.astype(bf16)
    for copy in copies[:2]:
        copy.wait()
    pre = dot(hidden[...], projection[...], 1, 0)
    pre_out[...] = pre
    packed_out[:rows, :] = normalize(pre).astype(bf16)


def parted(index, size):
    if size & (size - 1) == 0:
        return lax.shift_right_logical(index, size.bit_length() - 1)
    return index // size


def owners(dims, token):
    chip = lax.axis_index("group") // cores
    return jnp.bitwise_xor(parted(token, dims[2]), chip * dims[1])


def token_picks(dims, width):
    blocks, count, length = dims[:3]
    shape = (blocks * count * length, width)
    return jnp.where(owners(dims, iota(shape, 0)) == iota(shape, 1), 1.0, 0.0).astype(bf16)


def passage_kernel(dims, lens, hidden, projection, pre_out, embed_out):
    blocks, count, length, passages, tokens, slots, step = dims
    for start in range(0, hidden.shape[0], step * tokens):
        part = slice(start, start + step * tokens)
        pre = dot(hidden[part, :], projection[...], 1, 0)
        pre_out[part, :] = pre
        embed_out[part, :] = normalize(pre).astype(bf16)
    row = jnp.broadcast_to(lens[...].astype(f32).reshape(1, passages), (passages, passages))
    own = iota(row.shape, 0) == iota(row.shape, 1)
    column = jnp.sum(jnp.where(own, row, 0.0), axis=1, keepdims=True)
    embed_out[hidden.shape[0] :, :] = jnp.broadcast_to(column, (passages, lanes)).astype(bf16)


def fill_bias(dims, embed, bias_out):
    passages, tokens = dims[3:5]
    lens = embed[passages * tokens :, :].astype(f32).astype(jnp.int32)
    for p in range(passages):
        live = iota((tokens, lanes), 0) < lens[p : p + 1, :]
        bias_out[p * tokens : (p + 1) * tokens, :] = jnp.where(live, 0.0, padding).astype(bf16)


def forward_part(dims, embed, bias, queries, shares_out, summed, first):
    blocks, count, length, passages, tokens, slots, step = dims
    rows = count * length
    once = jnp.where(iota((rows, lanes), 1) == 0, 1.0, 0.0).astype(bf16)
    for at in range(passages // step):
        part = slice(at * step * tokens, (at + 1) * step * tokens)
        left = jnp.concatenate([embed[part, :], bias[part, :]], axis=1)
        for k, block in enumerate(queries):
            columns = slice(k * rows, (k + 1) * rows)
            similar = dot(left, jnp.concatenate([block[:rows, :], once], axis=1), 1, 1)
            for p in range(step):
                row = at * step + p
                grown = jnp.exp(similar[p * tokens : (p + 1) * tokens, :] * (1.0 / smooth_temp))
                shares_out[row * tokens : (row + 1) * tokens, columns] = grown.astype(bf16)
                summed[first + row : first + row + 1, columns] = jnp.sum(
                    grown, axis=0, keepdims=True
                )


def near_kernel(
    dims,
    embed,
    packed,
    query_pre,
    query_hidden,
    shares_out,
    summed_out,
    turned_out,
    bias_out,
    gather_out,
    pre_out,
    hidden_out,
):
    pre_out[...] = query_pre[...].T
    hidden_out[...] = query_hidden[...].T
    fill_bias(dims, embed, bias_out)
    forward_part(dims, embed, bias_out, [packed], shares_out, summed_out, 0)
    turned_out[...] = embed[: turned_out.shape[1], :].T
    gather_out[...] = token_picks(dims, gather_out.shape[1])


def other_kernel(dims, embed, packed, shares_out, summed_out, turned_out, bias_out):
    fill_bias(dims, embed, bias_out)
    forward_part(dims, embed, bias_out, [packed], shares_out, summed_out, 0)
    turned_out[...] = embed[: turned_out.shape[1], :].T


def far_kernel(dims, *refs):
    blocks, count, length, passages, tokens, slots, step = dims
    packed = refs[:blocks]
    embed, embed_other, bias, bias_other, summed_near, summed_other, gather, *refs = refs[blocks:]
    shares_far, shares_other, inverse_out, stats_out, packet_out, summed, summed_far, marks = refs
    rows = count * length
    me = lax.axis_index("group")
    marks[...] = jnp.full(marks.shape, -1.0, f32)
    for k in range(blocks):
        start = pl.multiple_of(jnp.bitwise_xor(me // cores, k) * count, count)
        marks[pl.ds(start, count), :] = packed[k][rows:, :].astype(f32)[:count]
    forward_part(dims, embed, bias, packed[1:], shares_far, summed_far, 0)
    forward_part(dims, embed_other, bias_other, packed[1:], shares_other, summed_far, passages)
    summed[:passages, :rows] = summed_near[...]
    summed[passages:, :rows] = summed_other[...]
    summed[:, rows:] = summed_far[...]
    total = summed[...]
    inverse_out[...] = 1.0 / total
    width = marks.shape[0]
    scores = exact_dot(smooth_temp * jnp.log(total), gather[...])
    marks_t = marks[...].T
    pair = cores * passages
    row = iota((pair, width), 0)
    other = jnp.bitwise_xor(me, 1)
    here = jnp.where(row < passages, row + me * passages, row + (other - 1) * passages)
    here = here.astype(f32)
    chosen = here == marks_t[slots : slots + 1, :]
    counts = jnp.zeros((pair, width), f32)
    for k in range(slots):
        counts += jnp.where(here == marks_t[k : k + 1, :], 1.0, 0.0)
    grown = jnp.exp(scores - center * length)
    boost = blocks * pair / slots
    boosted = jnp.where(chosen, 0.0, boost * counts)
    stats_out[:pair, :] = grown
    stats_out[pair : 2 * pair, :] = boosted
    stats_out[2 * pair :, :] = jnp.where(chosen, 1.0, 0.0)
    plain = jnp.sum(grown, axis=0, keepdims=True)
    hard = jnp.sum(boosted * grown * grown, axis=0, keepdims=True)
    kept = jnp.sum(jnp.where(chosen, scores, 0.0), axis=0, keepdims=True)
    sums = jnp.sum(counts * grown, axis=0, keepdims=True)
    sums = jnp.broadcast_to(jnp.sum(sums, axis=1, keepdims=True), sums.shape)
    queries = blocks * count
    if packet_out.shape[1] == 1:
        lane = iota(plain.shape, 1)
        packet = jnp.where(lane < queries, plain, sums)
        packet = jnp.where(lane // queries == 1, pltpu.roll(hard, queries, 1), packet)
        packet = jnp.where(lane // queries == 2, pltpu.roll(kept, 2 * queries, 1), packet)
    else:
        packet = jnp.concatenate([plain, hard, kept, sums] * 2, axis=0)
    for k in range(packet_out.shape[0]):
        packet_out[k] = packet


def coefficients(dims, shares, columns, weights, first, at):
    passages, tokens, _, step = dims[3:]
    parts = []
    for p in range(at * step, (at + 1) * step):
        weight = weights[first + p : first + p + 1, columns]
        weight = jnp.broadcast_to(weight, (tokens, weight.shape[1])).astype(bf16)
        parts.append(shares[p * tokens : (p + 1) * tokens, :] * weight)
    return jnp.concatenate(parts, axis=0)


def far_grad_kernel(
    dims,
    packets,
    stats,
    inverse,
    shares_far,
    shares_other_near,
    shares_other_far,
    embed_t,
    embed_other_t,
    *refs,
):
    blocks, count, length, passages, tokens, slots, step = dims
    packed, refs = refs[:blocks], refs[blocks:]
    parts_out = refs[: blocks - 1]
    weights, losses_out, grad_out, running, far_queries = refs[blocks - 1 :]
    rows = count * length
    pair = cores * passages
    width = stats.shape[1]
    devices = packets.shape[0]
    groups = cores * blocks
    core = lax.axis_index("group") % cores
    pool = packets[pl.ds(lax.axis_index("dp") * groups, groups)]
    pool = jnp.where(iota(pool.shape, 0) % cores == core, pool, 0.0).sum(axis=0)
    every = packets[...].sum(axis=0)
    queries = blocks * count
    if packets.shape[1] == 1:
        plain = pool
        hard = pltpu.roll(pool, width - queries, 1)
        kept = pltpu.roll(pool, width - 2 * queries, 1)
        sums = every[:, 3 * queries : 3 * queries + 1]
    else:
        plain, hard, kept, sums = pool[0:1, :], pool[1:2, :], pool[2:3, :], every[3:4, 0:1]
    hard_mean = sums * (1.0 / (devices * count * slots))
    partition = jnp.where(iota(plain.shape, 1) < queries, plain + hard / hard_mean, 1.0)
    losses = jnp.broadcast_to(
        jnp.log(partition) - (kept - center * length), losses_out.shape
    )
    chip = lax.axis_index("group") // cores
    losses_out[...] = pltpu.roll(losses, width - chip * count, 1)
    grown = stats[:pair, :]
    boosted = stats[pair : 2 * pair, :]
    chosen = stats[2 * pair :, :]
    grad = grown * (1.0 + boosted * grown / hard_mean) / partition - chosen
    spreaded = []
    for start in range(0, blocks * rows, lanes):
        owner = owners(dims, iota(grad.shape, 1) + start)
        spreaded.append(jnp.take_along_axis(grad, owner, axis=1))
    found = jnp.concatenate(spreaded, axis=1) * inverse[...]
    weights[...] = found
    for k in range(1, blocks):
        far_queries[(k - 1) * rows : k * rows, :] = packed[k][:rows, :]
    near, far = slice(0, rows), slice(rows, blocks * rows)
    for at in range(passages // step):
        part = slice(at * step * tokens, (at + 1) * step * tokens)
        own = coefficients(dims, shares_far, far, weights, 0, at)
        other_near = coefficients(dims, shares_other_near, near, weights, passages, at)
        other_far = coefficients(dims, shares_other_far, far, weights, passages, at)
        terms = dot(embed_t[:, part], own, 1, 0) + dot(embed_other_t[:, part], other_far, 1, 0)
        if at == 0:
            running[...] = terms
        else:
            running[...] += terms
        grad = dot(other_near, packed[0][:rows, :], 1, 0) + dot(other_far, far_queries[...], 1, 0)
        grad_out[part, :] = grad.astype(bf16)
    for k, out in enumerate(parts_out):
        out[...] = running[:, k * rows : (k + 1) * rows].astype(bf16)


def own_grad_kernel(
    dims,
    weights,
    shares_near,
    shares_far,
    shares_other,
    embed_t,
    embed_other_t,
    *refs,
):
    blocks, count, length, passages, tokens, slots, step = dims
    packed = refs[:blocks]
    part_out, grad_out, queries = refs[blocks:]
    rows = count * length
    for k in range(1, blocks):
        queries[(k - 1) * rows : k * rows, :] = packed[k][:rows, :]
    own, far = slice(0, rows), slice(rows, blocks * rows)
    for at in range(passages // step):
        part = slice(at * step * tokens, (at + 1) * step * tokens)
        near = coefficients(dims, shares_near, own, weights, 0, at)
        other = coefficients(dims, shares_other, own, weights, passages, at)
        terms = dot(embed_t[:, part], near, 1, 0) + dot(embed_other_t[:, part], other, 1, 0)
        if at == 0:
            part_out[...] = terms
        else:
            part_out[...] += terms
        grad_out[part, :] = dot(near, packed[0][:rows, :], 1, 0) + dot(
            coefficients(dims, shares_far, far, weights, 0, at), queries[...], 1, 0
        )


def passage_back_kernel(
    dims,
    grad,
    grad_other,
    pre,
    hidden,
    projection,
    weight_out,
    grad_hidden_hbm,
    backs,
    grad_hidden,
    sems,
):
    blocks, count, length, passages, tokens, slots, step = dims
    copies = []
    for at in range(passages // step):
        part = slice(at * step * tokens, (at + 1) * step * tokens)
        total = grad[part, :] + grad_other[part, :].astype(f32)
        back = normalize_back(pre[part, :], total).astype(bf16)
        grad_hidden[part, :] = dot(back, projection[...], 1, 1).astype(bf16)
        rows = pl.ds(at * step * tokens, step * tokens)
        copy = pltpu.make_async_copy(grad_hidden.at[rows], grad_hidden_hbm.at[rows], sems.at[at])
        copy.start()
        copies.append(copy)
        backs[:, part] = back.T
    weight_out[...] = dot(backs[...], hidden[...], 1, 0).T
    for copy in copies:
        copy.wait()


def normalize_back_columns(projected, grad):
    inverse = lax.rsqrt(jnp.sum(projected * projected, axis=0, keepdims=True) + norm_eps)
    along = jnp.sum(projected * grad, axis=0, keepdims=True)
    return grad * inverse - projected * (inverse * inverse * inverse * along)


def query_back_kernel(pre, hidden, weight, *refs):
    parts = refs[:-2]
    back_out, weight_out = refs[-2:]
    grad = sum(part[...].astype(f32) for part in parts)
    back = normalize_back_columns(pre[...], grad).astype(bf16)
    back_out[...] = back
    weight_out[...] = (weight[...] + dot(hidden[...], back, 1, 1)).astype(bf16)


def sum_kernel(parts, copies_out):
    devices = copies_out.shape[0]
    total = parts[0].astype(f32)
    for k in range(1, devices):
        total += parts[k].astype(f32)
    total = total.astype(bf16)
    for k in range(devices):
        copies_out[k] = total


def final_kernel(copies, back, projection, losses, grad_proj_out, grad_query_out, losses_out):
    grad_proj_out[...] = copies[...].astype(f32)
    grad_query_out[...] = dot(back[...].T, projection[...], 1, 1).astype(bf16)
    losses_out[...] = losses[0, : losses_out.shape[0]]


def local(query_hidden, passage_hidden, projection, positive, hard_ids, passage_len):
    count, length, width = query_hidden.shape
    passages, tokens, _ = passage_hidden.shape
    depth = projection.shape[1]
    slots = hard_ids.shape[1]
    groups = lax.axis_size("group")
    devices = lax.axis_size(axes)
    blocks = groups // cores
    rows = count * length
    all_rows = blocks * rows
    far_rows = all_rows - rows
    passage_rows = passages * tokens
    pair = cores * passages
    pool_width = -(-blocks * count // lanes) * lanes
    packet_rows = 1 if 3 * blocks * count < lanes else 8
    step = 4 if blocks <= 2 else 1
    dims = (blocks, count, length, passages, tokens, slots, step)
    query_flat = query_hidden.reshape(rows, width)
    passage_flat = passage_hidden.reshape(passage_rows, width)
    shape = jax.ShapeDtypeStruct

    query_pre, packed, projection_near, query_rows = pl.pallas_call(
        query_kernel,
        out_shape=(
            shape((rows, depth), f32),
            shape((rows + 16, depth), bf16),
            shape((width, depth), bf16),
            shape((rows, width), bf16),
        ),
        in_specs=[HBM] * 4,
        out_specs=(VMEM,) * 4,
        scratch_shapes=[
            pltpu.VMEM((count, slots), jnp.int32),
            pltpu.SMEM((count,), jnp.int32),
            pltpu.SemaphoreType.DMA((4,)),
        ],
        compiler_params=params(16),
        cost_estimate=cost(2e10, rows * width * 2),
        name="query_embed",
    )(*in_hbm(query_flat, projection, hard_ids, positive))

    def swap(value, k):
        return lax.ppermute(value, "group", [(i, i ^ k) for i in range(groups)])

    queries = [packed] + [swap(packed, cores * k) for k in range(1, blocks)]

    passage_pre, embed = pl.pallas_call(
        functools.partial(passage_kernel, dims),
        out_shape=(
            shape((passage_rows, depth), f32),
            shape((passage_rows + passages, depth), bf16),
        ),
        in_specs=[VMEM] * 3,
        out_specs=(VMEM,) * 2,
        compiler_params=params(16),
        cost_estimate=cost(2 * passage_rows * width * depth, passage_rows * (width * 2 + depth * 6)),
        name="passage_embed",
    )(passage_len, passage_flat, projection_near)
    embed_other = swap(embed, 1)

    def forward_cost(passage_count, query_rows):
        pairs = passage_count * tokens * query_rows
        return cost(2 * pairs * depth, pairs * 2, pairs)

    shares_near, summed_near, embed_t, bias, gather, pre_t, hidden_t = pl.pallas_call(
        functools.partial(near_kernel, dims),
        out_shape=(
            shape((passage_rows, rows), bf16),
            shape((passages, rows), f32),
            shape((depth, passage_rows), bf16),
            shape((passage_rows, lanes), bf16),
            shape((all_rows, pool_width), bf16),
            shape((depth, rows), f32),
            shape((width, rows), bf16),
        ),
        in_specs=[VMEM] * 4,
        out_specs=(VMEM,) * 7,
        compiler_params=params(16),
        cost_estimate=cost(5e10, 1e6),
        name="forward_near",
    )(embed, packed, query_pre, query_rows)
    shares_other_near, summed_other, embed_other_t, bias_other = pl.pallas_call(
        functools.partial(other_kernel, dims),
        out_shape=(
            shape((passage_rows, rows), bf16),
            shape((passages, rows), f32),
            shape((depth, passage_rows), bf16),
            shape((passage_rows, lanes), bf16),
        ),
        in_specs=[VMEM] * 2,
        out_specs=(VMEM,) * 4,
        compiler_params=params(16),
        cost_estimate=forward_cost(passages, rows),
        name="forward_other",
    )(embed_other, packed)
    shares_far, shares_other_far, inverse, stats, packets = pl.pallas_call(
        functools.partial(far_kernel, dims),
        out_shape=(
            shape((passage_rows, far_rows), bf16),
            shape((passage_rows, far_rows), bf16),
            shape((pair, all_rows), f32),
            shape((3 * pair, pool_width), f32),
            shape((devices, packet_rows, pool_width), f32),
        ),
        in_specs=[VMEM] * (blocks + 7),
        out_specs=(VMEM,) * 5,
        scratch_shapes=[
            pltpu.VMEM((pair, all_rows), f32),
            pltpu.VMEM((pair, far_rows), f32),
            pltpu.VMEM((pool_width, lanes), f32),
        ],
        compiler_params=params(32),
        cost_estimate=forward_cost(pair, far_rows),
        name="forward_far",
    )(
        *queries,
        embed,
        embed_other,
        bias,
        bias_other,
        summed_near,
        summed_other,
        gather,
    )

    packets = lax.all_to_all(packets, axes, 0, 0, tiled=True)

    *far_parts, weights, losses, grad_other = pl.pallas_call(
        functools.partial(far_grad_kernel, dims),
        out_shape=(
            *[shape((depth, rows), bf16)] * (blocks - 1),
            shape((pair, all_rows), f32),
            shape((8, pool_width), f32),
            shape((passage_rows, depth), bf16),
        ),
        in_specs=[VMEM] * (8 + blocks),
        out_specs=(VMEM,) * (blocks + 2),
        scratch_shapes=[
            pltpu.VMEM((depth, far_rows), f32),
            pltpu.VMEM((far_rows, depth), bf16),
        ],
        compiler_params=params(32),
        cost_estimate=forward_cost(pair, all_rows),
        name="far_grads",
    )(
        packets,
        stats,
        inverse,
        shares_far,
        shares_other_near,
        shares_other_far,
        embed_t,
        embed_other_t,
        *queries,
    )
    grad_other = swap(grad_other, 1)
    far_parts = [swap(part, cores * (k + 1)) for k, part in enumerate(far_parts)]

    own_part, grad_own = pl.pallas_call(
        functools.partial(own_grad_kernel, dims),
        out_shape=(
            shape((depth, rows), f32),
            shape((passage_rows, depth), f32),
        ),
        in_specs=[VMEM] * (6 + blocks),
        out_specs=(VMEM,) * 2,
        scratch_shapes=[pltpu.VMEM((far_rows, depth), bf16)],
        compiler_params=params(32),
        cost_estimate=forward_cost(pair, all_rows),
        name="own_grads",
    )(
        weights,
        shares_near,
        shares_far,
        shares_other_near,
        embed_t,
        embed_other_t,
        *queries,
    )

    weight, grad_passage = pl.pallas_call(
        functools.partial(passage_back_kernel, dims),
        out_shape=(shape((width, depth), f32), shape((passage_rows, width), bf16)),
        in_specs=[VMEM] * 5,
        out_specs=(VMEM, HBM),
        scratch_shapes=[
            pltpu.VMEM((depth, passage_rows), bf16),
            pltpu.VMEM((passage_rows, width), bf16),
            pltpu.SemaphoreType.DMA((passages // step,)),
        ],
        compiler_params=params(32),
        cost_estimate=cost(4 * passage_rows * width * depth, passage_rows * width * 4),
        name="passage_back",
    )(grad_own, grad_other, passage_pre, passage_flat, projection_near)

    parts = [*far_parts, own_part]
    query_back, weight = pl.pallas_call(
        query_back_kernel,
        out_shape=(shape((depth, rows), bf16), shape((width, depth), bf16)),
        in_specs=[VMEM] * (3 + blocks),
        out_specs=(VMEM, VMEM),
        compiler_params=params(16),
        cost_estimate=cost(2 * rows * width * depth, width * depth * 6 + rows * width * 2),
        name="query_back",
    )(pre_t, hidden_t, weight, *parts)

    weight = weight.reshape(devices, width // devices, depth)
    weight = lax.all_to_all(weight, axes, 0, 0, tiled=True)
    copies = pl.pallas_call(
        sum_kernel,
        out_shape=shape(weight.shape, bf16),
        in_specs=[VMEM],
        out_specs=VMEM,
        compiler_params=params(16),
        name="sum_parts",
    )(weight)
    copies = lax.all_to_all(copies, axes, 0, 0, tiled=True)
    grad_proj, grad_query, losses = pl.pallas_call(
        final_kernel,
        out_shape=(shape((width, depth), f32), shape((rows, width), bf16), shape((count,), f32)),
        in_specs=[VMEM] * 4,
        out_specs=(VMEM,) * 3,
        compiler_params=params(16),
        cost_estimate=cost(2 * rows * width * depth, rows * width * 4),
        name="outputs",
    )(copies.reshape(width, depth), query_back, projection_near, losses)
    return (
        losses,
        grad_proj,
        grad_query.reshape(query_hidden.shape),
        grad_passage.reshape(passage_hidden.shape),
    )


def solution(mesh):
    in_specs = (
        P(axes, None, None),
        P(axes, None, None),
        P(),
        P(axes),
        P(axes, None),
        P(axes),
    )
    out_specs = (P(axes), P(), P(axes, None, None), P(axes, None, None))
    return jax.shard_map(local, mesh=mesh, in_specs=in_specs, out_specs=out_specs, check_vma=False)
```

```python
import functools

import jax
import jax.numpy as jnp
from jax import lax
from jax.experimental import pallas as pl
from jax.experimental.pallas import tpu as pltpu
from jax.sharding import PartitionSpec as P

smooth_temp = 0.1
norm_eps = 1e-06
center = 0.375
lanes = 128
cores = 2
padding = -30.0
axes = ("dp", "group")
f32 = jnp.float32
bf16 = jnp.bfloat16


def dot(left, right, left_dim, right_dim):
    return lax.dot_general(
        left, right, (((left_dim,), (right_dim,)), ((), ())), preferred_element_type=f32
    )


def exact_dot(value, picks):
    high = value.astype(bf16)
    rest = value - high.astype(f32)
    middle = rest.astype(bf16)
    low = (rest - middle.astype(f32)).astype(bf16)
    rows = value.shape[0]
    got = dot(jnp.concatenate([high, middle, low], axis=0), picks, 1, 0)
    return got[:rows] + got[rows : 2 * rows] + got[2 * rows :]


def normalize(projected):
    return projected * lax.rsqrt(jnp.sum(projected * projected, axis=-1, keepdims=True) + norm_eps)


def normalize_back(projected, grad):
    inverse = lax.rsqrt(jnp.sum(projected * projected, axis=-1, keepdims=True) + norm_eps)
    along = jnp.sum(projected * grad, axis=-1, keepdims=True)
    return grad * inverse - projected * (inverse * inverse * inverse * along)


def iota(shape, dim):
    return lax.broadcasted_iota(jnp.int32, shape, dim)


def params(megabytes):
    return pltpu.CompilerParams(vmem_limit_bytes=megabytes * 2**20)


def cost(flops, nbytes, exps=0):
    return pl.CostEstimate(flops=int(flops), bytes_accessed=int(nbytes), transcendentals=int(exps))


VMEM = pl.BlockSpec(memory_space=pltpu.VMEM)
HBM = pl.BlockSpec(memory_space=pltpu.HBM)


def in_hbm(*values):
    return [pltpu.with_memory_space_constraint(value, pltpu.HBM) for value in values]


def query_kernel(
    hidden_hbm,
    projection_hbm,
    ids_hbm,
    positive_hbm,
    pre_out,
    packed_out,
    projection,
    hidden,
    hard_ids,
    positive,
    sems,
):
    copies = [
        pltpu.make_async_copy(source, target, sems.at[k])
        for k, (source, target) in enumerate(
            [
                (projection_hbm, projection),
                (hidden_hbm, hidden),
                (ids_hbm, hard_ids),
                (positive_hbm, positive),
            ]
        )
    ]
    for copy in copies:
        copy.start()
    for copy in copies[2:]:
        copy.wait()
    rows = hidden.shape[0]
    count, slots = hard_ids.shape
    row = iota((count, lanes), 0)
    column = iota((count, lanes), 1)
    marks = jnp.full((count, lanes), -1.0, f32)
    for k in range(count):
        marks = jnp.where((row == k) & (column == slots), positive[k].astype(f32), marks)
    ids = jnp.concatenate(
        [hard_ids[...].astype(f32), jnp.full((count, lanes - slots), -1.0, f32)], axis=1
    )
    marks = jnp.where(column < slots, ids, marks)
    extra = packed_out.shape[0] - rows
    marks = jnp.concatenate([marks, jnp.full((extra - count, lanes), -1.0, f32)], axis=0)
    packed_out[rows:, :] = marks.astype(bf16)
    for copy in copies[:2]:
        copy.wait()
    pre = dot(hidden[...], projection[...], 1, 0)
    pre_out[...] = pre
    packed_out[:rows, :] = normalize(pre).astype(bf16)


def parted(index, size):
    if size & (size - 1) == 0:
        return lax.shift_right_logical(index, size.bit_length() - 1)
    return index // size


def owners(dims, token):
    chip = lax.axis_index("group") // cores
    return jnp.bitwise_xor(parted(token, dims[2]), chip * dims[1])


def token_picks(dims, width):
    blocks, count, length = dims[:3]
    shape = (blocks * count * length, width)
    return jnp.where(owners(dims, iota(shape, 0)) == iota(shape, 1), 1.0, 0.0).astype(bf16)


def passage_kernel(dims, lens, hidden, projection, pre_out, embed_out):
    blocks, count, length, passages, tokens, slots, step = dims
    for start in range(0, hidden.shape[0], step * tokens):
        part = slice(start, start + step * tokens)
        pre = dot(hidden[part, :], projection[...], 1, 0)
        pre_out[part, :] = pre
        embed_out[part, :] = normalize(pre).astype(bf16)
    row = jnp.broadcast_to(lens[...].astype(f32).reshape(1, passages), (passages, passages))
    own = iota(row.shape, 0) == iota(row.shape, 1)
    column = jnp.sum(jnp.where(own, row, 0.0), axis=1, keepdims=True)
    embed_out[hidden.shape[0] :, :] = jnp.broadcast_to(column, (passages, lanes)).astype(bf16)


def fill_bias(dims, embed, bias_out):
    passages, tokens = dims[3:5]
    lens = embed[passages * tokens :, :].astype(f32).astype(jnp.int32)
    for p in range(passages):
        live = iota((tokens, lanes), 0) < lens[p : p + 1, :]
        bias_out[p * tokens : (p + 1) * tokens, :] = jnp.where(live, 0.0, padding).astype(bf16)


def forward_part(dims, embed, bias, queries, shares_out, summed, first):
    blocks, count, length, passages, tokens, slots, step = dims
    rows = count * length
    once = jnp.where(iota((rows, lanes), 1) == 0, 1.0, 0.0).astype(bf16)
    for at in range(passages // step):
        part = slice(at * step * tokens, (at + 1) * step * tokens)
        left = jnp.concatenate([embed[part, :], bias[part, :]], axis=1)
        for k, block in enumerate(queries):
            columns = slice(k * rows, (k + 1) * rows)
            similar = dot(left, jnp.concatenate([block[:rows, :], once], axis=1), 1, 1)
            for p in range(step):
                row = at * step + p
                grown = jnp.exp(similar[p * tokens : (p + 1) * tokens, :] * (1.0 / smooth_temp))
                shares_out[row * tokens : (row + 1) * tokens, columns] = grown.astype(bf16)
                summed[first + row : first + row + 1, columns] = jnp.sum(
                    grown, axis=0, keepdims=True
                )


def near_kernel(
    dims,
    embed,
    packed,
    query_pre,
    query_hidden,
    shares_out,
    summed_out,
    turned_out,
    bias_out,
    gather_out,
    pre_out,
    hidden_out,
):
    pre_out[...] = query_pre[...].T
    hidden_out[...] = query_hidden[...].T
    fill_bias(dims, embed, bias_out)
    forward_part(dims, embed, bias_out, [packed], shares_out, summed_out, 0)
    turned_out[...] = embed[: turned_out.shape[1], :].T
    gather_out[...] = token_picks(dims, gather_out.shape[1])


def other_kernel(dims, embed, packed, shares_out, summed_out, bias_out):
    fill_bias(dims, embed, bias_out)
    forward_part(dims, embed, bias_out, [packed], shares_out, summed_out, 0)


def far_kernel(dims, *refs):
    blocks, count, length, passages, tokens, slots, step = dims
    packed = refs[:blocks]
    embed, embed_other, bias, bias_other, summed_near, summed_other, gather, *refs = refs[blocks:]
    shares_far, shares_other, inverse_out, stats_out, packet_out, summed, summed_far, marks = refs
    rows = count * length
    me = lax.axis_index("group")
    marks[...] = jnp.full(marks.shape, -1.0, f32)
    for k in range(blocks):
        start = pl.multiple_of(jnp.bitwise_xor(me // cores, k) * count, count)
        marks[pl.ds(start, count), :] = packed[k][rows:, :].astype(f32)[:count]
    forward_part(dims, embed, bias, packed[1:], shares_far, summed_far, 0)
    forward_part(dims, embed_other, bias_other, packed[1:], shares_other, summed_far, passages)
    summed[:passages, :rows] = summed_near[...]
    summed[passages:, :rows] = summed_other[...]
    summed[:, rows:] = summed_far[...]
    total = summed[...]
    width = marks.shape[0]
    scores = exact_dot(smooth_temp * jnp.log(total), gather[...])
    marks_t = marks[...].T
    pair = cores * passages
    row = iota((pair, width), 0)
    other = jnp.bitwise_xor(me, 1)
    here = jnp.where(row < passages, row + me * passages, row + (other - 1) * passages)
    here = here.astype(f32)
    chosen = here == marks_t[slots : slots + 1, :]
    counts = jnp.zeros((pair, width), f32)
    for k in range(slots):
        counts += jnp.where(here == marks_t[k : k + 1, :], 1.0, 0.0)
    grown = jnp.exp(scores - center * length)
    boost = blocks * pair / slots
    boosted = jnp.where(chosen, 0.0, boost * counts)
    stats_out[:pair, :] = grown
    stats_out[pair : 2 * pair, :] = boosted
    stats_out[2 * pair :, :] = jnp.where(chosen, 1.0, 0.0)
    plain = jnp.sum(grown, axis=0, keepdims=True)
    hard = jnp.sum(boosted * grown * grown, axis=0, keepdims=True)
    kept = jnp.sum(jnp.where(chosen, scores, 0.0), axis=0, keepdims=True)
    sums = jnp.sum(counts * grown, axis=0, keepdims=True)
    sums = jnp.broadcast_to(jnp.sum(sums, axis=1, keepdims=True), sums.shape)
    queries = blocks * count
    if packet_out.shape[1] == 1:
        lane = iota(plain.shape, 1)
        packet = jnp.where(lane < queries, plain, sums)
        packet = jnp.where(lane // queries == 1, pltpu.roll(hard, queries, 1), packet)
        packet = jnp.where(lane // queries == 2, pltpu.roll(kept, 2 * queries, 1), packet)
    else:
        packet = jnp.concatenate([plain, hard, kept, sums] * 2, axis=0)
    for k in range(packet_out.shape[0]):
        packet_out[k] = packet
    inverse_out[...] = 1.0 / total


def coefficients(dims, shares, columns, weights, first, at):
    passages, tokens, _, step = dims[3:]
    parts = []
    for p in range(at * step, (at + 1) * step):
        weight = weights[first + p : first + p + 1, columns]
        weight = jnp.broadcast_to(weight, (tokens, weight.shape[1])).astype(bf16)
        parts.append(shares[p * tokens : (p + 1) * tokens, :] * weight)
    return jnp.concatenate(parts, axis=0)


def far_grad_kernel(
    dims,
    packets,
    stats,
    inverse,
    shares_far,
    shares_other_near,
    shares_other_far,
    embed_t,
    embed_other,
    *refs,
):
    blocks, count, length, passages, tokens, slots, step = dims
    packed, refs = refs[:blocks], refs[blocks:]
    parts_out = refs[: blocks - 1]
    weights, losses_out, grad_out, running, far_queries = refs[blocks - 1 :]
    rows = count * length
    pair = cores * passages
    width = stats.shape[1]
    devices = packets.shape[0]
    groups = cores * blocks
    core = lax.axis_index("group") % cores
    pool = packets[pl.ds(lax.axis_index("dp") * groups, groups)]
    pool = jnp.where(iota(pool.shape, 0) % cores == core, pool, 0.0).sum(axis=0)
    every = packets[...].sum(axis=0)
    queries = blocks * count
    if packets.shape[1] == 1:
        plain = pool
        hard = pltpu.roll(pool, width - queries, 1)
        kept = pltpu.roll(pool, width - 2 * queries, 1)
        sums = every[:, 3 * queries : 3 * queries + 1]
    else:
        plain, hard, kept, sums = pool[0:1, :], pool[1:2, :], pool[2:3, :], every[3:4, 0:1]
    hard_mean = sums * (1.0 / (devices * count * slots))
    partition = jnp.where(iota(plain.shape, 1) < queries, plain + hard / hard_mean, 1.0)
    losses = jnp.broadcast_to(
        jnp.log(partition) - (kept - center * length), losses_out.shape
    )
    chip = lax.axis_index("group") // cores
    losses_out[...] = pltpu.roll(losses, width - chip * count, 1)
    grown = stats[:pair, :]
    boosted = stats[pair : 2 * pair, :]
    chosen = stats[2 * pair :, :]
    grad = grown * (1.0 + boosted * grown / hard_mean) / partition - chosen
    spreaded = []
    for start in range(0, blocks * rows, lanes):
        owner = owners(dims, iota(grad.shape, 1) + start)
        spreaded.append(jnp.take_along_axis(grad, owner, axis=1))
    found = jnp.concatenate(spreaded, axis=1) * inverse[...]
    weights[...] = found
    for k in range(1, blocks):
        far_queries[(k - 1) * rows : k * rows, :] = packed[k][:rows, :]
    near, far = slice(0, rows), slice(rows, blocks * rows)
    for at in range(passages // step):
        part = slice(at * step * tokens, (at + 1) * step * tokens)
        own = coefficients(dims, shares_far, far, weights, 0, at)
        other_near = coefficients(dims, shares_other_near, near, weights, passages, at)
        other_far = coefficients(dims, shares_other_far, far, weights, passages, at)
        terms = dot(embed_t[:, part], own, 1, 0) + dot(embed_other[part, :].T, other_far, 1, 0)
        if at == 0:
            running[...] = terms
        else:
            running[...] += terms
        grad = dot(other_near, packed[0][:rows, :], 1, 0) + dot(other_far, far_queries[...], 1, 0)
        grad_out[part, :] = grad.astype(bf16)
    for k, out in enumerate(parts_out):
        out[...] = running[:, k * rows : (k + 1) * rows].astype(bf16)


def own_grad_kernel(
    dims,
    weights,
    shares_near,
    shares_far,
    shares_other,
    embed_t,
    embed_other,
    *refs,
):
    blocks, count, length, passages, tokens, slots, step = dims
    packed = refs[:blocks]
    part_out, grad_out, queries = refs[blocks:]
    rows = count * length
    for k in range(1, blocks):
        queries[(k - 1) * rows : k * rows, :] = packed[k][:rows, :]
    own, far = slice(0, rows), slice(rows, blocks * rows)
    for at in range(passages // step):
        part = slice(at * step * tokens, (at + 1) * step * tokens)
        near = coefficients(dims, shares_near, own, weights, 0, at)
        other = coefficients(dims, shares_other, own, weights, passages, at)
        terms = dot(embed_t[:, part], near, 1, 0) + dot(embed_other[part, :].T, other, 1, 0)
        if at == 0:
            part_out[...] = terms
        else:
            part_out[...] += terms
        grad_out[part, :] = dot(near, packed[0][:rows, :], 1, 0) + dot(
            coefficients(dims, shares_far, far, weights, 0, at), queries[...], 1, 0
        )


def passage_back_kernel(
    dims,
    grad,
    grad_other,
    pre,
    hidden,
    projection,
    weight_out,
    grad_hidden_hbm,
    backs,
    grad_hidden,
    sems,
):
    blocks, count, length, passages, tokens, slots, step = dims
    copies = []
    for at in range(passages // step):
        part = slice(at * step * tokens, (at + 1) * step * tokens)
        total = grad[part, :] + grad_other[part, :].astype(f32)
        back = normalize_back(pre[part, :], total).astype(bf16)
        grad_hidden[part, :] = dot(back, projection[...], 1, 1).astype(bf16)
        rows = pl.ds(at * step * tokens, step * tokens)
        copy = pltpu.make_async_copy(grad_hidden.at[rows], grad_hidden_hbm.at[rows], sems.at[at])
        copy.start()
        copies.append(copy)
        backs[:, part] = back.T
    weight_out[...] = dot(backs[...], hidden[...], 1, 0).T
    for copy in copies:
        copy.wait()


def normalize_back_columns(projected, grad):
    inverse = lax.rsqrt(jnp.sum(projected * projected, axis=0, keepdims=True) + norm_eps)
    along = jnp.sum(projected * grad, axis=0, keepdims=True)
    return grad * inverse - projected * (inverse * inverse * inverse * along)


def query_back_kernel(pre, hidden, weight, *refs):
    parts = refs[:-2]
    back_out, weight_out = refs[-2:]
    grad = sum(part[...].astype(f32) for part in parts)
    back = normalize_back_columns(pre[...], grad).astype(bf16)
    back_out[...] = back
    weight_out[...] = (weight[...] + dot(hidden[...], back, 1, 1)).astype(bf16)


def sum_kernel(parts, copies_out):
    devices = copies_out.shape[0]
    total = parts[0].astype(f32)
    for k in range(1, devices):
        total += parts[k].astype(f32)
    total = total.astype(bf16)
    for k in range(devices):
        copies_out[k] = total


def final_kernel(copies, back, projection, losses, grad_proj_out, grad_query_out, losses_out):
    grad_proj_out[...] = copies[...].astype(f32)
    grad_query_out[...] = dot(back[...].T, projection[...], 1, 1).astype(bf16)
    losses_out[...] = losses[0, : losses_out.shape[0]]


def local(query_hidden, passage_hidden, projection, positive, hard_ids, passage_len):
    count, length, width = query_hidden.shape
    passages, tokens, _ = passage_hidden.shape
    depth = projection.shape[1]
    slots = hard_ids.shape[1]
    groups = lax.axis_size("group")
    devices = lax.axis_size(axes)
    blocks = groups // cores
    rows = count * length
    all_rows = blocks * rows
    far_rows = all_rows - rows
    passage_rows = passages * tokens
    pair = cores * passages
    pool_width = -(-blocks * count // lanes) * lanes
    packet_rows = 1 if 3 * blocks * count < lanes else 8
    step = 4 if blocks <= 2 else 1
    dims = (blocks, count, length, passages, tokens, slots, step)
    query_flat = query_hidden.reshape(rows, width)
    passage_flat = passage_hidden.reshape(passage_rows, width)
    shape = jax.ShapeDtypeStruct

    query_pre, packed, projection_near, query_rows = pl.pallas_call(
        query_kernel,
        out_shape=(
            shape((rows, depth), f32),
            shape((rows + 16, depth), bf16),
            shape((width, depth), bf16),
            shape((rows, width), bf16),
        ),
        in_specs=[HBM] * 4,
        out_specs=(VMEM,) * 4,
        scratch_shapes=[
            pltpu.VMEM((count, slots), jnp.int32),
            pltpu.SMEM((count,), jnp.int32),
            pltpu.SemaphoreType.DMA((4,)),
        ],
        compiler_params=params(16),
        cost_estimate=cost(2e10, rows * width * 2),
        name="query_embed",
    )(*in_hbm(query_flat, projection, hard_ids, positive))

    def swap(value, k):
        return lax.ppermute(value, "group", [(i, i ^ k) for i in range(groups)])

    queries = [packed] + [swap(packed, cores * k) for k in range(1, blocks)]

    passage_pre, embed = pl.pallas_call(
        functools.partial(passage_kernel, dims),
        out_shape=(
            shape((passage_rows, depth), f32),
            shape((passage_rows + passages, depth), bf16),
        ),
        in_specs=[VMEM] * 3,
        out_specs=(VMEM,) * 2,
        compiler_params=params(16),
        cost_estimate=cost(2 * passage_rows * width * depth, passage_rows * (width * 2 + depth * 6)),
        name="passage_embed",
    )(passage_len, passage_flat, projection_near)
    embed_other = swap(embed, 1)

    def forward_cost(passage_count, query_rows):
        pairs = passage_count * tokens * query_rows
        return cost(2 * pairs * depth, pairs * 2, pairs)

    shares_near, summed_near, embed_t, bias, gather, pre_t, hidden_t = pl.pallas_call(
        functools.partial(near_kernel, dims),
        out_shape=(
            shape((passage_rows, rows), bf16),
            shape((passages, rows), f32),
            shape((depth, passage_rows), bf16),
            shape((passage_rows, lanes), bf16),
            shape((all_rows, pool_width), bf16),
            shape((depth, rows), f32),
            shape((width, rows), bf16),
        ),
        in_specs=[VMEM] * 4,
        out_specs=(VMEM,) * 7,
        compiler_params=params(16),
        cost_estimate=cost(5e10, 1e6),
        name="forward_near",
    )(embed, packed, query_pre, query_rows)
    shares_other_near, summed_other, bias_other = pl.pallas_call(
        functools.partial(other_kernel, dims),
        out_shape=(
            shape((passage_rows, rows), bf16),
            shape((passages, rows), f32),
            shape((passage_rows, lanes), bf16),
        ),
        in_specs=[VMEM] * 2,
        out_specs=(VMEM,) * 3,
        compiler_params=params(16),
        cost_estimate=forward_cost(passages, rows),
        name="forward_other",
    )(embed_other, packed)
    shares_far, shares_other_far, inverse, stats, packets = pl.pallas_call(
        functools.partial(far_kernel, dims),
        out_shape=(
            shape((passage_rows, far_rows), bf16),
            shape((passage_rows, far_rows), bf16),
            shape((pair, all_rows), f32),
            shape((3 * pair, pool_width), f32),
            shape((devices, packet_rows, pool_width), f32),
        ),
        in_specs=[VMEM] * (blocks + 7),
        out_specs=(VMEM,) * 5,
        scratch_shapes=[
            pltpu.VMEM((pair, all_rows), f32),
            pltpu.VMEM((pair, far_rows), f32),
            pltpu.VMEM((pool_width, lanes), f32),
        ],
        compiler_params=params(32),
        cost_estimate=forward_cost(pair, far_rows),
        name="forward_far",
    )(
        *queries,
        embed,
        embed_other,
        bias,
        bias_other,
        summed_near,
        summed_other,
        gather,
    )

    packets = lax.all_to_all(packets, axes, 0, 0, tiled=True)

    *far_parts, weights, losses, grad_other = pl.pallas_call(
        functools.partial(far_grad_kernel, dims),
        out_shape=(
            *[shape((depth, rows), bf16)] * (blocks - 1),
            shape((pair, all_rows), f32),
            shape((8, pool_width), f32),
            shape((passage_rows, depth), bf16),
        ),
        in_specs=[VMEM] * (8 + blocks),
        out_specs=(VMEM,) * (blocks + 2),
        scratch_shapes=[
            pltpu.VMEM((depth, far_rows), f32),
            pltpu.VMEM((far_rows, depth), bf16),
        ],
        compiler_params=params(32),
        cost_estimate=forward_cost(pair, all_rows),
        name="far_grads",
    )(
        packets,
        stats,
        inverse,
        shares_far,
        shares_other_near,
        shares_other_far,
        embed_t,
        embed_other,
        *queries,
    )
    grad_other = swap(grad_other, 1)
    far_parts = [swap(part, cores * (k + 1)) for k, part in enumerate(far_parts)]

    own_part, grad_own = pl.pallas_call(
        functools.partial(own_grad_kernel, dims),
        out_shape=(
            shape((depth, rows), f32),
            shape((passage_rows, depth), f32),
        ),
        in_specs=[VMEM] * (6 + blocks),
        out_specs=(VMEM,) * 2,
        scratch_shapes=[pltpu.VMEM((far_rows, depth), bf16)],
        compiler_params=params(32),
        cost_estimate=forward_cost(pair, all_rows),
        name="own_grads",
    )(
        weights,
        shares_near,
        shares_far,
        shares_other_near,
        embed_t,
        embed_other,
        *queries,
    )

    weight, grad_passage = pl.pallas_call(
        functools.partial(passage_back_kernel, dims),
        out_shape=(shape((width, depth), f32), shape((passage_rows, width), bf16)),
        in_specs=[VMEM] * 5,
        out_specs=(VMEM, HBM),
        scratch_shapes=[
            pltpu.VMEM((depth, passage_rows), bf16),
            pltpu.VMEM((passage_rows, width), bf16),
            pltpu.SemaphoreType.DMA((passages // step,)),
        ],
        compiler_params=params(32),
        cost_estimate=cost(4 * passage_rows * width * depth, passage_rows * width * 4),
        name="passage_back",
    )(grad_own, grad_other, passage_pre, passage_flat, projection_near)

    parts = [*far_parts, own_part]
    query_back, weight = pl.pallas_call(
        query_back_kernel,
        out_shape=(shape((depth, rows), bf16), shape((width, depth), bf16)),
        in_specs=[VMEM] * (3 + blocks),
        out_specs=(VMEM, VMEM),
        compiler_params=params(16),
        cost_estimate=cost(2 * rows * width * depth, width * depth * 6 + rows * width * 2),
        name="query_back",
    )(pre_t, hidden_t, weight, *parts)

    weight = weight.reshape(devices, width // devices, depth)
    weight = lax.all_to_all(weight, axes, 0, 0, tiled=True)
    copies = pl.pallas_call(
        sum_kernel,
        out_shape=shape(weight.shape, bf16),
        in_specs=[VMEM],
        out_specs=VMEM,
        compiler_params=params(16),
        name="sum_parts",
    )(weight)
    copies = lax.all_to_all(copies, axes, 0, 0, tiled=True)
    grad_proj, grad_query, losses = pl.pallas_call(
        final_kernel,
        out_shape=(shape((width, depth), f32), shape((rows, width), bf16), shape((count,), f32)),
        in_specs=[VMEM] * 4,
        out_specs=(VMEM,) * 3,
        compiler_params=params(16),
        cost_estimate=cost(2 * rows * width * depth, rows * width * 4),
        name="outputs",
    )(copies.reshape(width, depth), query_back, projection_near, losses)
    return (
        losses,
        grad_proj,
        grad_query.reshape(query_hidden.shape),
        grad_passage.reshape(passage_hidden.shape),
    )


def solution(mesh):
    in_specs = (
        P(axes, None, None),
        P(axes, None, None),
        P(),
        P(axes),
        P(axes, None),
        P(axes),
    )
    out_specs = (P(axes), P(), P(axes, None, None), P(axes, None, None))
    return jax.shard_map(local, mesh=mesh, in_specs=in_specs, out_specs=out_specs, check_vma=False)
```
